256 devices in a mesh: dp: 32 (over z_lo, x, core), vocab: 8 (over y, z_hi).
Axes of the slice: x: 4, y: 4, z: 8 (z_hi: 2, z_lo: 4; z = z_hi * 4 + z_lo), core: 2. Of those that a mesh axis runs over, the one named last changes fastest.
Arguments:
- teacher_rows: bfloat16 [256, 16384], P('vocab', 'dp')
- teacher_gain: bfloat16 [16384], replicated, may hold values from 0.5 to 1.5
- teacher_head: bfloat16 [16384, 65536], P(None, ('dp', 'vocab'))
- student_rows: bfloat16 [256, 8192], P('dp', 'vocab')
- student_gain: bfloat16 [8192], replicated, may hold values from 0.5 to 1.5
- student_head: bfloat16 [8192, 65536], P(None, ('dp', 'vocab'))
- sampled_ids: int32 [256], replicated, may hold values from 0 to 65535
- response_mask: int32 [256], replicated, may hold values from 0 to 1, as said below
Outputs:
- distill_loss: float32 [], replicated
- student_rows_grad: bfloat16 [256, 8192], P('dp', 'vocab')
- student_gain_grad: float32 [8192], P('vocab')
The draws below stay inside these ranges and needn't reach their ends.
Inputs may be any that keep to these rules, and one draw needn't show every extreme that they name: response_mask[255] is 1.
All inputs are finite; a program needn't handle non-finite values.
Results may differ from the reference program's by a relative error of at most 0.0067.
Values may be sent and summed in bfloat16 or wider, within the bound.
A program may use at most 128 MiB of HBM per device.

```python
import math
import jax
import jax.numpy as jnp
import numpy as np
from jax import lax

DT = 16384
DS = 8192
VOCAB = 65536
TOKENS = 256


def drawn_rows(key, width):
    return jax.random.truncated_normal(key, -6.0, 6.0, (TOKENS, width), jnp.float32)


def head_values(key, width):
    scale_key, value_key = jax.random.split(key)
    column_scale = jnp.exp(jax.random.uniform(scale_key, (1, VOCAB), jnp.float32, math.log(0.2), math.log(2.0)))
    values = jax.random.truncated_normal(value_key, -6.0, 6.0, (width, VOCAB), jnp.float32)
    return values * column_scale / math.sqrt(width)


def draw_teacher_rows(key, part):
    key = jax.random.fold_in(key, 1)
    values = drawn_rows(key, DT)
    return values.astype(jnp.bfloat16)


def draw_teacher_head(key, part):
    key = jax.random.fold_in(key, 2)
    value_key = jax.random.fold_in(key, 0)
    values = head_values(value_key, DT)
    return values.astype(jnp.bfloat16)


def draw_student_rows(key, part):
    key = jax.random.fold_in(key, 3)
    values = drawn_rows(key, DS)
    return values.astype(jnp.bfloat16)


def draw_student_head(key, part):
    key = jax.random.fold_in(key, 4)
    value_key = jax.random.fold_in(key, 0)
    values = head_values(value_key, DS)
    return values.astype(jnp.bfloat16)


def draw_response_mask(key, part):
    key = jax.random.fold_in(key, 5)
    levels = jax.random.randint(key, (TOKENS,), 0, 4)
    marks = jnp.where(levels > 0, 1, 0).astype(jnp.int32)
    return marks.at[TOKENS - 1].set(1)


def set_ends(values, own_key, least, high):
    longest = values.shape.index(max(values.shape))
    spots = []
    for shift in (0, 1):
        where = [jax.random.randint(jax.random.fold_in(own_key, axis), (), 0, length) for axis, length in enumerate(values.shape)]
        where[longest] = (where[longest] + shift) % values.shape[longest]
        spots.append(tuple(where))
    return values.at[spots[0]].set(least).at[spots[1]].set(high)


def rank_bounds(count, slope):
    loads = [(1 << 20) // math.isqrt(grade ** slope) + 1 for grade in range(1, count + 1)]
    scale = 1 + sum(loads) // (1 << 30)
    return np.cumsum(np.array([max(1, weight // scale) for weight in loads]))


def ranked(key, extent, number_of, lean):
    listing = rank_bounds(number_of, lean)
    lot = jax.random.randint(jax.random.fold_in(key, 1), extent, 0, int(listing[number_of - 1]))
    rank = jnp.searchsorted(jnp.asarray(listing, jnp.int32), lot, side="right")
    return jax.random.permutation(jax.random.fold_in(key, 2), number_of)[rank].astype(jnp.int32)


def setup_inputs(seed: int = 0) -> dict:
    arg_keys = jax.random.split(jax.random.key(seed), 9)
    return {
        "teacher_rows": draw_teacher_rows(jax.random.fold_in(arg_keys[8], 71), 0),
        "teacher_gain": jnp.clip(1.0 + 0.1 * jax.random.normal(arg_keys[1], (DT,), jnp.float32), 0.5, 1.5).astype(jnp.bfloat16),
        "teacher_head": draw_teacher_head(jax.random.fold_in(arg_keys[8], 71), 0),
        "student_rows": draw_student_rows(jax.random.fold_in(arg_keys[8], 71), 0),
        "student_gain": jnp.clip(1.0 + 0.1 * jax.random.normal(arg_keys[4], (DS,), jnp.float32), 0.5, 1.5).astype(jnp.bfloat16),
        "student_head": draw_student_head(jax.random.fold_in(arg_keys[8], 71), 0),
        "sampled_ids": set_ends(ranked(arg_keys[6], (TOKENS,), VOCAB, 2), jax.random.fold_in(arg_keys[6], 3), 0, VOCAB - 1).astype(jnp.int32),
        "response_mask": draw_response_mask(jax.random.fold_in(arg_keys[8], 71), 0),
    }


EPSILON = 1e-05
MIX_WEIGHT = 0.3
NLL_WEIGHT = 0.03
LOSS_SCALE = 8192.0

def rms_inverse(hidden_rows):
    widened = hidden_rows.astype(jnp.float32)
    return lax.rsqrt(lax.optimization_barrier(jnp.mean(widened * widened, axis=1, keepdims=True)) + EPSILON)

def log_total(logits):
    top_value = lax.optimization_barrier(jnp.max(logits, axis=1, keepdims=True))
    return top_value + jnp.log(lax.optimization_barrier(jnp.sum(jnp.exp(logits - top_value), axis=1, keepdims=True)))

def reference(teacher_rows, teacher_gain, teacher_head, student_rows, student_gain, student_head, sampled_ids, response_mask):
    teacher_inv = rms_inverse(teacher_rows)
    teacher_normed = (teacher_rows.astype(jnp.float32) * teacher_inv * teacher_gain.astype(jnp.float32)).astype(jnp.bfloat16)
    teacher_logits = jnp.dot(teacher_normed, teacher_head, preferred_element_type=jnp.float32)
    student_inv = rms_inverse(student_rows)
    student_scaled = student_rows.astype(jnp.float32) * student_inv
    student_normed = (student_scaled * student_gain.astype(jnp.float32)).astype(jnp.bfloat16)
    student_logits = jnp.dot(student_normed, student_head, preferred_element_type=jnp.float32)
    teacher_lse = log_total(teacher_logits)
    student_lse = log_total(student_logits)
    teacher_logp = teacher_logits - teacher_lse
    student_logp = student_logits - student_lse
    mix_logp = jnp.logaddexp(math.log(MIX_WEIGHT) + teacher_logp, math.log(1.0 - MIX_WEIGHT) + student_logp)
    teacher_prob = jnp.exp(teacher_logp)
    student_prob = jnp.exp(student_logp)
    student_gap = student_logp - mix_logp
    jsd = lax.optimization_barrier(jnp.sum(MIX_WEIGHT * teacher_prob * (teacher_logp - mix_logp) + (1.0 - MIX_WEIGHT) * student_prob * student_gap, axis=1))
    kl_student = lax.optimization_barrier(jnp.sum(student_prob * student_gap, axis=1, keepdims=True))
    columns = lax.broadcasted_iota(jnp.int32, student_logits.shape, 1)
    onehot = (columns == sampled_ids.astype(jnp.int32)[:, None]).astype(jnp.float32)
    picked = lax.optimization_barrier(jnp.sum(onehot * student_logits, axis=1))
    weights = response_mask.astype(jnp.float32)
    count = jnp.sum(weights)
    distill_loss = jnp.sum(weights * (jsd + NLL_WEIGHT * (student_lse[:, 0] - picked))) / count
    row_scale = (LOSS_SCALE * weights / count)[:, None]
    logit_grad = (row_scale * (student_prob * ((1.0 - MIX_WEIGHT) * student_gap - (1.0 - MIX_WEIGHT) * kl_student) + NLL_WEIGHT * (student_prob - onehot))).astype(jnp.bfloat16)
    normed_grad = jnp.dot(logit_grad, student_head.T, preferred_element_type=jnp.float32)
    student_gain_grad = lax.optimization_barrier(jnp.sum(normed_grad * student_scaled, axis=0))
    scaled_grad = normed_grad * student_gain.astype(jnp.float32)
    row_dot = lax.optimization_barrier(jnp.mean(scaled_grad * student_scaled, axis=1, keepdims=True))
    student_rows_grad = (student_inv * (scaled_grad - student_scaled * row_dot)).astype(jnp.bfloat16)
    return (distill_loss, student_rows_grad, student_gain_grad)
```

```python
import functools
import math

import jax
import jax.numpy as jnp
from jax import lax
from jax.experimental import pallas as pl
from jax.experimental.pallas import tpu as pltpu
from jax.sharding import PartitionSpec as P

EPSILON = 1e-05
MIX_WEIGHT = 0.3
NLL_WEIGHT = 0.03
LOSS_SCALE = 8192.0
MESH = pl.DeviceIdType.MESH
F32 = jnp.float32
BF16 = jnp.bfloat16
X, Y, Z = 4, 4, 8
TOKENS, DT, DS, WIDTH = 256, 16384, 8192, 256


def kernel(
    t_rows, t_gain, t_head, s_rows, s_gain, s_head, ids, mask,
    loss_out, grad_out, gain_out,
    g0, g1, g2, t_w, s_w, t_inv, s_inv, t_acc, s_acc, dot_col, lg,
    sib_out, sib_in, ra, rb, ra_in1, rb_in1, ra2, rb2, ra_in2, rb_in2, ra3, rb3, ra_in3, rb_in3,
    st_c, st_x, st_y, st_z, gg_c, gg_x, gg_z,
    head_sem, ab_send, ab_recv, ring_send, ring_recv, core_send, core_recv,
    st_send, st_recv, sib_send_sem, sib_recv_sem, rs_send, rs_recv, gg_send, gg_recv,
):
    dp = lax.axis_index("dp")
    vo = lax.axis_index("vocab")
    c = lax.rem(dp, 2)
    x = lax.rem(lax.div(dp, 2), X)
    zl = lax.div(dp, 2 * X)
    y = lax.div(vo, 2)
    zh = lax.rem(vo, 2)
    z = zh * 4 + zl

    def device(x_, y_, z_, c_):
        return ((lax.rem(z_, 4) * X + x_) * 2 + c_, y_ * 2 + lax.div(z_, 4))

    to_c = lambda j: (dp - c + j, vo)
    to_x = lambda j: (dp + (j - x) * 2, vo)
    to_y = lambda j: (dp, vo + (j - y) * 2)
    to_z = lambda j: device(x, y, j, c)
    to_zl = lambda j: (dp + (j - zl) * 2 * X, vo)
    axis_c, axis_x, axis_y, axis_z = (2, c, to_c), (X, x, to_x), (Y, y, to_y), (Z, z, to_z)

    def remote(src, dst, send, recv, to):
        return pltpu.make_async_remote_copy(
            src_ref=src, dst_ref=dst, send_sem=send, recv_sem=recv, device_id=to, device_id_type=MESH
        )

    t_load = pltpu.make_async_copy(t_head, t_w, head_sem.at[0])
    s_load = pltpu.make_async_copy(s_head, s_w, head_sem.at[1])
    t_load.start()
    s_load.start()

    g0[c, z, y, x] = t_rows[0:16, :]
    g1[c, x, y, z] = t_rows[16:32, :]
    own_rows = s_rows[...].astype(F32)
    g2[c, y, x, z] = jnp.concatenate([own_rows[:, :512], own_rows[:, 512:]], axis=0).astype(BF16)

    def lane_sums(block):
        total = block[:, 0:128]
        for k in range(1, block.shape[1] // 128):
            total = total + block[:, k * 128 : (k + 1) * 128]
        total = jnp.concatenate([total] * (TOKENS // total.shape[0]), axis=0)
        return jnp.sum(total.T, axis=0, keepdims=True)

    lanes = lax.broadcasted_iota(jnp.int32, (1, TOKENS), 1)
    t_own = t_rows[...].astype(F32)
    t_squares = jnp.where(lax.div(lanes, 32) == vo, lane_sums(t_own * t_own), 0.0)
    s_squares = jnp.where(lax.div(lanes, 8) == dp, lane_sums(own_rows * own_rows), 0.0)
    pad = lambda rows: jnp.concatenate(rows + [jnp.zeros((8 - len(rows), TOKENS), F32)], axis=0)

    barrier = pltpu.get_barrier_semaphore()
    partners = 0
    for n, me, to in (axis_c, axis_x, axis_y, axis_z):
        for k in range(1, n):
            pl.semaphore_signal(barrier, inc=1, device_id=to(lax.rem(me + k, n)), device_id_type=MESH)
            partners += 1
    pl.semaphore_wait(barrier, partners)

    def all_partners(n, me, to, src, dst, send, recv):
        copies = []
        for k in range(1, n):
            j = lax.rem(me + k, n)
            copy = remote(src(j), dst(me), send(k), recv(me), to(j))
            copy.start()
            copies.append((copy, remote(dst(j), dst(j), send(k), recv(j), to(j))))

        def wait():
            for copy, arrival in copies:
                arrival.wait_recv()
            for copy, arrival in copies:
                copy.wait_send()

        return wait

    def exchange(r, value, combine, result):
        base = 0
        for (n, me, to), buf in zip((axis_c, axis_x, axis_y, axis_z), (st_c, st_x, st_y, st_z)):
            buf[r, me] = value
            wait = all_partners(
                n, me, to,
                lambda j: buf.at[r, me],
                lambda j: buf.at[r, j],
                lambda k: st_send.at[r, base + k],
                lambda j: st_recv.at[r, base + j],
            )
            yield
            wait()
            value = combine([buf[r, j] for j in range(n)])
            base += n
        result.append(value)

    def finish(steps):
        for _ in steps:
            pass

    def add_all(values):
        return functools.reduce(lambda a, b: a + b, values)

    parts = (
        (g0, (axis_x, axis_y, axis_z)),
        (g1, (axis_z, axis_y, axis_x)),
        (g2, (axis_z, axis_x, axis_y)),
    )
    waits = []
    for p, (g, ((na, a, to_a), (_, b, _), (_, cc, _))) in enumerate(parts):
        waits.append(
            all_partners(
                na, a, to_a,
                lambda j: g.at[c, cc, b, a],
                lambda j: g.at[c, cc, b, j],
                lambda k: ab_send.at[p, 0, k],
                lambda j: ab_recv.at[p, 0, j],
            )
        )
    squares = []
    round0 = exchange(0, pad([t_squares, s_squares]), add_all, squares)
    next(round0)
    next_waits = []
    for p, (g, (_, (nb, b, to_b), (_, cc, _))) in enumerate(parts):
        waits[p]()
        next_waits.append(
            all_partners(
                nb, b, to_b,
                lambda j: g.at[c, cc, b],
                lambda j: g.at[c, cc, j],
                lambda k: ab_send.at[p, 1, k],
                lambda j: ab_recv.at[p, 1, j],
            )
        )
    next(round0)

    class Ring:
        def __init__(self, p, g, n, me, to):
            self.p, self.g, self.n, self.me = p, g, n, me
            self.to = (to(lax.rem(me + 1, n)), to(lax.rem(me + n - 1, n)))
            self.sent, self.forwarded = [], []

        def piece(self, way, i, distance, core):
            half = i % 2 if way == 0 else 1 - i % 2
            plane = lax.rem(self.me + (self.n - distance if way == 0 else distance), self.n)
            return self.g.at[core, plane, 2 * half : 2 * half + 2]

        def send(self, way, i):
            ref = self.piece(way, i, i // 2, c)
            copy = remote(ref, ref, ring_send.at[self.p, way, i], ring_recv.at[self.p, way, i], self.to[way])
            copy.start()
            self.sent.append(copy)

        def forward(self, mine, theirs, k):
            copy = remote(mine, mine, core_send.at[self.p, k], core_recv.at[self.p, k], to_c(1 - c))
            copy.start()
            self.forwarded.append((copy, remote(theirs, theirs, core_send.at[self.p, k], core_recv.at[self.p, k], to_c(1 - c))))

        def begin(self):
            for i in range(2):
                for way in range(2):
                    self.send(way, i)
            self.forward(self.g.at[c, self.me], self.g.at[1 - c, self.me], 0)

        def event(self, i):
            for way in range(2):
                ref = self.piece(way, i, i // 2 + 1, c)
                remote(ref, ref, ring_send.at[self.p, way, i], ring_recv.at[self.p, way, i], self.to[way]).wait_recv()
                if i + 2 <= self.n - 2:
                    self.send(way, i + 2)
                self.forward(ref, self.piece(way, i, i // 2 + 1, 1 - c), 1 + 2 * i + way)

        def end(self):
            for copy in self.sent:
                copy.wait_send()
            for copy, arrival in self.forwarded:
                arrival.wait_recv()
                copy.wait_send()

    rings = []
    for p, (g, (_, _, (n, me, to))) in enumerate(parts):
        next_waits[p]()
        ring = Ring(p, g, n, me, to)
        ring.begin()
        rings.append(ring)
    next(round0)
    rings[0].event(0)
    next(round0)
    rings[0].event(1)
    finish(round0)
    squares = squares[0]
    t_inv_row = lax.rsqrt(squares[0:1] / DT + EPSILON)
    s_inv_row = lax.rsqrt(squares[1:2] / DS + EPSILON)
    column = lambda row: jnp.broadcast_to(row, (128, TOKENS)).T
    t_inv[...] = column(t_inv_row)
    s_inv[...] = column(s_inv_row)
    rings[1].event(0)
    rings[2].event(0)
    rings[0].event(2)
    rings[0].event(3)
    rings[1].event(1)
    rings[2].event(1)
    rings[0].event(4)
    rings[0].event(5)
    rings[1].event(2)
    rings[2].event(2)
    rings[0].event(6)
    t_load.wait()
    s_load.wait()
    wide = lambda block: jnp.concatenate([block] * 4, axis=1)

    rings[2].end()
    s_acc[...] = jnp.zeros_like(s_acc)

    def student_step(v, carry):
        y_, zh_ = lax.div(v, 2), lax.rem(v, 2)
        gains = [s_gain[pl.ds(v * 2 + h, 1), :] for h in range(2)]
        blocks = ([], [])
        for pair in range(16):
            scaled = []
            for core in range(2):
                d = pair * 2 + core
                raw = g2[core, y_, pair % 4, zh_ * 4 + pair // 4].astype(F32)
                inv = wide(s_inv[d * 8 : d * 8 + 8, :])
                scaled.append((raw[0:8] * inv, raw[8:16] * inv))
            for h in range(2):
                both = jnp.concatenate([scaled[0][h], scaled[1][h]], axis=0) * gains[h]
                blocks[h].append(both.astype(BF16))
        total = s_acc[...]
        for h in range(2):
            w = s_w[pl.ds(pl.multiple_of(v * 1024 + h * 512, 512), 512), :]
            total += jnp.dot(jnp.concatenate(blocks[h], axis=0), w, preferred_element_type=F32)
        s_acc[...] = total
        return carry

    lax.fori_loop(0, 8, student_step, 0)

    rings[0].end()
    rings[1].end()
    t_acc[...] = jnp.zeros_like(t_acc)

    def teacher_step(d, carry):
        c_, x_, zl_ = lax.rem(d, 2), lax.rem(lax.div(d, 2), X), lax.div(d, 2 * X)
        gain = t_gain[pl.ds(d, 1), :]
        blocks = []
        for v in range(8):
            for p in range(2):
                z_ = (v % 2) * 4 + zl_
                raw = g0[c_, z_, v // 2, x_] if p == 0 else g1[c_, x_, v // 2, z_]
                inv = wide(t_inv[v * 32 + p * 16 : v * 32 + p * 16 + 16, :])
                blocks.append((raw.astype(F32) * inv * gain).astype(BF16))
        w = t_w[pl.ds(pl.multiple_of(d * 512, 512), 512), :]
        t_acc[...] += jnp.dot(jnp.concatenate(blocks, axis=0), w, preferred_element_type=F32)
        return carry

    lax.fori_loop(0, 32, teacher_step, 0)

    t_acc[...] = t_acc[...].T
    s_acc[...] = s_acc[...].T
    tl, sl = t_acc[...], s_acc[...]
    column_start = (dp * 8 + vo) * WIDTH
    onehot = (column_start + lax.broadcasted_iota(jnp.int32, (WIDTH, TOKENS), 0) == ids[...]).astype(F32)
    t_top = jnp.max(tl, axis=0, keepdims=True)
    s_top = jnp.max(sl, axis=0, keepdims=True)
    over_v = lambda a: jnp.sum(a, axis=0, keepdims=True)

    def merge(values):
        rows = []
        for k in (0, 2):
            top = functools.reduce(jnp.maximum, [v[k : k + 1] for v in values])
            rows += [top, add_all([v[k + 1 : k + 2] * jnp.exp(v[k : k + 1] - top) for v in values])]
        return pad(rows + [add_all([v[4:5] for v in values])])

    first = []
    finish(
        exchange(
            1,
            pad([t_top, over_v(jnp.exp(tl - t_top)), s_top, over_v(jnp.exp(sl - s_top)), over_v(onehot * sl)]),
            merge,
            first,
        )
    )
    first = first[0]
    t_lse = first[0:1] + jnp.log(first[1:2])
    s_lse = first[2:3] + jnp.log(first[3:4])
    picked = first[4:5]
    t_logp = t_acc[...] - t_lse
    s_logp = s_acc[...] - s_lse
    a, b = math.log(MIX_WEIGHT) + t_logp, math.log(1.0 - MIX_WEIGHT) + s_logp
    mix_logp = jnp.maximum(a, b) + jnp.log1p(jnp.exp(-jnp.abs(a - b)))
    p_, q = jnp.exp(t_logp), jnp.exp(s_logp)
    gap = s_logp - mix_logp
    q_gap = q * gap
    jsd_part = over_v(MIX_WEIGHT * p_ * (t_logp - mix_logp) + (1.0 - MIX_WEIGHT) * q_gap)
    second = []
    finish(
        exchange(
            2,
            pad([jsd_part, over_v(q_gap), over_v(q_gap * s_logp), over_v(q * s_logp)]),
            add_all,
            second,
        )
    )
    second = second[0]
    jsd, kl = second[0:1], second[1:2]
    weights = mask[...].astype(F32)
    count = jnp.sum(weights, axis=1, keepdims=True)
    loss = jnp.sum(weights * (jsd + NLL_WEIGHT * (s_lse - picked)), axis=1, keepdims=True) / count
    loss_out[...] = jnp.broadcast_to(loss, loss_out.shape)
    row_scale = LOSS_SCALE * weights / count
    rest = 1.0 - MIX_WEIGHT
    row_dot = row_scale * (
        rest * (second[2:3] - kl * second[3:4]) + NLL_WEIGHT * (second[3:4] - (picked - s_lse))
    ) / DS
    dot_col[...] = column(row_dot)
    logit_grad = row_scale * (q * (rest * gap - rest * kl) + NLL_WEIGHT * (q - onehot))
    lg[...] = logit_grad.T.reshape(16, 2, 8, WIDTH)
    lhs = jnp.concatenate([lg[:, 1 - c].reshape(128, WIDTH), lg[:, c].reshape(128, WIDTH)], axis=0).astype(BF16)

    sibling = to_c(1 - c)

    def sib_copy(v):
        return remote(sib_out.at[v], sib_in.at[v], sib_send_sem.at[v], sib_recv_sem.at[v], sibling)

    def grad_step(v, carry):
        y_, zh_ = lax.div(v, 2), lax.rem(v, 2)
        halves = []
        for h in range(2):
            w = s_w[pl.ds(pl.multiple_of(v * 1024 + h * 512, 512), 512), :]
            halves.append(
                lax.dot_general(lhs, w, (((1,), (1,)), ((), ())), preferred_element_type=F32).reshape(2, 16, 8, 512)
            )
        both = jnp.concatenate(halves, axis=2).astype(BF16)
        sib_out[v] = both[0]
        sib_copy(v).start()
        for i in range(16):
            ra[i % 4, y_, zh_ * 4 + i // 4] = both[1, i, :, :256]
            rb[y_, i % 4, zh_ * 4 + i // 4] = both[1, i, :, 256:]
        return carry

    lax.fori_loop(0, 8, grad_step, 0)

    def sib_step(v, carry):
        y_, zh_ = lax.div(v, 2), lax.rem(v, 2)
        sib_copy(v).wait()
        for i in range(16):
            got = sib_in[v, i].astype(F32)
            at_a = (i % 4, y_, zh_ * 4 + i // 4)
            at_b = (y_, i % 4, zh_ * 4 + i // 4)
            ra[at_a] = (ra[at_a].astype(F32) + got[:, :256]).astype(BF16)
            rb[at_b] = (rb[at_b].astype(F32) + got[:, 256:]).astype(BF16)
        return carry

    lax.fori_loop(0, 8, sib_step, 0)

    def scatter(axis, src, landing, part, phase):
        n, me, to = axis
        return all_partners(
            n, me, to,
            lambda j: src.at[j],
            lambda j: landing.at[j],
            lambda k: rs_send.at[part, phase, k],
            lambda j: rs_recv.at[part, phase, j],
        )

    def add_up(axis, src, landing, out):
        n, me, _ = axis

        def total(at):
            value = src[(me,) + at].astype(F32)
            for k in range(1, n):
                value = value + landing[(lax.rem(me + k, n),) + at].astype(F32)
            return value

        if out is None:
            return total(())
        lead = out.shape[:-2]

        def step(i, carry):
            for j in range(lead[-1]):
                at = (i, j) if len(lead) == 2 else (j,)
                out[at] = total(at).astype(BF16)
            return carry

        if len(lead) == 2:
            lax.fori_loop(0, lead[0], step, 0)
        else:
            step(0, 0)

    wait_a = scatter(axis_x, ra, ra_in1, 0, 0)
    wait_b = scatter(axis_y, rb, rb_in1, 1, 0)
    wait_a()
    add_up(axis_x, ra, ra_in1, ra2)
    wait_a = scatter(axis_y, ra2, ra_in2, 0, 1)
    wait_b()
    add_up(axis_y, rb, rb_in1, rb2)
    wait_b = scatter(axis_x, rb2, rb_in2, 1, 1)
    wait_a()
    add_up(axis_y, ra2, ra_in2, ra3)
    wait_a = scatter(axis_z, ra3, ra_in3, 0, 2)
    wait_b()
    add_up(axis_x, rb2, rb_in2, rb3)
    wait_b = scatter(axis_z, rb3, rb_in3, 1, 2)
    wait_a()
    total_a = add_up(axis_z, ra3, ra_in3, None)
    wait_b()
    total_b = add_up(axis_z, rb3, rb_in3, None)
    normed_grad = jnp.concatenate([total_a, total_b], axis=1)

    own = pl.ds(pl.multiple_of(dp * 8, 8), 8)
    inv = wide(s_inv[own, :])
    dots = wide(dot_col[own, :])
    pieces = []
    for h in range(2):
        grad = normed_grad[h * 8 : h * 8 + 8]
        scaled = own_rows[:, h * 512 : (h + 1) * 512] * inv
        gain = s_gain[pl.ds(vo * 2 + h, 1), :]
        grad_out[:, h * 512 : (h + 1) * 512] = inv * (grad * gain - scaled * dots)
        row = jnp.sum(grad * scaled, axis=0, keepdims=True)
        pieces += [row[:, k * 128 : (k + 1) * 128] for k in range(4)]
    value = jnp.concatenate(pieces, axis=0)
    base = 0
    for (n, me, to), buf in ((axis_c, gg_c), (axis_x, gg_x), ((4, zl, to_zl), gg_z)):
        buf[me] = value
        all_partners(
            n, me, to,
            lambda j: buf.at[me],
            lambda j: buf.at[j],
            lambda k: gg_send.at[base + k],
            lambda j: gg_recv.at[base + j],
        )()
        value = add_all([buf[j] for j in range(n)])
        base += n
    gain_out[...] = value


def shards(t_rows, t_gain, t_head, s_rows, s_gain, s_head, ids, mask):
    vmem = pl.BlockSpec(memory_space=pltpu.VMEM)
    hbm = pl.BlockSpec(memory_space=pl.ANY)
    dma = pltpu.SemaphoreType.DMA
    scratch = [
        pltpu.VMEM((2, Z, Y, X, 16, 512), BF16),
        pltpu.VMEM((2, X, Y, Z, 16, 512), BF16),
        pltpu.VMEM((2, Y, X, Z, 16, 512), BF16),
        pltpu.VMEM((DT, WIDTH), BF16),
        pltpu.VMEM((DS, WIDTH), BF16),
        pltpu.VMEM((TOKENS, 128), F32),
        pltpu.VMEM((TOKENS, 128), F32),
        pltpu.VMEM((TOKENS, WIDTH), F32),
        pltpu.VMEM((TOKENS, WIDTH), F32),
        pltpu.VMEM((TOKENS, 128), F32),
        pltpu.VMEM((16, 2, 8, WIDTH), F32),
        pltpu.VMEM((8, 16, 16, 512), BF16),
        pltpu.VMEM((8, 16, 16, 512), BF16),
        pltpu.VMEM((X, Y, Z, 16, 256), BF16),
        pltpu.VMEM((Y, X, Z, 16, 256), BF16),
        pltpu.VMEM((X, Y, Z, 16, 256), BF16),
        pltpu.VMEM((Y, X, Z, 16, 256), BF16),
        pltpu.VMEM((Y, Z, 16, 256), BF16),
        pltpu.VMEM((X, Z, 16, 256), BF16),
        pltpu.VMEM((Y, Z, 16, 256), BF16),
        pltpu.VMEM((X, Z, 16, 256), BF16),
        pltpu.VMEM((Z, 16, 256), BF16),
        pltpu.VMEM((Z, 16, 256), BF16),
        pltpu.VMEM((Z, 16, 256), BF16),
        pltpu.VMEM((Z, 16, 256), BF16),
        pltpu.VMEM((3, 2, 8, TOKENS), F32),
        pltpu.VMEM((3, X, 8, TOKENS), F32),
        pltpu.VMEM((3, Y, 8, TOKENS), F32),
        pltpu.VMEM((3, Z, 8, TOKENS), F32),
        pltpu.VMEM((2, 8, 128), F32),
        pltpu.VMEM((X, 8, 128), F32),
        pltpu.VMEM((4, 8, 128), F32),
        dma((2,)),
        dma((3, 2, 8)),
        dma((3, 2, 8)),
        dma((3, 2, 7)),
        dma((3, 2, 7)),
        dma((3, 15)),
        dma((3, 15)),
        dma((3, 18)),
        dma((3, 18)),
        dma((8,)),
        dma((8,)),
        dma((2, 3, 8)),
        dma((2, 3, 8)),
        dma((10,)),
        dma((10,)),
    ]
    flops = 2 * TOKENS * WIDTH * (DT + 2 * DS)
    loss, grad, gain = pl.pallas_call(
        kernel,
        out_shape=(
            jax.ShapeDtypeStruct((8, 128), F32),
            jax.ShapeDtypeStruct(s_rows.shape, F32),
            jax.ShapeDtypeStruct((8, 128), F32),
        ),
        in_specs=[vmem, vmem, hbm, vmem, vmem, hbm, vmem, vmem],
        out_specs=(vmem, vmem, vmem),
        scratch_shapes=scratch,
        compiler_params=pltpu.CompilerParams(
            collective_id=0, has_side_effects=True, vmem_limit_bytes=56 * 1024 * 1024
        ),
        cost_estimate=pl.CostEstimate(flops=flops, bytes_accessed=2 * WIDTH * (DT + DS), transcendentals=0),
    )(
        t_rows,
        t_gain.astype(F32).reshape(DT // 512, 512),
        t_head,
        s_rows,
        s_gain.astype(F32).reshape(DS // 512, 512),
        s_head,
        ids.reshape(1, TOKENS),
        mask.reshape(1, TOKENS),
    )
    return loss[0, 0], grad.astype(BF16), gain.reshape(1024)


def solution(mesh):
    return jax.shard_map(
        shards,
        mesh=mesh,
        in_specs=(
            P("vocab", "dp"),
            P(),
            P(None, ("dp", "vocab")),
            P("dp", "vocab"),
            P(),
            P(None, ("dp", "vocab")),
            P(),
            P(),
        ),
        out_specs=(P(), P("dp", "vocab"), P("vocab")),
        check_vma=False,
    )
```

```python
import functools
import math

import jax
import jax.numpy as jnp
from jax import lax
from jax.experimental import pallas as pl
from jax.experimental.pallas import tpu as pltpu
from jax.sharding import PartitionSpec as P

EPSILON = 1e-05
MIX_WEIGHT = 0.3
NLL_WEIGHT = 0.03
LOSS_SCALE = 8192.0
MESH = pl.DeviceIdType.MESH
F32 = jnp.float32
BF16 = jnp.bfloat16
X, Y, Z = 4, 4, 8
TOKENS, DT, DS, WIDTH = 256, 16384, 8192, 256


def kernel(
    t_rows, t_gain_in, t_head, s_rows, s_gain_in, s_head, ids, mask,
    loss_out, grad_out, gain_out,
    g0, g1, g2, t_w, s_w, t_gain, s_gain, t_inv, s_inv, t_acc0, t_acc1, t_acc, s_acc, dot_col, lg,
    sib_out, sib_in, raf, rbf, ra_out, rb_out, ra_via, rb_via, ra_in, rb_in,
    raf2, rbf2, ra2, rb2, ra_in2, rb_in2, raf3, rbf3, ra3, rb3, ra_in3, rb_in3,
    st_c, st_p, st_z, gp_c, gp1, gp_y, gp_x, gp3, gp_z,
    head_sem, a_send, a_recv, b_send, b_recv, ring_send, ring_recv, core_send, core_recv,
    st_send, st_recv, sib_send_sem, sib_recv_sem, first_send, first_recv, rs_send, rs_recv, gp_send, gp_recv,
):
    dp = lax.axis_index("dp")
    vo = lax.axis_index("vocab")
    c = lax.rem(dp, 2)
    x = lax.rem(lax.div(dp, 2), X)
    zl = lax.div(dp, 2 * X)
    y = lax.div(vo, 2)
    zh = lax.rem(vo, 2)
    z = zh * 4 + zl

    def device(x_, y_, z_, c_):
        return ((lax.rem(z_, 4) * X + x_) * 2 + c_, y_ * 2 + lax.div(z_, 4))

    to_c = lambda j: (dp - c + j, vo)
    to_x = lambda j: (dp + (j - x) * 2, vo)
    to_y = lambda j: (dp, vo + (j - y) * 2)
    to_z = lambda j: device(x, y, j, c)
    to_p = lambda j: device(lax.div(j, Y), lax.rem(j, Y), z, c)
    axis_c, axis_x, axis_y, axis_z = (2, c, to_c), (X, x, to_x), (Y, y, to_y), (Z, z, to_z)
    axis_p = (X * Y, x * Y + y, to_p)

    barrier = pltpu.get_barrier_semaphore()
    partners = 0
    for n, me, to in (axis_z, axis_p, axis_c):
        for k in range(1, n):
            pl.semaphore_signal(barrier, inc=1, device_id=to(lax.rem(me + k, n)), device_id_type=MESH)
            partners += 1

    def remote(src, dst, send, recv, to):
        return pltpu.make_async_remote_copy(
            src_ref=src, dst_ref=dst, send_sem=send, recv_sem=recv, device_id=to, device_id_type=MESH
        )

    late = []

    def start(src, dst, send, recv, to):
        copy = remote(src, dst, send, recv, to)
        copy.start()
        late.append(copy)

    def arrived(dst, send, recv, to):
        remote(dst, dst, send, recv, to).wait_recv()

    p0 = x * Y + y
    g0[c, z, p0] = t_rows[0:16, :]
    g1[c, x, y, z] = t_rows[16:32, :]
    own_rows = s_rows[...].astype(F32)
    g2[c, y, x, z] = jnp.concatenate([own_rows[:, :512], own_rows[:, 512:]], axis=0).astype(BF16)

    def lane_sums(block):
        total = block[:, 0:128]
        for k in range(1, block.shape[1] // 128):
            total = total + block[:, k * 128 : (k + 1) * 128]
        total = jnp.concatenate([total] * (TOKENS // total.shape[0]), axis=0)
        return jnp.sum(total.T, axis=0, keepdims=True)

    lanes = lax.broadcasted_iota(jnp.int32, (1, TOKENS), 1)
    t_own = t_rows[...].astype(F32)
    t_squares = jnp.where(lax.div(lanes, 32) == vo, lane_sums(t_own * t_own), 0.0)
    s_squares = jnp.where(lax.div(lanes, 8) == dp, lane_sums(own_rows * own_rows), 0.0)
    pad = lambda rows: jnp.concatenate(rows + [jnp.zeros((8 - len(rows), TOKENS), F32)], axis=0)
    squares_value = pad([t_squares, s_squares])

    pl.semaphore_wait(barrier, partners)

    def all_partners(axis, src, dst, send, recv):
        n, me, to = axis
        arrivals = []
        for k in range(1, n):
            j = lax.rem(me + k, n)
            start(src(j), dst(me), send(k), recv(me), to(j))
            arrivals.append(remote(dst(j), dst(j), send(k), recv(j), to(j)))

        def wait():
            for arrival in arrivals:
                arrival.wait_recv()

        return wait

    def exchange(r, value, combine, result):
        base = 0
        for axis, buf in ((axis_c, st_c), (axis_p, st_p), (axis_z, st_z)):
            n, me, _ = axis
            buf[r, me] = value
            wait = all_partners(
                axis,
                lambda j: buf.at[r, me],
                lambda j: buf.at[r, j],
                lambda k: st_send.at[r, base + k],
                lambda j: st_recv.at[r, base + j],
            )
            yield
            wait()
            value = combine([buf[r, j] for j in range(n)])
            base += n
        result.append(value)

    def finish(steps):
        for _ in steps:
            pass

    def add_all(values):
        return functools.reduce(lambda a, b: a + b, values)

    class Rows:
        def __init__(self, p, g, a, b, cc):
            self.p, self.g, self.a, self.b, self.c = p, g, a, b, cc
            step = lambda axis: tuple(axis[2](lax.rem(axis[1] + k, 4)) for k in (1, 3))
            self.to_b, self.to_c = step(b), step(cc)
            self.ready = set()

        def begin(self):
            mine, theirs = self.c[1], self.b[1]
            self.wait_a = all_partners(
                self.a,
                lambda j: self.g.at[c, mine, theirs, self.a[1]],
                lambda j: self.g.at[c, mine, theirs, j],
                lambda k: a_send.at[self.p, k],
                lambda j: a_recv.at[self.p, j],
            )

        def row(self, core, plane, r):
            return self.g.at[core, lax.rem(self.c[1] + plane, 4), lax.rem(self.b[1] + r, 4)]

        def cross(self, plane, r):
            k = plane * 4 + r
            ref = self.row(c, plane, r)
            start(ref, ref, core_send.at[self.p, k], core_recv.at[self.p, k], to_c(1 - c))

        def crossed(self, plane):
            for r in range(4):
                k = plane * 4 + r
                arrived(self.row(1 - c, plane, r), core_send.at[self.p, k], core_recv.at[self.p, k], to_c(1 - c))

        def half(self, r, way):
            return self.row(c, 0, r).at[4 * way : 4 * way + 4]

        def send_b(self, way, item):
            ref = self.row(c, 0, 0) if item == 0 else self.half(3 if way == 0 else 1, way)
            start(ref, ref, b_send.at[self.p, way, item], b_recv.at[self.p, way, item], self.to_b[way])

        def take_b(self, item):
            for way in range(2):
                ref = self.row(c, 0, 3 if way == 0 else 1) if item == 0 else self.half(2, way)
                arrived(ref, b_send.at[self.p, way, item], b_recv.at[self.p, way, item], self.to_b[way])
                if item == 0:
                    self.send_b(way, 1)
            if item == 0:
                self.send_c(0, 1)
                self.send_c(1, 3)
                self.cross(0, 1)
                self.cross(0, 3)
            else:
                self.send_c(0, 2)
                self.send_c(1, 2)
                self.cross(0, 2)

        def send_c(self, way, r, hop=0):
            ref = self.row(c, 0 if hop == 0 else (3 if way == 0 else 1), r)
            k = r + 4 * hop
            start(ref, ref, ring_send.at[self.p, way, k], ring_recv.at[self.p, way, k], self.to_c[way])

        def take_c(self, way, r, hop=0):
            plane = 2 if hop else (3 if way == 0 else 1)
            k = r + 4 * hop
            arrived(self.row(c, plane, r), ring_send.at[self.p, way, k], ring_recv.at[self.p, way, k], self.to_c[way])
            if hop == 0 and r in ((0, 1), (3, 2))[way]:
                self.send_c(way, r, 1)
            self.cross(plane, r)

        def after_a(self):
            self.wait_a()
            for way in range(2):
                self.send_b(way, 0)
                self.send_c(way, 0)
            self.cross(0, 0)

    class Ring:
        def __init__(self, g, n, me, to):
            self.g, self.n, self.me = g, n, me
            self.to = (to(lax.rem(me + 1, n)), to(lax.rem(me + n - 1, n)))

        def piece(self, way, i, distance, core):
            half = i % 2 if way == 0 else 1 - i % 2
            plane = lax.rem(self.me + (self.n - distance if way == 0 else distance), self.n)
            return self.g.at[core, plane, 8 * half : 8 * half + 8]

        def send(self, way, i):
            ref = self.piece(way, i, i // 2, c)
            start(ref, ref, ring_send.at[0, way, i], ring_recv.at[0, way, i], self.to[way])

        def begin(self):
            for i in range(2):
                for way in range(2):
                    self.send(way, i)
            ref = self.g.at[c, self.me]
            start(ref, ref, core_send.at[0, 0], core_recv.at[0, 0], to_c(1 - c))

        def event(self, i):
            for way in range(2):
                ref = self.piece(way, i, i // 2 + 1, c)
                arrived(ref, ring_send.at[0, way, i], ring_recv.at[0, way, i], self.to[way])
                if i + 2 <= self.n - 2:
                    self.send(way, i + 2)
                k = 1 + 2 * i + way
                start(ref, ref, core_send.at[0, k], core_recv.at[0, k], to_c(1 - c))

        def crossed(self, i):
            for way in range(2):
                k = 1 + 2 * i + way
                arrived(self.piece(way, i, i // 2 + 1, 1 - c), core_send.at[0, k], core_recv.at[0, k], to_c(1 - c))

        def crossed_own(self):
            arrived(self.g.at[1 - c, self.me], core_send.at[0, 0], core_recv.at[0, 0], to_c(1 - c))

    part1 = Rows(1, g1, axis_z, axis_y, axis_x)
    part2 = Rows(2, g2, axis_z, axis_x, axis_y)
    part0 = Ring(g0, Z, z, to_z)
    both = (part1, part2)

    wide = lambda block: jnp.concatenate([block] * 4, axis=1)

    def student_planes(count, plane_of):
        def step(i, carry):
            y_, zh_ = plane_of(lax.div(i, 2)), lax.rem(i, 2)
            v = y_ * 2 + zh_
            gains = [s_gain[pl.ds(v * 2 + h, 1), :] for h in range(2)]
            blocks = ([], [])
            for pair in range(16):
                scaled = []
                for core in range(2):
                    raw = g2[core, y_, pair % 4, zh_ * 4 + pair // 4].astype(F32)
                    inv = wide(s_inv[pair, core])
                    scaled.append((raw[0:8] * inv, raw[8:16] * inv))
                for h in range(2):
                    rows = jnp.concatenate([scaled[0][h], scaled[1][h]], axis=0) * gains[h]
                    blocks[h].append(rows.astype(BF16))
            total = s_acc[...]
            for h in range(2):
                w = s_w[pl.ds(pl.multiple_of(v * 1024 + h * 512, 512), 512), :]
                total += jnp.dot(jnp.concatenate(blocks[h], axis=0), w, preferred_element_type=F32)
            s_acc[...] = total
            return carry

        lax.fori_loop(0, 2 * count, step, 0)

    def teacher_step(acc, p, load, d):
        gain = t_gain[pl.ds(d, 1), :]
        blocks = []
        for v in range(8):
            inv = wide(t_inv[v * 32 + p * 16 : v * 32 + p * 16 + 16, :])
            blocks.append((load(v).astype(F32) * inv * gain).astype(BF16))
        w = t_w[pl.ds(pl.multiple_of(d * 512, 512), 512), :]
        acc[...] += jnp.dot(jnp.concatenate(blocks, axis=0), w, preferred_element_type=F32)

    def teacher_x(count, plane_of):
        def step(i, carry):
            x_, zl_, c_ = plane_of(lax.div(i, 8)), lax.div(lax.rem(i, 8), 2), lax.rem(i, 2)
            load = lambda v: g1[c_, x_, v // 2, (v % 2) * 4 + zl_]
            teacher_step(t_acc1, 1, load, (zl_ * X + x_) * 2 + c_)
            return carry

        lax.fori_loop(0, 8 * count, step, 0)

    def teacher_z(count, plane_of):
        def step(i, carry):
            zl_, x_, c_ = plane_of(lax.div(i, 8)), lax.div(lax.rem(i, 8), 2), lax.rem(i, 2)
            load = lambda v: g0[c_, (v % 2) * 4 + zl_, x_ * Y + v // 2]
            teacher_step(t_acc0, 0, load, (zl_ * X + x_) * 2 + c_)
            return carry

        lax.fori_loop(0, 8 * count, step, 0)

    for part in both:
        part.begin()
    wait_plane = all_partners(
        axis_p,
        lambda j: g0.at[c, z, p0],
        lambda j: g0.at[c, z, j],
        lambda k: a_send.at[0, k],
        lambda j: a_recv.at[0, j],
    )
    t_load = pltpu.make_async_copy(t_head, t_w, head_sem.at[0])
    s_load = pltpu.make_async_copy(s_head, s_w, head_sem.at[1])
    t_load.start()
    s_load.start()
    squares = []
    round0 = exchange(0, squares_value, add_all, squares)
    next(round0)
    t_gain[...] = t_gain_in[...].astype(F32).reshape(t_gain.shape)
    s_gain[...] = s_gain_in[...].astype(F32).reshape(s_gain.shape)
    for acc in (t_acc0, t_acc1, s_acc):
        acc[...] = jnp.zeros_like(acc)
    next(round0)
    for part in both:
        part.after_a()
    wait_plane()
    part0.begin()
    for part in both:
        part.take_b(0)
    for part in both:
        part.take_c(0, 0)
        part.take_c(1, 0)
        part.send_c(0, 3)
        part.send_c(1, 1)
    next(round0)
    part0.event(0)
    part0.event(1)
    for part in both:
        part.take_b(1)
    finish(round0)
    squares = squares[0]
    t_inv_row = lax.rsqrt(squares[0:1] / DT + EPSILON)
    s_inv_row = lax.rsqrt(squares[1:2] / DS + EPSILON)
    column = lambda row: jnp.broadcast_to(row, (128, TOKENS)).T
    t_inv[...] = column(t_inv_row)
    s_inv[...] = column(s_inv_row).reshape(s_inv.shape)
    for part in both:
        part.take_c(0, 1)
        part.take_c(1, 3)
    part0.event(2)
    t_load.wait()
    s_load.wait()
    part2.crossed(0)
    student_planes(1, lambda i: y)
    part0.event(3)
    for part in both:
        part.take_c(0, 3)
        part.take_c(1, 1)
    part1.crossed(0)
    teacher_x(1, lambda i: x)
    for part in both:
        part.take_c(0, 2)
        part.take_c(1, 2)
    part0.event(4)
    for i in range(4):
        part0.crossed(i)
    teacher_z(1, lambda i: lax.rem(zl + 2, 4))
    part0.event(5)
    part2.crossed(1)
    part2.crossed(3)
    student_planes(2, lambda i: lax.rem(y + 1 + 2 * i, Y))
    for part in both:
        for way, r in ((0, 0), (0, 1), (1, 3), (1, 2)):
            part.take_c(way, r, 1)
    part0.event(6)
    part1.crossed(1)
    part1.crossed(3)
    teacher_x(2, lambda i: lax.rem(x + 1 + 2 * i, X))
    part0.crossed(4)
    part0.crossed(5)
    teacher_z(2, lambda i: lax.rem(zl + 1 + 2 * i, 4))
    part2.crossed(2)
    student_planes(1, lambda i: lax.rem(y + 2, Y))
    part1.crossed(2)
    teacher_x(1, lambda i: lax.rem(x + 2, X))
    part0.crossed(6)
    part0.crossed_own()
    teacher_z(1, lambda i: zl)

    order = []
    for v in range(8):
        order += [t_acc0[v * 16 : v * 16 + 16, :], t_acc1[v * 16 : v * 16 + 16, :]]
    tl = jnp.concatenate(order, axis=0).T
    sl = s_acc[...].T
    t_acc[...] = tl
    s_acc[...] = sl
    column_start = (dp * 8 + vo) * WIDTH
    onehot = (column_start + lax.broadcasted_iota(jnp.int32, (WIDTH, TOKENS), 0) == ids[...]).astype(F32)
    t_top = jnp.max(tl, axis=0, keepdims=True)
    s_top = jnp.max(sl, axis=0, keepdims=True)
    over_v = lambda a: jnp.sum(a, axis=0, keepdims=True)

    def merge(values):
        rows = []
        for k in (0, 2):
            top = functools.reduce(jnp.maximum, [v[k : k + 1] for v in values])
            rows += [top, add_all([v[k + 1 : k + 2] * jnp.exp(v[k : k + 1] - top) for v in values])]
        return pad(rows + [add_all([v[4:5] for v in values])])

    first = []
    finish(
        exchange(
            1,
            pad([t_top, over_v(jnp.exp(tl - t_top)), s_top, over_v(jnp.exp(sl - s_top)), over_v(onehot * sl)]),
            merge,
            first,
        )
    )
    first = first[0]
    t_lse = first[0:1] + jnp.log(first[1:2])
    s_lse = first[2:3] + jnp.log(first[3:4])
    picked = first[4:5]
    t_logp = t_acc[...] - t_lse
    s_logp = s_acc[...] - s_lse
    a, b = math.log(MIX_WEIGHT) + t_logp, math.log(1.0 - MIX_WEIGHT) + s_logp
    mix_logp = jnp.maximum(a, b) + jnp.log1p(jnp.exp(-jnp.abs(a - b)))
    p_, q = jnp.exp(t_logp), jnp.exp(s_logp)
    gap = s_logp - mix_logp
    q_gap = q * gap
    jsd_part = over_v(MIX_WEIGHT * p_ * (t_logp - mix_logp) + (1.0 - MIX_WEIGHT) * q_gap)
    second = []
    finish(
        exchange(
            2,
            pad([jsd_part, over_v(q_gap), over_v(q_gap * s_logp), over_v(q * s_logp)]),
            add_all,
            second,
        )
    )
    second = second[0]
    jsd, kl = second[0:1], second[1:2]
    weights = mask[...].astype(F32)
    count = jnp.sum(weights, axis=1, keepdims=True)
    row_scale = LOSS_SCALE * weights / count
    rest = 1.0 - MIX_WEIGHT
    logit_grad = row_scale * (q * (rest * gap - rest * kl) + NLL_WEIGHT * (q - onehot))
    lg[...] = logit_grad.T.reshape(16, 2, 8, WIDTH)
    lhs = jnp.concatenate([lg[:, 1 - c].reshape(128, WIDTH), lg[:, c].reshape(128, WIDTH)], axis=0).astype(BF16)

    sibling = to_c(1 - c)

    def sib_copy(v):
        return remote(sib_out.at[v], sib_in.at[v], sib_send_sem.at[v], sib_recv_sem.at[v], sibling)

    def grad_step(v, carry):
        y_, zh_ = lax.div(v, 2), lax.rem(v, 2)
        halves = []
        for h in range(2):
            w = s_w[pl.ds(pl.multiple_of(v * 1024 + h * 512, 512), 512), :]
            halves.append(
                lax.dot_general(lhs, w, (((1,), (1,)), ((), ())), preferred_element_type=F32).reshape(2, 16, 8, 512)
            )
        chunks = jnp.concatenate(halves, axis=2)
        sib_out[v] = chunks[0].astype(BF16)
        sib_copy(v).start()
        for i in range(16):
            raf[i % 4, y_, zh_ * 4 + i // 4] = chunks[1, i, :, :256]
            rbf[y_, i % 4, zh_ * 4 + i // 4] = chunks[1, i, :, 256:]
        return carry

    lax.fori_loop(0, 8, grad_step, 0)

    def sib_step(v, carry):
        y_, zh_ = lax.div(v, 2), lax.rem(v, 2)
        sib_copy(v).wait()
        for i in range(16):
            got = sib_in[v, i].astype(F32)
            at_a = (i % 4, y_, zh_ * 4 + i // 4)
            at_b = (y_, i % 4, zh_ * 4 + i // 4)
            sum_a = raf[at_a] + got[:, :256]
            sum_b = rbf[at_b] + got[:, 256:]
            raf[at_a] = sum_a
            rbf[at_b] = sum_b
            ra_out[at_a] = sum_a.astype(BF16)
            rb_out[at_b] = sum_b.astype(BF16)
        return carry

    class First:
        def __init__(self, part, axis, own, out, via, landing):
            self.part, self.own, self.out, self.via, self.landing = part, own, out, via, landing
            _, self.me, to = axis
            self.to = (to(lax.rem(self.me + 1, 4)), to(lax.rem(self.me + 3, 4)))

        def plane(self, k):
            return lax.rem(self.me + k, 4)

        def send(self, way, item):
            half = way if item != 1 else 1 - way
            k = 2 if item == 0 else (1 if way == 0 else 3)
            src = self.out.at[self.plane(k), 2 * half : 2 * half + 2]
            dst = self.via.at[way] if item == 0 else self.landing.at[way, 2 * half : 2 * half + 2]
            start(src, dst, first_send.at[self.part, way, item], first_recv.at[self.part, way, item], self.to[way])

        def take(self, way, item):
            half = way if item != 1 else 1 - way
            dst = self.via.at[way] if item == 0 else self.landing.at[way, 2 * half : 2 * half + 2]
            arrived(dst, first_send.at[self.part, way, item], first_recv.at[self.part, way, item], self.to[way])

        def middle(self):
            for way in range(2):
                self.take(way, 0)
                to = self.plane(1 if way == 0 else 3)

                def step(i, carry, way=way, to=to):
                    row = 2 * way + lax.div(i, 8)
                    at = lax.rem(i, 8)
                    total = self.own[to, row, at] + self.via[way, lax.div(i, 8), at].astype(F32)
                    self.out[to, row, at] = total.astype(BF16)
                    return carry

                lax.fori_loop(0, 16, step, 0, unroll=4)
                self.send(way, 2)

        def last(self, total, out):
            for way in range(2):
                self.take(way, 1)
                self.take(way, 2)

            def step(i, carry):
                row, at = lax.div(i, 8), lax.rem(i, 8)
                value = self.own[self.me, row, at] + (
                    self.landing[0, row, at].astype(F32) + self.landing[1, row, at].astype(F32)
                )
                total[row, at] = value
                out[row, at] = value.astype(BF16)
                return carry

            lax.fori_loop(0, 32, step, 0, unroll=4)

    first_a = First(0, axis_x, raf, ra_out, ra_via, ra_in)
    first_b = First(1, axis_y, rbf, rb_out, rb_via, rb_in)
    lax.fori_loop(0, 4, sib_step, 0)
    first_a.send(0, 0)
    first_a.send(1, 1)
    lax.fori_loop(4, 8, sib_step, 0)
    first_a.send(1, 0)
    for way in range(2):
        first_b.send(way, 0)
    first_a.send(0, 1)
    for way in range(2):
        first_b.send(way, 1)

    def gain_step(v, carry):
        y_, zh_ = lax.div(v, 2), lax.rem(v, 2)
        total = jnp.zeros((16, 512), F32)
        for i in range(16):
            z_ = zh_ * 4 + i // 4
            inv = s_inv[i, c]
            scaled = g2[c, y_, i % 4, z_].astype(F32) * wide(jnp.concatenate([inv, inv], axis=0))
            total += scaled * jnp.concatenate([raf[i % 4, y_, z_], rbf[y_, i % 4, z_]], axis=1)
        pieces = []
        for h in range(2):
            row = jnp.sum(total[8 * h : 8 * h + 8], axis=0, keepdims=True)
            pieces += [row[:, k * 128 : (k + 1) * 128] for k in range(4)]
        gp_c[c, y_, zh_] = jnp.concatenate(pieces, axis=0)
        return carry

    lax.fori_loop(0, 8, gain_step, 0)
    gain_wait = all_partners(
        axis_c, lambda j: gp_c.at[c], lambda j: gp_c.at[j], lambda k: gp_send.at[0, k], lambda j: gp_recv.at[0, j]
    )
    first_a.middle()
    gain_wait()
    gp1[...] = gp_c[0] + gp_c[1]
    gp_y[y] = gp1[y]
    gain_wait = all_partners(
        axis_y, lambda j: gp1.at[j], lambda j: gp_y.at[j], lambda k: gp_send.at[1, k], lambda j: gp_recv.at[1, j]
    )
    first_b.middle()

    def scatter(axis, src, landing, part, phase):
        return all_partners(
            axis,
            lambda j: src.at[j],
            lambda j: landing.at[j],
            lambda k: rs_send.at[part, phase, k],
            lambda j: rs_recv.at[part, phase, j],
        )

    def second_sum(axis, own, landing, total, out):
        n, me, _ = axis
        for at in range(Z):
            value = own[me, at]
            for k in range(1, n):
                value = value + landing[lax.rem(me + k, n), at].astype(F32)
            total[at] = value
            out[at] = value.astype(BF16)

    def third_sum(own, landing):
        value = own[z]
        for k in range(1, Z):
            value = value + landing[lax.rem(z + k, Z)].astype(F32)
        return value

    first_a.last(raf2, ra2)
    wait_a = scatter(axis_y, ra2, ra_in2, 0, 0)
    first_b.last(rbf2, rb2)
    wait_b = scatter(axis_x, rb2, rb_in2, 1, 0)
    gain_wait()
    gp_x[x] = add_all([gp_y[j] for j in range(Y)])
    gain_wait = all_partners(
        axis_x, lambda j: gp_x.at[x], lambda j: gp_x.at[j], lambda k: gp_send.at[2, k], lambda j: gp_recv.at[2, j]
    )

    row_dot = row_scale * (
        rest * (second[2:3] - kl * second[3:4]) + NLL_WEIGHT * (second[3:4] - (picked - s_lse))
    ) / DS
    dot_col[...] = column(row_dot).reshape(dot_col.shape)
    loss = jnp.sum(weights * (jsd + NLL_WEIGHT * (s_lse - picked)), axis=1, keepdims=True) / count
    loss_out[...] = jnp.broadcast_to(loss, loss_out.shape)

    wait_a()
    second_sum(axis_y, raf2, ra_in2, raf3, ra3)
    wait_a = scatter(axis_z, ra3, ra_in3, 0, 1)
    wait_b()
    second_sum(axis_x, rbf2, rb_in2, rbf3, rb3)
    wait_b = scatter(axis_z, rb3, rb_in3, 1, 1)
    gain_wait()
    gp3[...] = add_all([gp_x[j] for j in range(X)])
    gp_z[z] = gp3[zh]
    gain_wait = all_partners(
        axis_z,
        lambda j: gp3.at[lax.div(j, 4)],
        lambda j: gp_z.at[j],
        lambda k: gp_send.at[3, k],
        lambda j: gp_recv.at[3, j],
    )
    wait_a()
    wait_b()
    normed_grad = jnp.concatenate([third_sum(raf3, ra_in3), third_sum(rbf3, rb_in3)], axis=1)
    inv = wide(s_inv[lax.div(dp, 2), c])
    dots = wide(dot_col[lax.div(dp, 2), c])
    for h in range(2):
        grad = normed_grad[h * 8 : h * 8 + 8]
        scaled = own_rows[:, h * 512 : (h + 1) * 512] * inv
        gain = s_gain[pl.ds(vo * 2 + h, 1), :]
        grad_out[:, h * 512 : (h + 1) * 512] = inv * (grad * gain - scaled * dots)
    gain_wait()
    gain_out[...] = add_all([gp_z[j] for j in range(Z)])
    for copy in late:
        copy.wait_send()


def results(loss, grad, gain, loss_out, grad_out, gain_out):
    loss_out[...] = loss[...]
    grad_out[...] = grad[...].astype(BF16)
    gain_out[...] = gain[...]


def shards(t_rows, t_gain, t_head, s_rows, s_gain, s_head, ids, mask):
    vmem = pl.BlockSpec(memory_space=pltpu.VMEM)
    hbm = pl.BlockSpec(memory_space=pl.ANY)
    dma = pltpu.SemaphoreType.DMA
    scratch = [
        pltpu.VMEM((2, Z, X * Y, 16, 512), BF16),
        pltpu.VMEM((2, X, Y, Z, 16, 512), BF16),
        pltpu.VMEM((2, Y, X, Z, 16, 512), BF16),
        pltpu.VMEM((DT, WIDTH), BF16),
        pltpu.VMEM((DS, WIDTH), BF16),
        pltpu.VMEM((DT // 512, 512), F32),
        pltpu.VMEM((DS // 512, 512), F32),
        pltpu.VMEM((TOKENS, 128), F32),
        pltpu.VMEM((16, 2, 8, 128), F32),
        pltpu.VMEM((TOKENS // 2, WIDTH), F32),
        pltpu.VMEM((TOKENS // 2, WIDTH), F32),
        pltpu.VMEM((TOKENS, WIDTH), F32),
        pltpu.VMEM((TOKENS, WIDTH), F32),
        pltpu.VMEM((16, 2, 8, 128), F32),
        pltpu.VMEM((16, 2, 8, WIDTH), F32),
        pltpu.VMEM((8, 16, 16, 512), BF16),
        pltpu.VMEM((8, 16, 16, 512), BF16),
        pltpu.VMEM((X, Y, Z, 16, 256), F32),
        pltpu.VMEM((Y, X, Z, 16, 256), F32),
        pltpu.VMEM((X, Y, Z, 16, 256), BF16),
        pltpu.VMEM((Y, X, Z, 16, 256), BF16),
        pltpu.VMEM((2, 2, Z, 16, 256), BF16),
        pltpu.VMEM((2, 2, Z, 16, 256), BF16),
        pltpu.VMEM((2, Y, Z, 16, 256), BF16),
        pltpu.VMEM((2, X, Z, 16, 256), BF16),
        pltpu.VMEM((Y, Z, 16, 256), F32),
        pltpu.VMEM((X, Z, 16, 256), F32),
        pltpu.VMEM((Y, Z, 16, 256), BF16),
        pltpu.VMEM((X, Z, 16, 256), BF16),
        pltpu.VMEM((Y, Z, 16, 256), BF16),
        pltpu.VMEM((X, Z, 16, 256), BF16),
        pltpu.VMEM((Z, 16, 256), F32),
        pltpu.VMEM((Z, 16, 256), F32),
        pltpu.VMEM((Z, 16, 256), BF16),
        pltpu.VMEM((Z, 16, 256), BF16),
        pltpu.VMEM((Z, 16, 256), BF16),
        pltpu.VMEM((Z, 16, 256), BF16),
        pltpu.VMEM((3, 2, 8, TOKENS), F32),
        pltpu.VMEM((3, X * Y, 8, TOKENS), F32),
        pltpu.VMEM((3, Z, 8, TOKENS), F32),
        pltpu.VMEM((2, Y, 2, 8, 128), F32),
        pltpu.VMEM((Y, 2, 8, 128), F32),
        pltpu.VMEM((Y, 2, 8, 128), F32),
        pltpu.VMEM((X, 2, 8, 128), F32),
        pltpu.VMEM((2, 8, 128), F32),
        pltpu.VMEM((Z, 8, 128), F32),
        dma((2,)),
        dma((3, 16)),
        dma((3, 16)),
        dma((3, 2, 2)),
        dma((3, 2, 2)),
        dma((3, 2, 8)),
        dma((3, 2, 8)),
        dma((3, 16)),
        dma((3, 16)),
        dma((3, 26)),
        dma((3, 26)),
        dma((8,)),
        dma((8,)),
        dma((2, 2, 3)),
        dma((2, 2, 3)),
        dma((2, 2, 8)),
        dma((2, 2, 8)),
        dma((4, 8)),
        dma((4, 8)),
    ]
    flops = 2 * TOKENS * WIDTH * (DT + 2 * DS)
    shapes = (
        jax.ShapeDtypeStruct((8, 128), F32),
        jax.ShapeDtypeStruct(s_rows.shape, F32),
        jax.ShapeDtypeStruct((8, 128), F32),
    )
    values = pl.pallas_call(
        kernel,
        out_shape=shapes,
        in_specs=[vmem, vmem, hbm, vmem, vmem, hbm, vmem, vmem],
        out_specs=(vmem, vmem, vmem),
        scratch_shapes=scratch,
        compiler_params=pltpu.CompilerParams(
            collective_id=0, has_side_effects=True, vmem_limit_bytes=60 * 1024 * 1024
        ),
        cost_estimate=pl.CostEstimate(flops=flops, bytes_accessed=2 * WIDTH * (DT + DS), transcendentals=0),
    )(t_rows, t_gain, t_head, s_rows, s_gain, s_head, ids.reshape(1, TOKENS), mask.reshape(1, TOKENS))
    loss, grad, gain = pl.pallas_call(
        results,
        out_shape=(shapes[0], jax.ShapeDtypeStruct(s_rows.shape, BF16), shapes[2]),
        in_specs=[vmem] * 3,
        out_specs=(vmem, vmem, vmem),
    )(*values)
    return loss[0, 0], grad, gain.reshape(1024)


def solution(mesh):
    return jax.shard_map(
        shards,
        mesh=mesh,
        in_specs=(
            P("vocab", "dp"),
            P(),
            P(None, ("dp", "vocab")),
            P("dp", "vocab"),
            P(),
            P(None, ("dp", "vocab")),
            P(),
            P(),
        ),
        out_specs=(P(), P("dp", "vocab"), P("vocab")),
        check_vma=False,
    )
```

```python
import functools
import math

import jax
import jax.numpy as jnp
from jax import lax
from jax.experimental import pallas as pl
from jax.experimental.pallas import tpu as pltpu
from jax.sharding import PartitionSpec as P

EPSILON = 1e-05
MIX_WEIGHT = 0.3
NLL_WEIGHT = 0.03
LOSS_SCALE = 8192.0
MESH = pl.DeviceIdType.MESH
F32 = jnp.float32
BF16 = jnp.bfloat16
X, Y, Z = 4, 4, 8
TOKENS, DT, DS, WIDTH = 256, 16384, 8192, 256


def kernel(
    t_rows, t_gain_in, t_head, s_rows, s_gain_in, s_head, ids, mask,
    loss_out, grad_out, gain_out,
    g0, g1, g2, t_w, s_w, t_gain, s_gain, t_inv, s_inv, t_acc0, t_acc1, t_acc, s_acc, dot_col, lg,
    sib_out, sib_in, raf, rbf, ra_out, rb_out, ra_via, rb_via, ra_in, rb_in,
    raf2, rbf2, ra2, rb2, ra_in2, rb_in2, raf3, rbf3, ra3, rb3, ra_in3, rb_in3,
    st_c, st_p, st_z, gp_c, gp1, gp_y, gp_x, gp3, gp_z,
    head_sem, a_send, a_recv, b_send, b_recv, ring_send, ring_recv, core_send, core_recv,
    st_send, st_recv, sib_send_sem, sib_recv_sem, first_send, first_recv, rs_send, rs_recv, gp_send, gp_recv,
):
    dp = lax.axis_index("dp")
    vo = lax.axis_index("vocab")
    c = lax.rem(dp, 2)
    x = lax.rem(lax.div(dp, 2), X)
    zl = lax.div(dp, 2 * X)
    y = lax.div(vo, 2)
    zh = lax.rem(vo, 2)
    z = zh * 4 + zl

    def device(x_, y_, z_, c_):
        return ((lax.rem(z_, 4) * X + x_) * 2 + c_, y_ * 2 + lax.div(z_, 4))

    to_c = lambda j: (dp - c + j, vo)
    to_x = lambda j: (dp + (j - x) * 2, vo)
    to_y = lambda j: (dp, vo + (j - y) * 2)
    to_z = lambda j: device(x, y, j, c)
    to_p = lambda j: device(lax.div(j, Y), lax.rem(j, Y), z, c)
    axis_c, axis_x, axis_y, axis_z = (2, c, to_c), (X, x, to_x), (Y, y, to_y), (Z, z, to_z)
    axis_p = (X * Y, x * Y + y, to_p)

    barrier = pltpu.get_barrier_semaphore()
    partners = 0
    for n, me, to in (axis_z, axis_p, axis_c):
        for k in range(1, n):
            pl.semaphore_signal(barrier, inc=1, device_id=to(lax.rem(me + k, n)), device_id_type=MESH)
            partners += 1

    t_load = pltpu.make_async_copy(t_head, t_w, head_sem.at[0])
    s_load = pltpu.make_async_copy(s_head, s_w, head_sem.at[1])
    t_load.start()
    s_load.start()

    def remote(src, dst, send, recv, to):
        return pltpu.make_async_remote_copy(
            src_ref=src, dst_ref=dst, send_sem=send, recv_sem=recv, device_id=to, device_id_type=MESH
        )

    late = []

    def start(src, dst, send, recv, to):
        copy = remote(src, dst, send, recv, to)
        copy.start()
        late.append(copy)

    def arrived(dst, send, recv, to):
        remote(dst, dst, send, recv, to).wait_recv()

    p0 = x * Y + y
    g0[c, z, p0] = t_rows[0:16, :]
    g1[c, x, y, z] = t_rows[16:32, :]
    own_rows = s_rows[...].astype(F32)
    g2[c, y, x, z] = jnp.concatenate([own_rows[:, :512], own_rows[:, 512:]], axis=0).astype(BF16)

    def lane_sums(block):
        total = block[:, 0:128]
        for k in range(1, block.shape[1] // 128):
            total = total + block[:, k * 128 : (k + 1) * 128]
        total = jnp.concatenate([total] * (TOKENS // total.shape[0]), axis=0)
        return jnp.sum(total.T, axis=0, keepdims=True)

    lanes = lax.broadcasted_iota(jnp.int32, (1, TOKENS), 1)
    t_own = t_rows[...].astype(F32)
    t_squares = jnp.where(lax.div(lanes, 32) == vo, lane_sums(t_own * t_own), 0.0)
    s_squares = jnp.where(lax.div(lanes, 8) == dp, lane_sums(own_rows * own_rows), 0.0)

    def pack(rows):
        halves = [row[:, 128 * h : 128 * h + 128] for row in rows for h in range(2)]
        return jnp.concatenate(halves + [jnp.zeros((1, 128), F32)] * (8 - len(halves)), axis=0)

    def unpack(block, k):
        return jnp.concatenate([block[2 * k : 2 * k + 1], block[2 * k + 1 : 2 * k + 2]], axis=1)

    squares_value = pack([t_squares, s_squares])

    t_gain[...] = t_gain_in[...].astype(F32).reshape(t_gain.shape)
    s_gain[...] = s_gain_in[...].astype(F32).reshape(s_gain.shape)
    for acc in (t_acc0, t_acc1, s_acc):
        acc[...] = jnp.zeros_like(acc)

    pl.semaphore_wait(barrier, partners)

    def all_partners(axis, src, dst, send, recv):
        n, me, to = axis
        arrivals = []
        for k in range(1, n):
            j = lax.rem(me + k, n)
            start(src(j), dst(me), send(k), recv(me), to(j))
            arrivals.append(remote(dst(j), dst(j), send(k), recv(j), to(j)))

        def wait():
            for arrival in arrivals:
                arrival.wait_recv()

        return wait

    over_c, over_p, over_z = (axis_c, st_c, 0), (axis_p, st_p, 2), (axis_z, st_z, 18)

    def exchange(r, value, combine, result, steps=(over_c, over_p, over_z)):
        for axis, buf, base in steps:
            n, me, _ = axis
            buf[r, me] = value
            wait = all_partners(
                axis,
                lambda j: buf.at[r, me],
                lambda j: buf.at[r, j],
                lambda k: st_send.at[r, base + k],
                lambda j: st_recv.at[r, base + j],
            )
            yield
            wait()
            value = combine([buf[r, j] for j in range(n)])
        result.append(value)

    def finish(steps):
        for _ in steps:
            pass

    def add_all(values):
        return functools.reduce(lambda a, b: a + b, values)

    class Rows:
        def __init__(self, p, g, a, b, cc):
            self.p, self.g, self.a, self.b, self.c = p, g, a, b, cc
            step = lambda axis: tuple(axis[2](lax.rem(axis[1] + k, 4)) for k in (1, 3))
            self.to_b, self.to_c = step(b), step(cc)
            self.ready = set()

        def begin(self):
            mine, theirs = self.c[1], self.b[1]
            self.wait_a = all_partners(
                self.a,
                lambda j: self.g.at[c, mine, theirs, self.a[1]],
                lambda j: self.g.at[c, mine, theirs, j],
                lambda k: a_send.at[self.p, k],
                lambda j: a_recv.at[self.p, j],
            )

        def row(self, core, plane, r):
            return self.g.at[core, lax.rem(self.c[1] + plane, 4), lax.rem(self.b[1] + r, 4)]

        def cross(self, plane, r):
            k = plane * 4 + r
            ref = self.row(c, plane, r)
            start(ref, ref, core_send.at[self.p, k], core_recv.at[self.p, k], to_c(1 - c))

        def crossed(self, plane):
            for r in range(4):
                k = plane * 4 + r
                arrived(self.row(1 - c, plane, r), core_send.at[self.p, k], core_recv.at[self.p, k], to_c(1 - c))

        def half(self, r, way):
            return self.row(c, 0, r).at[4 * way : 4 * way + 4]

        def send_b(self, way, item):
            ref = self.row(c, 0, 0) if item == 0 else self.half(3 if way == 0 else 1, way)
            start(ref, ref, b_send.at[self.p, way, item], b_recv.at[self.p, way, item], self.to_b[way])

        def take_b(self, item):
            for way in range(2):
                ref = self.row(c, 0, 3 if way == 0 else 1) if item == 0 else self.half(2, way)
                arrived(ref, b_send.at[self.p, way, item], b_recv.at[self.p, way, item], self.to_b[way])
                if item == 0:
                    self.send_b(way, 1)
            if item == 0:
                self.send_c(0, 1)
                self.send_c(1, 3)
                self.cross(0, 1)
                self.cross(0, 3)
            else:
                self.send_c(0, 2)
                self.send_c(1, 2)
                self.cross(0, 2)

        def send_c(self, way, r, hop=0):
            ref = self.row(c, 0 if hop == 0 else (3 if way == 0 else 1), r)
            k = r + 4 * hop
            start(ref, ref, ring_send.at[self.p, way, k], ring_recv.at[self.p, way, k], self.to_c[way])

        def take_c(self, way, r, hop=0):
            plane = 2 if hop else (3 if way == 0 else 1)
            k = r + 4 * hop
            arrived(self.row(c, plane, r), ring_send.at[self.p, way, k], ring_recv.at[self.p, way, k], self.to_c[way])
            if hop == 0 and r in ((0, 1), (3, 2))[way]:
                self.send_c(way, r, 1)
            self.cross(plane, r)

        def after_a(self):
            self.wait_a()
            for way in range(2):
                self.send_b(way, 0)
                self.send_c(way, 0)
            self.cross(0, 0)

    class Ring:
        def __init__(self, g, n, me, to):
            self.g, self.n, self.me = g, n, me
            self.to = (to(lax.rem(me + 1, n)), to(lax.rem(me + n - 1, n)))

        def piece(self, way, i, distance, core):
            half = i % 2 if way == 0 else 1 - i % 2
            plane = lax.rem(self.me + (self.n - distance if way == 0 else distance), self.n)
            return self.g.at[core, plane, 8 * half : 8 * half + 8]

        def send(self, way, i):
            ref = self.piece(way, i, i // 2, c)
            start(ref, ref, ring_send.at[0, way, i], ring_recv.at[0, way, i], self.to[way])

        def begin(self):
            for i in range(2):
                for way in range(2):
                    self.send(way, i)
            ref = self.g.at[c, self.me]
            start(ref, ref, core_send.at[0, 0], core_recv.at[0, 0], to_c(1 - c))

        def event(self, i):
            for way in range(2):
                ref = self.piece(way, i, i // 2 + 1, c)
                arrived(ref, ring_send.at[0, way, i], ring_recv.at[0, way, i], self.to[way])
                if i + 2 <= self.n - 2:
                    self.send(way, i + 2)
                k = 1 + 2 * i + way
                start(ref, ref, core_send.at[0, k], core_recv.at[0, k], to_c(1 - c))

        def crossed(self, i):
            for way in range(2):
                k = 1 + 2 * i + way
                arrived(self.piece(way, i, i // 2 + 1, 1 - c), core_send.at[0, k], core_recv.at[0, k], to_c(1 - c))

        def crossed_own(self):
            arrived(self.g.at[1 - c, self.me], core_send.at[0, 0], core_recv.at[0, 0], to_c(1 - c))

    part1 = Rows(1, g1, axis_z, axis_y, axis_x)
    part2 = Rows(2, g2, axis_z, axis_x, axis_y)
    part0 = Ring(g0, Z, z, to_z)
    both = (part1, part2)

    wide = lambda block: jnp.concatenate([block] * 4, axis=1)

    def student_planes(count, plane_of):
        def step(i, carry):
            y_, zh_ = plane_of(lax.div(i, 2)), lax.rem(i, 2)
            v = y_ * 2 + zh_
            gains = [s_gain[pl.ds(v * 2 + h, 1), :] for h in range(2)]
            blocks = ([], [])
            for pair in range(16):
                scaled = []
                for core in range(2):
                    raw = g2[core, y_, pair % 4, zh_ * 4 + pair // 4].astype(F32)
                    inv = wide(s_inv[pair, core])
                    scaled.append((raw[0:8] * inv, raw[8:16] * inv))
                for h in range(2):
                    rows = jnp.concatenate([scaled[0][h], scaled[1][h]], axis=0) * gains[h]
                    blocks[h].append(rows.astype(BF16))
            total = s_acc[...]
            for h in range(2):
                w = s_w[pl.ds(pl.multiple_of(v * 1024 + h * 512, 512), 512), :]
                total += jnp.dot(jnp.concatenate(blocks[h], axis=0), w, preferred_element_type=F32)
            s_acc[...] = total
            return carry

        lax.fori_loop(0, 2 * count, step, 0)

    def teacher_step(acc, p, load, first, count):
        lhs = []
        for v in range(8):
            inv = wide(t_inv[v * 32 + p * 16 : v * 32 + p * 16 + 16, :])
            blocks = []
            for k in range(count):
                gain = t_gain[pl.ds(first + k, 1), :]
                blocks.append((load(v, k).astype(F32) * inv * gain).astype(BF16))
            lhs.append(jnp.concatenate(blocks, axis=1))
        w = t_w[pl.ds(pl.multiple_of(first * 512, 512), count * 512), :]
        acc[...] += jnp.dot(jnp.concatenate(lhs, axis=0), w, preferred_element_type=F32)

    def teacher_x(count, plane_of):
        def step(i, carry):
            x_, zl_ = plane_of(lax.div(i, 4)), lax.rem(i, 4)
            load = lambda v, k: g1[k, x_, v // 2, (v % 2) * 4 + zl_]
            teacher_step(t_acc1, 1, load, (zl_ * X + x_) * 2, 2)
            return carry

        lax.fori_loop(0, 4 * count, step, 0, unroll=2)

    def teacher_z(count, plane_of):
        def step(i, carry):
            zl_, x_ = plane_of(lax.div(i, 2)), 2 * lax.rem(i, 2)
            load = lambda v, k: g0[k % 2, (v % 2) * 4 + zl_, (x_ + k // 2) * Y + v // 2]
            teacher_step(t_acc0, 0, load, (zl_ * X + x_) * 2, 4)
            return carry

        lax.fori_loop(0, 2 * count, step, 0)

    squares = []
    round0 = exchange(0, squares_value, add_all, squares, (over_z, over_c, over_p))
    next(round0)
    for part in both:
        part.begin()
    wait_plane = all_partners(
        axis_p,
        lambda j: g0.at[c, z, p0],
        lambda j: g0.at[c, z, j],
        lambda k: a_send.at[0, k],
        lambda j: a_recv.at[0, j],
    )
    next(round0)
    next(round0)
    wait_plane()
    part0.begin()
    for part in both:
        part.after_a()
    part0.event(0)
    for part in both:
        part.take_b(0)
    for part in both:
        part.take_c(0, 0)
        part.take_c(1, 0)
        part.send_c(0, 3)
        part.send_c(1, 1)
    part0.event(1)
    finish(round0)
    squares = squares[0]
    t_inv_row = lax.rsqrt(unpack(squares, 0) / DT + EPSILON)
    s_inv_row = lax.rsqrt(unpack(squares, 1) / DS + EPSILON)
    column = lambda row: jnp.broadcast_to(row, (128, TOKENS)).T
    t_inv[...] = column(t_inv_row)
    s_inv[...] = column(s_inv_row).reshape(s_inv.shape)
    t_load.wait()
    s_load.wait()
    for part in both:
        part.take_b(1)
    part0.event(2)
    for part in both:
        part.take_c(0, 1)
        part.take_c(1, 3)
    part0.event(3)
    part2.crossed(0)
    student_planes(1, lambda i: y)
    for part in both:
        part.take_c(0, 3)
        part.take_c(1, 1)
    part0.event(4)
    part1.crossed(0)
    teacher_x(1, lambda i: x)
    for part in both:
        part.take_c(0, 2)
        part.take_c(1, 2)
    for i in range(4):
        part0.crossed(i)
    teacher_z(1, lambda i: lax.rem(zl + 2, 4))
    part0.event(5)
    for part in both:
        for way, r in ((0, 0), (1, 3)):
            part.take_c(way, r, 1)
    part2.crossed(1)
    part2.crossed(3)
    student_planes(2, lambda i: lax.rem(y + 1 + 2 * i, Y))
    for part in both:
        part.take_c(0, 1, 1)
    part0.crossed(4)
    part0.crossed(5)
    teacher_z(2, lambda i: lax.rem(zl + 1 + 2 * i, 4))
    part0.event(6)
    part1.crossed(1)
    part1.crossed(3)
    teacher_x(2, lambda i: lax.rem(x + 1 + 2 * i, X))
    for part in both:
        part.take_c(1, 2, 1)
    part0.crossed(6)
    part0.crossed_own()
    teacher_z(1, lambda i: zl)
    part2.crossed(2)
    student_planes(1, lambda i: lax.rem(y + 2, Y))
    part1.crossed(2)
    teacher_x(1, lambda i: lax.rem(x + 2, X))

    order = []
    for v in range(8):
        order += [t_acc0[v * 16 : v * 16 + 16, :], t_acc1[v * 16 : v * 16 + 16, :]]
    tl = jnp.concatenate(order, axis=0).T
    sl = s_acc[...].T
    t_acc[...] = tl
    s_acc[...] = sl
    column_start = (dp * 8 + vo) * WIDTH
    onehot = (column_start + lax.broadcasted_iota(jnp.int32, (WIDTH, TOKENS), 0) == ids[...]).astype(F32)
    t_top = jnp.max(tl, axis=0, keepdims=True)
    s_top = jnp.max(sl, axis=0, keepdims=True)
    over_v = lambda a: jnp.sum(a, axis=0, keepdims=True)

    def merge(values):
        top = functools.reduce(jnp.maximum, [v[0:4] for v in values])
        return jnp.concatenate([top, add_all([v[4:8] * jnp.exp(v[0:4] - top) for v in values])], axis=0)

    first = []
    value = pack([t_top, s_top, over_v(jnp.exp(tl - t_top)), over_v(jnp.exp(sl - s_top))])
    finish(exchange(1, value, merge, first))
    first = first[0]
    t_lse = unpack(first, 0) + jnp.log(unpack(first, 2))
    s_lse = unpack(first, 1) + jnp.log(unpack(first, 3))
    t_logp = t_acc[...] - t_lse
    s_logp = s_acc[...] - s_lse
    a, b = math.log(MIX_WEIGHT) + t_logp, math.log(1.0 - MIX_WEIGHT) + s_logp
    mix_logp = jnp.maximum(a, b) + jnp.log1p(jnp.exp(-jnp.abs(a - b)))
    p_, q = jnp.exp(t_logp), jnp.exp(s_logp)
    gap = s_logp - mix_logp
    q_gap = q * gap
    weights = mask[...].astype(F32)
    rest = 1.0 - MIX_WEIGHT
    loss_part = weights * over_v(
        MIX_WEIGHT * p_ * (t_logp - mix_logp) + rest * q_gap - NLL_WEIGHT * (onehot * s_logp)
    )
    dot_part = over_v((rest * q_gap + NLL_WEIGHT * (q - onehot)) * s_logp)
    second = []
    finish(exchange(2, pack([loss_part, over_v(q_gap), dot_part, over_v(q * s_logp)]), add_all, second))
    second = second[0]
    kl = unpack(second, 1)
    count = jnp.sum(weights, axis=1, keepdims=True)
    row_scale = LOSS_SCALE * weights / count
    logit_grad = row_scale * (q * (rest * gap - rest * kl) + NLL_WEIGHT * (q - onehot))
    lg[...] = logit_grad.T.reshape(16, 2, 8, WIDTH)
    lhs = jnp.concatenate([lg[:, 1 - c].reshape(128, WIDTH), lg[:, c].reshape(128, WIDTH)], axis=0).astype(BF16)

    sibling = to_c(1 - c)

    def sib_copy(v):
        return remote(sib_out.at[v], sib_in.at[v], sib_send_sem.at[v], sib_recv_sem.at[v], sibling)

    def place(i):
        return lax.rem(y + 2 + 3 * i, Y), lax.div(i, 4)

    def grad_step(i, carry):
        y_, zh_ = place(i)
        v = y_ * 2 + zh_
        halves = []
        for h in range(2):
            w = s_w[pl.ds(pl.multiple_of(v * 1024 + h * 512, 512), 512), :]
            halves.append(
                lax.dot_general(lhs, w, (((1,), (1,)), ((), ())), preferred_element_type=F32).reshape(2, 16, 8, 512)
            )
        chunks = jnp.concatenate(halves, axis=2)
        sib_out[v] = chunks[0].astype(BF16)
        sib_copy(v).start()
        for k in range(16):
            raf[k % 4, zh_, y_, k // 4] = chunks[1, k, :, :256]
            rbf[y_, zh_, k % 4, k // 4] = chunks[1, k, :, 256:]
        return carry

    def sib_step(i, carry):
        y_, zh_ = place(i)
        v = y_ * 2 + zh_
        sib_copy(v).wait()
        for k in range(16):
            got = sib_in[v, k].astype(F32)
            at_a = (k % 4, zh_, y_, k // 4)
            at_b = (y_, zh_, k % 4, k // 4)
            sum_a = raf[at_a] + got[:, :256]
            sum_b = rbf[at_b] + got[:, 256:]
            raf[at_a] = sum_a
            rbf[at_b] = sum_b
            ra_out[at_a] = sum_a.astype(BF16)
            rb_out[at_b] = sum_b.astype(BF16)
        return carry

    class First:
        def __init__(self, part, axis, own, out, via, landing):
            self.part, self.own, self.out, self.via, self.landing = part, own, out, via, landing
            _, self.me, to = axis
            self.to = (to(lax.rem(self.me + 1, 4)), to(lax.rem(self.me + 3, 4)))

        def plane(self, k):
            return lax.rem(self.me + k, 4)

        def send(self, way, item):
            half = way if item != 1 else 1 - way
            k = 2 if item == 0 else (1 if way == 0 else 3)
            src = self.out.at[self.plane(k), half]
            dst = self.via.at[way] if item == 0 else self.landing.at[way, half]
            start(src, dst, first_send.at[self.part, way, item], first_recv.at[self.part, way, item], self.to[way])

        def take(self, way, item):
            half = way if item != 1 else 1 - way
            dst = self.via.at[way] if item == 0 else self.landing.at[way, half]
            arrived(dst, first_send.at[self.part, way, item], first_recv.at[self.part, way, item], self.to[way])

        def middle(self, way):
            self.take(way, 0)
            to = self.plane(1 if way == 0 else 3)

            def step(i, carry):
                row, at = lax.div(i, 4), lax.rem(i, 4)
                total = self.own[to, way, row, at] + self.via[way, row, at].astype(F32)
                self.out[to, way, row, at] = total.astype(BF16)
                return carry

            lax.fori_loop(0, 16, step, 0, unroll=4)
            self.send(way, 2)

        def last(self, total, out):
            for way in range(2):
                self.take(way, 1)
                self.take(way, 2)

            def step(i, carry):
                row, zl_ = lax.div(i, 4), lax.rem(i, 4)
                for zh_ in range(2):
                    value = self.own[self.me, zh_, row, zl_] + (
                        self.landing[0, zh_, row, zl_].astype(F32) + self.landing[1, zh_, row, zl_].astype(F32)
                    )
                    total[row, zh_ * 4 + zl_] = value
                    out[row, zh_ * 4 + zl_] = value.astype(BF16)
                return carry

            lax.fori_loop(0, 16, step, 0, unroll=2)

    first_a = First(0, axis_x, raf, ra_out, ra_via, ra_in)
    first_b = First(1, axis_y, rbf, rb_out, rb_via, rb_in)
    lax.fori_loop(0, 4, grad_step, 0)
    lax.fori_loop(0, 1, sib_step, 0)
    first_b.send(0, 0)
    lax.fori_loop(4, 8, grad_step, 0)
    lax.fori_loop(1, 4, sib_step, 0)
    first_a.send(0, 0)
    first_a.send(1, 1)
    first_b.send(1, 1)
    lax.fori_loop(4, 5, sib_step, 0)
    first_b.send(1, 0)
    lax.fori_loop(5, 6, sib_step, 0)
    first_b.send(0, 1)
    lax.fori_loop(6, 8, sib_step, 0)
    first_a.send(1, 0)
    first_a.send(0, 1)

    def gain_step(v, carry):
        y_, zh_ = lax.div(v, 2), lax.rem(v, 2)
        total = jnp.zeros((16, 512), F32)
        for i in range(16):
            z_ = zh_ * 4 + i // 4
            inv = s_inv[i, c]
            scaled = g2[c, y_, i % 4, z_].astype(F32) * wide(jnp.concatenate([inv, inv], axis=0))
            total += scaled * jnp.concatenate([raf[i % 4, zh_, y_, i // 4], rbf[y_, zh_, i % 4, i // 4]], axis=1)
        pieces = []
        for h in range(2):
            row = jnp.sum(total[8 * h : 8 * h + 8], axis=0, keepdims=True)
            pieces += [row[:, k * 128 : (k + 1) * 128] for k in range(4)]
        gp_c[c, y_, zh_] = jnp.concatenate(pieces, axis=0)
        return carry

    lax.fori_loop(0, 4, gain_step, 0)
    first_b.middle(0)
    first_a.middle(0)
    lax.fori_loop(4, 8, gain_step, 0)
    gain_wait = all_partners(
        axis_c, lambda j: gp_c.at[c], lambda j: gp_c.at[j], lambda k: gp_send.at[0, k], lambda j: gp_recv.at[0, j]
    )
    first_b.middle(1)
    first_a.middle(1)
    gain_wait()
    gp1[...] = gp_c[0] + gp_c[1]
    gp_y[y] = gp1[y]
    gain_wait = all_partners(
        axis_y, lambda j: gp1.at[j], lambda j: gp_y.at[j], lambda k: gp_send.at[1, k], lambda j: gp_recv.at[1, j]
    )

    def scatter(axis, src, landing, part, phase):
        return all_partners(
            axis,
            lambda j: src.at[j],
            lambda j: landing.at[j],
            lambda k: rs_send.at[part, phase, k],
            lambda j: rs_recv.at[part, phase, j],
        )

    def second_sum(axis, own, landing, total, out):
        n, me, _ = axis
        for at in range(Z):
            value = own[me, at]
            for k in range(1, n):
                value = value + landing[lax.rem(me + k, n), at].astype(F32)
            total[at] = value
            out[at] = value.astype(BF16)

    def third_sum(own, landing):
        value = own[z]
        for k in range(1, Z):
            value = value + landing[lax.rem(z + k, Z)].astype(F32)
        return value

    first_a.last(raf2, ra2)
    wait_a = scatter(axis_y, ra2, ra_in2, 0, 0)
    first_b.last(rbf2, rb2)
    wait_b = scatter(axis_x, rb2, rb_in2, 1, 0)
    gain_wait()
    gp_x[x] = add_all([gp_y[j] for j in range(Y)])
    gain_wait = all_partners(
        axis_x, lambda j: gp_x.at[x], lambda j: gp_x.at[j], lambda k: gp_send.at[2, k], lambda j: gp_recv.at[2, j]
    )

    row_dot = row_scale * (unpack(second, 2) - rest * kl * unpack(second, 3)) / DS
    dot_col[...] = column(row_dot).reshape(dot_col.shape)
    loss = jnp.sum(unpack(second, 0), axis=1, keepdims=True) / count
    loss_out[...] = jnp.broadcast_to(loss, loss_out.shape)

    wait_a()
    second_sum(axis_y, raf2, ra_in2, raf3, ra3)
    wait_a = scatter(axis_z, ra3, ra_in3, 0, 1)
    wait_b()
    second_sum(axis_x, rbf2, rb_in2, rbf3, rb3)
    wait_b = scatter(axis_z, rb3, rb_in3, 1, 1)
    gain_wait()
    gp3[...] = add_all([gp_x[j] for j in range(X)])
    gp_z[z] = gp3[zh]
    gain_wait = all_partners(
        axis_z,
        lambda j: gp3.at[lax.div(j, 4)],
        lambda j: gp_z.at[j],
        lambda k: gp_send.at[3, k],
        lambda j: gp_recv.at[3, j],
    )
    wait_a()
    wait_b()
    normed_grad = jnp.concatenate([third_sum(raf3, ra_in3), third_sum(rbf3, rb_in3)], axis=1)
    inv = wide(s_inv[lax.div(dp, 2), c])
    dots = wide(dot_col[lax.div(dp, 2), c])
    for h in range(2):
        grad = normed_grad[h * 8 : h * 8 + 8]
        scaled = own_rows[:, h * 512 : (h + 1) * 512] * inv
        gain = s_gain[pl.ds(vo * 2 + h, 1), :]
        grad_out[:, h * 512 : (h + 1) * 512] = inv * (grad * gain - scaled * dots)
    gain_wait()
    gain_out[...] = add_all([gp_z[j] for j in range(Z)])
    for copy in late:
        copy.wait_send()


def results(loss, grad, gain, loss_out, grad_out, gain_out):
    loss_out[0, 0] = loss[0, 0]
    grad_out[...] = grad[...].astype(BF16)
    gain_out[...] = gain[...]


def shards(t_rows, t_gain, t_head, s_rows, s_gain, s_head, ids, mask):
    vmem = pl.BlockSpec(memory_space=pltpu.VMEM)
    hbm = pl.BlockSpec(memory_space=pl.ANY)
    dma = pltpu.SemaphoreType.DMA
    scratch = [
        pltpu.VMEM((2, Z, X * Y, 16, 512), BF16),
        pltpu.VMEM((2, X, Y, Z, 16, 512), BF16),
        pltpu.VMEM((2, Y, X, Z, 16, 512), BF16),
        pltpu.VMEM((DT, WIDTH), BF16),
        pltpu.VMEM((DS, WIDTH), BF16),
        pltpu.VMEM((DT // 512, 512), F32),
        pltpu.VMEM((DS // 512, 512), F32),
        pltpu.VMEM((TOKENS, 128), F32),
        pltpu.VMEM((16, 2, 8, 128), F32),
        pltpu.VMEM((TOKENS // 2, WIDTH), F32),
        pltpu.VMEM((TOKENS // 2, WIDTH), F32),
        pltpu.VMEM((TOKENS, WIDTH), F32),
        pltpu.VMEM((TOKENS, WIDTH), F32),
        pltpu.VMEM((16, 2, 8, 128), F32),
        pltpu.VMEM((16, 2, 8, WIDTH), F32),
        pltpu.VMEM((8, 16, 16, 512), BF16),
        pltpu.VMEM((8, 16, 16, 512), BF16),
        pltpu.VMEM((X, 2, Y, 4, 16, 256), F32),
        pltpu.VMEM((Y, 2, X, 4, 16, 256), F32),
        pltpu.VMEM((X, 2, Y, 4, 16, 256), BF16),
        pltpu.VMEM((Y, 2, X, 4, 16, 256), BF16),
        pltpu.VMEM((2, 4, 4, 16, 256), BF16),
        pltpu.VMEM((2, 4, 4, 16, 256), BF16),
        pltpu.VMEM((2, 2, Y, 4, 16, 256), BF16),
        pltpu.VMEM((2, 2, X, 4, 16, 256), BF16),
        pltpu.VMEM((Y, Z, 16, 256), F32),
        pltpu.VMEM((X, Z, 16, 256), F32),
        pltpu.VMEM((Y, Z, 16, 256), BF16),
        pltpu.VMEM((X, Z, 16, 256), BF16),
        pltpu.VMEM((Y, Z, 16, 256), BF16),
        pltpu.VMEM((X, Z, 16, 256), BF16),
        pltpu.VMEM((Z, 16, 256), F32),
        pltpu.VMEM((Z, 16, 256), F32),
        pltpu.VMEM((Z, 16, 256), BF16),
        pltpu.VMEM((Z, 16, 256), BF16),
        pltpu.VMEM((Z, 16, 256), BF16),
        pltpu.VMEM((Z, 16, 256), BF16),
        pltpu.VMEM((3, 2, 8, 128), F32),
        pltpu.VMEM((3, X * Y, 8, 128), F32),
        pltpu.VMEM((3, Z, 8, 128), F32),
        pltpu.VMEM((2, Y, 2, 8, 128), F32),
        pltpu.VMEM((Y, 2, 8, 128), F32),
        pltpu.VMEM((Y, 2, 8, 128), F32),
        pltpu.VMEM((X, 2, 8, 128), F32),
        pltpu.VMEM((2, 8, 128), F32),
        pltpu.VMEM((Z, 8, 128), F32),
        dma((2,)),
        dma((3, 16)),
        dma((3, 16)),
        dma((3, 2, 2)),
        dma((3, 2, 2)),
        dma((3, 2, 8)),
        dma((3, 2, 8)),
        dma((3, 16)),
        dma((3, 16)),
        dma((3, 26)),
        dma((3, 26)),
        dma((8,)),
        dma((8,)),
        dma((2, 2, 3)),
        dma((2, 2, 3)),
        dma((2, 2, 8)),
        dma((2, 2, 8)),
        dma((4, 8)),
        dma((4, 8)),
    ]
    flops = 2 * TOKENS * WIDTH * (DT + 2 * DS)
    shapes = (
        jax.ShapeDtypeStruct((8, 128), F32),
        jax.ShapeDtypeStruct(s_rows.shape, F32),
        jax.ShapeDtypeStruct((8, 128), F32),
    )
    values = pl.pallas_call(
        kernel,
        out_shape=shapes,
        in_specs=[vmem, vmem, hbm, vmem, vmem, hbm, vmem, vmem],
        out_specs=(vmem, vmem, vmem),
        scratch_shapes=scratch,
        compiler_params=pltpu.CompilerParams(
            collective_id=0, has_side_effects=True, vmem_limit_bytes=60 * 1024 * 1024
        ),
        cost_estimate=pl.CostEstimate(flops=flops, bytes_accessed=2 * WIDTH * (DT + DS), transcendentals=0),
    )(t_rows, t_gain, t_head, s_rows, s_gain, s_head, ids.reshape(1, TOKENS), mask.reshape(1, TOKENS))
    loss, grad, gain = pl.pallas_call(
        results,
        out_shape=(jax.ShapeDtypeStruct((1, 1), F32), jax.ShapeDtypeStruct(s_rows.shape, BF16), shapes[2]),
        in_specs=[vmem] * 3,
        out_specs=(pl.BlockSpec(memory_space=pltpu.SMEM), vmem, vmem),
    )(*values)
    return loss.reshape(()), grad, gain.reshape(1024)


def solution(mesh):
    return jax.shard_map(
        shards,
        mesh=mesh,
        in_specs=(
            P("vocab", "dp"),
            P(),
            P(None, ("dp", "vocab")),
            P("dp", "vocab"),
            P(),
            P(None, ("dp", "vocab")),
            P(),
            P(),
        ),
        out_specs=(P(), P("dp", "vocab"), P("vocab")),
        check_vma=False,
    )
```

```python
import functools
import math

import jax
import jax.numpy as jnp
from jax import lax
from jax.experimental import pallas as pl
from jax.experimental.pallas import tpu as pltpu
from jax.sharding import PartitionSpec as P

EPSILON = 1e-05
MIX_WEIGHT = 0.3
NLL_WEIGHT = 0.03
LOSS_SCALE = 8192.0
MESH = pl.DeviceIdType.MESH
F32 = jnp.float32
BF16 = jnp.bfloat16
X, Y, Z = 4, 4, 8
TOKENS, DT, DS, WIDTH = 256, 16384, 8192, 256


def kernel(
    t_rows_in, t_gain_in, t_head, s_rows_in, s_gain_in, s_head, ids_in, mask_in,
    loss_out, grad_out, gain_out,
    g0, g1, g2, t_w, s_w, t_gain, s_gain, t_inv, s_inv, t_acc0, t_acc1, t_acc, s_acc, dot_col, lg,
    sib_out, sib_in, raf, rbf, ra_out, rb_out, ra_via, rb_via, ra_in, rb_in,
    raf2, rbf2, ra2, rb2, ra_in2, rb_in2, raf3, rbf3, ra3, rb3, ra_in3, rb_in3,
    st_c, st_p, st_z, gp_c, gp1, gp_y, gp_x, gp3, gp_z,
    t_rows, t_gain_raw, s_rows, s_gain_raw, ids, mask,
    head_sem, input_sem, a_send, a_recv, b_send, b_recv, ring_send, ring_recv, core_send, core_recv,
    st_send, st_recv, sib_send_sem, sib_recv_sem, first_send, first_recv, rs_send, rs_recv, z_send, z_recv, gp_send, gp_recv,
):
    dp = lax.axis_index("dp")
    vo = lax.axis_index("vocab")
    c = lax.rem(dp, 2)
    x = lax.rem(lax.div(dp, 2), X)
    zl = lax.div(dp, 2 * X)
    y = lax.div(vo, 2)
    zh = lax.rem(vo, 2)
    z = zh * 4 + zl

    def device(x_, y_, z_, c_):
        return ((lax.rem(z_, 4) * X + x_) * 2 + c_, y_ * 2 + lax.div(z_, 4))

    to_c = lambda j: (dp - c + j, vo)
    to_x = lambda j: (dp + (j - x) * 2, vo)
    to_y = lambda j: (dp, vo + (j - y) * 2)
    to_z = lambda j: device(x, y, j, c)
    to_p = lambda j: device(lax.div(j, Y), lax.rem(j, Y), z, c)
    axis_c, axis_x, axis_y, axis_z = (2, c, to_c), (X, x, to_x), (Y, y, to_y), (Z, z, to_z)
    axis_p = (X * Y, x * Y + y, to_p)

    barrier = pltpu.get_barrier_semaphore()
    partners = 0
    for n, me, to in (axis_z, axis_p, axis_c):
        for k in range(1, n):
            pl.semaphore_signal(barrier, inc=1, device_id=to(lax.rem(me + k, n)), device_id_type=MESH)
            partners += 1

    t_load = pltpu.make_async_copy(t_head, t_w, head_sem.at[0])
    s_load = pltpu.make_async_copy(s_head, s_w, head_sem.at[1])
    loads = [
        pltpu.make_async_copy(src, dst, input_sem.at[k])
        for k, (src, dst) in enumerate(
            (
                (t_rows_in, t_rows), (s_rows_in, s_rows), (t_gain_in, t_gain_raw),
                (s_gain_in, s_gain_raw), (ids_in, ids), (mask_in, mask),
            )
        )
    ]
    for load in loads:
        load.start()
    t_load.start()
    s_load.start()
    for load in loads:
        load.wait()

    def remote(src, dst, send, recv, to):
        return pltpu.make_async_remote_copy(
            src_ref=src, dst_ref=dst, send_sem=send, recv_sem=recv, device_id=to, device_id_type=MESH
        )

    late = []

    def start(src, dst, send, recv, to):
        copy = remote(src, dst, send, recv, to)
        copy.start()
        late.append(copy)

    def arrived(dst, send, recv, to):
        remote(dst, dst, send, recv, to).wait_recv()

    p0 = x * Y + y
    g0[c, z, p0] = t_rows[0:16, :]
    g1[c, x, y, z] = t_rows[16:32, :]
    own_rows = s_rows[...].astype(F32)
    g2[c, y, x, z] = jnp.concatenate([own_rows[:, :512], own_rows[:, 512:]], axis=0).astype(BF16)

    def lane_sums(block):
        total = block[:, 0:128]
        for k in range(1, block.shape[1] // 128):
            total = total + block[:, k * 128 : (k + 1) * 128]
        total = jnp.concatenate([total] * (TOKENS // total.shape[0]), axis=0)
        return jnp.sum(total.T, axis=0, keepdims=True)

    lanes = lax.broadcasted_iota(jnp.int32, (1, TOKENS), 1)
    t_own = t_rows[...].astype(F32)
    t_squares = jnp.where(lax.div(lanes, 32) == vo, lane_sums(t_own * t_own), 0.0)
    s_squares = jnp.where(lax.div(lanes, 8) == dp, lane_sums(own_rows * own_rows), 0.0)

    def pack(rows):
        halves = [row[:, 128 * h : 128 * h + 128] for row in rows for h in range(2)]
        return jnp.concatenate(halves + [jnp.zeros((1, 128), F32)] * (8 - len(halves)), axis=0)

    def unpack(block, k):
        return jnp.concatenate([block[2 * k : 2 * k + 1], block[2 * k + 1 : 2 * k + 2]], axis=1)

    squares_value = pack([t_squares, s_squares])

    t_gain[...] = t_gain_raw[...].astype(F32).reshape(t_gain.shape)
    s_gain[...] = s_gain_raw[...].astype(F32).reshape(s_gain.shape)
    for acc in (t_acc0, t_acc1, s_acc):
        acc[...] = jnp.zeros_like(acc)

    pl.semaphore_wait(barrier, partners)

    def all_partners(axis, src, dst, send, recv):
        n, me, to = axis
        arrivals = []
        for k in range(1, n):
            j = lax.rem(me + k, n)
            start(src(j), dst(me), send(k), recv(me), to(j))
            arrivals.append(remote(dst(j), dst(j), send(k), recv(j), to(j)))

        def wait():
            for arrival in arrivals:
                arrival.wait_recv()

        return wait

    over_c, over_p, over_z = (axis_c, st_c, 0), (axis_p, st_p, 2), (axis_z, st_z, 18)

    def exchange(r, value, combine, result, steps=(over_c, over_p, over_z)):
        for axis, buf, base in steps:
            n, me, _ = axis
            buf[r, me] = value
            wait = all_partners(
                axis,
                lambda j: buf.at[r, me],
                lambda j: buf.at[r, j],
                lambda k: st_send.at[r, base + k],
                lambda j: st_recv.at[r, base + j],
            )
            yield
            wait()
            value = combine([buf[r, j] for j in range(n)])
        result.append(value)

    def finish(steps):
        for _ in steps:
            pass

    def add_all(values):
        return functools.reduce(lambda a, b: a + b, values)

    class Rows:
        def __init__(self, p, g, a, b, cc):
            self.p, self.g, self.a, self.b, self.c = p, g, a, b, cc
            step = lambda axis: tuple(axis[2](lax.rem(axis[1] + k, 4)) for k in (1, 3))
            self.to_b, self.to_c = step(b), step(cc)
            self.ready = set()

        def begin(self):
            mine, theirs = self.c[1], self.b[1]
            n, me, to = self.a
            slot = self.g.at[c, mine, theirs, me]
            for k in self.ORDER[1:]:
                j = lax.rem(me + k, n)
                start(slot, slot, a_send.at[self.p, k], a_recv.at[self.p, me], to(j))

        def row(self, core, plane, r):
            return self.g.at[core, lax.rem(self.c[1] + plane, 4), lax.rem(self.b[1] + r, 4)]

        def cross(self, plane, r):
            k = plane * 4 + r
            ref = self.row(c, plane, r)
            start(ref, ref, core_send.at[self.p, k], core_recv.at[self.p, k], to_c(1 - c))

        def crossed(self, plane):
            for r in range(4):
                k = plane * 4 + r
                arrived(self.row(1 - c, plane, r), core_send.at[self.p, k], core_recv.at[self.p, k], to_c(1 - c))

        def half(self, r, way):
            return self.row(c, 0, r).at[4 * way : 4 * way + 4]

        def send_b(self, way, item):
            ref = self.row(c, 0, 0) if item == 0 else self.half(3 if way == 0 else 1, way)
            start(ref, ref, b_send.at[self.p, way, item], b_recv.at[self.p, way, item], self.to_b[way])

        def take_b(self, item):
            for way in range(2):
                ref = self.row(c, 0, 3 if way == 0 else 1) if item == 0 else self.half(2, way)
                arrived(ref, b_send.at[self.p, way, item], b_recv.at[self.p, way, item], self.to_b[way])
                if item == 0:
                    self.send_b(way, 1)
            if item == 0:
                self.send_c(0, 1)
                self.send_c(1, 3)
                self.cross(0, 1)
                self.cross(0, 3)
            else:
                self.send_c(0, 2)
                self.send_c(1, 2)
                self.cross(0, 2)

        def send_c(self, way, r, hop=0):
            ref = self.row(c, 0 if hop == 0 else (3 if way == 0 else 1), r)
            k = r + 4 * hop
            start(ref, ref, ring_send.at[self.p, way, k], ring_recv.at[self.p, way, k], self.to_c[way])

        def take_c(self, way, r, hop=0):
            plane = 2 if hop else (3 if way == 0 else 1)
            k = r + 4 * hop
            arrived(self.row(c, plane, r), ring_send.at[self.p, way, k], ring_recv.at[self.p, way, k], self.to_c[way])
            if hop == 0 and r in ((0, 1), (3, 2))[way]:
                self.send_c(way, r, 1)
            self.cross(plane, r)

        ORDER = (0, 1, 7, 2, 6, 3, 5, 4)

        def after_a(self, steps):
            n, me, to = self.a
            for k in steps:
                j = lax.rem(me + k, n)
                slot = self.g.at[c, self.c[1], self.b[1], j]
                if k:
                    arrived(slot, a_send.at[self.p, k], a_recv.at[self.p, j], to(j))
                for way in range(2):
                    for send, recv, target in (
                        (b_send, b_recv, self.to_b[way]),
                        (ring_send, ring_recv, self.to_c[way]),
                    ):
                        remote(slot, slot, send.at[self.p, way, 0], recv.at[self.p, way, 0], target).start()

        def row_sent(self):
            row = self.row(c, 0, 0)
            for way in range(2):
                for send, recv, target in (
                    (b_send, b_recv, self.to_b[way]),
                    (ring_send, ring_recv, self.to_c[way]),
                ):
                    late.append(remote(row, row, send.at[self.p, way, 0], recv.at[self.p, way, 0], target))
            self.cross(0, 0)

    class Ring:
        def __init__(self, g, n, me, to):
            self.g, self.n, self.me = g, n, me
            self.to = (to(lax.rem(me + 1, n)), to(lax.rem(me + n - 1, n)))

        def piece(self, way, i, distance, core):
            half = i % 2 if way == 0 else 1 - i % 2
            plane = lax.rem(self.me + (self.n - distance if way == 0 else distance), self.n)
            return self.g.at[core, plane, 8 * half : 8 * half + 8]

        def send(self, way, i):
            ref = self.piece(way, i, i // 2, c)
            start(ref, ref, ring_send.at[0, way, i], ring_recv.at[0, way, i], self.to[way])

        def begin(self):
            for i in range(2):
                for way in range(2):
                    self.send(way, i)
            ref = self.g.at[c, self.me]
            start(ref, ref, core_send.at[0, 0], core_recv.at[0, 0], to_c(1 - c))

        def event(self, i):
            for way in range(2):
                ref = self.piece(way, i, i // 2 + 1, c)
                arrived(ref, ring_send.at[0, way, i], ring_recv.at[0, way, i], self.to[way])
                if i + 2 <= self.n - 2:
                    self.send(way, i + 2)
                k = 1 + 2 * i + way
                start(ref, ref, core_send.at[0, k], core_recv.at[0, k], to_c(1 - c))

        def crossed(self, i):
            for way in range(2):
                k = 1 + 2 * i + way
                arrived(self.piece(way, i, i // 2 + 1, 1 - c), core_send.at[0, k], core_recv.at[0, k], to_c(1 - c))

        def crossed_own(self):
            arrived(self.g.at[1 - c, self.me], core_send.at[0, 0], core_recv.at[0, 0], to_c(1 - c))

    part1 = Rows(1, g1, axis_z, axis_y, axis_x)
    part2 = Rows(2, g2, axis_z, axis_x, axis_y)
    part0 = Ring(g0, Z, z, to_z)
    both = (part1, part2)

    wide = lambda block: jnp.concatenate([block] * 4, axis=1)

    def student_planes(count, plane_of):
        def step(i, carry):
            y_, zh_ = plane_of(lax.div(i, 2)), lax.rem(i, 2)
            v = y_ * 2 + zh_
            gains = [s_gain[pl.ds(v * 2 + h, 1), :] for h in range(2)]
            blocks = ([], [])
            for pair in range(16):
                scaled = []
                for core in range(2):
                    raw = g2[core, y_, pair % 4, zh_ * 4 + pair // 4].astype(F32)
                    inv = wide(s_inv[pair, core])
                    scaled.append((raw[0:8] * inv, raw[8:16] * inv))
                for h in range(2):
                    rows = jnp.concatenate([scaled[0][h], scaled[1][h]], axis=0) * gains[h]
                    blocks[h].append(rows.astype(BF16))
            total = s_acc[...]
            for h in range(2):
                w = s_w[pl.ds(pl.multiple_of(v * 1024 + h * 512, 512), 512), :]
                total += jnp.dot(jnp.concatenate(blocks[h], axis=0), w, preferred_element_type=F32)
            s_acc[...] = total
            return carry

        lax.fori_loop(0, 2 * count, step, 0)

    def teacher_step(acc, p, load, first, count):
        lhs = []
        for v in range(8):
            inv = wide(t_inv[v * 32 + p * 16 : v * 32 + p * 16 + 16, :])
            blocks = []
            for k in range(count):
                gain = t_gain[pl.ds(first + k, 1), :]
                blocks.append((load(v, k).astype(F32) * inv * gain).astype(BF16))
            lhs.append(jnp.concatenate(blocks, axis=1))
        w = t_w[pl.ds(pl.multiple_of(first * 512, 512), count * 512), :]
        acc[...] += jnp.dot(jnp.concatenate(lhs, axis=0), w, preferred_element_type=F32)

    def teacher_x(count, plane_of):
        def step(i, carry):
            x_, zl_ = plane_of(lax.div(i, 4)), lax.rem(i, 4)
            load = lambda v, k: g1[k, x_, v // 2, (v % 2) * 4 + zl_]
            teacher_step(t_acc1, 1, load, (zl_ * X + x_) * 2, 2)
            return carry

        lax.fori_loop(0, 4 * count, step, 0, unroll=2)

    def teacher_z(count, plane_of):
        def step(i, carry):
            zl_, x_ = plane_of(lax.div(i, 2)), 2 * lax.rem(i, 2)
            load = lambda v, k: g0[k % 2, (v % 2) * 4 + zl_, (x_ + k // 2) * Y + v // 2]
            teacher_step(t_acc0, 0, load, (zl_ * X + x_) * 2, 4)
            return carry

        lax.fori_loop(0, 2 * count, step, 0)

    squares = []
    round0 = exchange(0, squares_value, add_all, squares, (over_z, over_c, over_p))
    next(round0)
    for part in both:
        part.begin()
    wait_plane = all_partners(
        axis_p,
        lambda j: g0.at[c, z, p0],
        lambda j: g0.at[c, z, j],
        lambda k: a_send.at[0, k],
        lambda j: a_recv.at[0, j],
    )
    for part in both:
        part.after_a(Rows.ORDER[:1])
    part1.after_a(Rows.ORDER[1:])
    wait_plane()
    part0.begin()
    next(round0)
    part2.after_a(Rows.ORDER[1:])
    next(round0)
    for part in both:
        part.row_sent()
    part0.event(0)
    for part in both:
        part.take_b(0)
    for part in both:
        part.take_c(0, 0)
        part.take_c(1, 0)
        part.send_c(0, 3)
        part.send_c(1, 1)
    part0.event(1)
    finish(round0)
    squares = squares[0]
    t_inv_row = lax.rsqrt(unpack(squares, 0) / DT + EPSILON)
    s_inv_row = lax.rsqrt(unpack(squares, 1) / DS + EPSILON)
    column = lambda row: jnp.broadcast_to(row, (128, TOKENS)).T
    t_inv[...] = column(t_inv_row)
    s_inv[...] = column(s_inv_row).reshape(s_inv.shape)
    t_load.wait()
    s_load.wait()
    for part in both:
        part.take_b(1)
    part0.event(2)
    for part in both:
        part.take_c(0, 1)
        part.take_c(1, 3)
    part0.event(3)
    part2.crossed(0)
    student_planes(1, lambda i: y)
    for part in both:
        part.take_c(0, 3)
        part.take_c(1, 1)
    part0.event(4)
    part1.crossed(0)
    teacher_x(1, lambda i: x)
    for part in both:
        part.take_c(0, 2)
        part.take_c(1, 2)
    for i in range(4):
        part0.crossed(i)
    teacher_z(1, lambda i: lax.rem(zl + 2, 4))
    part0.event(5)
    for part in both:
        for way, r in ((0, 0), (1, 3)):
            part.take_c(way, r, 1)
    part2.crossed(1)
    part2.crossed(3)
    student_planes(2, lambda i: lax.rem(y + 1 + 2 * i, Y))
    for part in both:
        part.take_c(0, 1, 1)
    part0.crossed(4)
    part0.crossed(5)
    teacher_z(2, lambda i: lax.rem(zl + 1 + 2 * i, 4))
    part0.event(6)
    part1.crossed(1)
    part1.crossed(3)
    teacher_x(2, lambda i: lax.rem(x + 1 + 2 * i, X))
    for part in both:
        part.take_c(1, 2, 1)
    part0.crossed(6)
    part0.crossed_own()
    teacher_z(1, lambda i: zl)
    part2.crossed(2)
    student_planes(1, lambda i: lax.rem(y + 2, Y))
    part1.crossed(2)
    teacher_x(1, lambda i: lax.rem(x + 2, X))

    order = []
    for v in range(8):
        order += [t_acc0[v * 16 : v * 16 + 16, :], t_acc1[v * 16 : v * 16 + 16, :]]
    tl = jnp.concatenate(order, axis=0).T
    sl = s_acc[...].T
    t_acc[...] = tl
    s_acc[...] = sl
    column_start = (dp * 8 + vo) * WIDTH
    onehot = (column_start + lax.broadcasted_iota(jnp.int32, (WIDTH, TOKENS), 0) == ids[...]).astype(F32)
    t_top = jnp.max(tl, axis=0, keepdims=True)
    s_top = jnp.max(sl, axis=0, keepdims=True)
    over_v = lambda a: jnp.sum(a, axis=0, keepdims=True)

    def merge(values):
        top = functools.reduce(jnp.maximum, [v[0:4] for v in values])
        return jnp.concatenate([top, add_all([v[4:8] * jnp.exp(v[0:4] - top) for v in values])], axis=0)

    first = []
    value = pack([t_top, s_top, over_v(jnp.exp(tl - t_top)), over_v(jnp.exp(sl - s_top))])
    finish(exchange(1, value, merge, first))
    first = first[0]
    t_lse = unpack(first, 0) + jnp.log(unpack(first, 2))
    s_lse = unpack(first, 1) + jnp.log(unpack(first, 3))
    t_logp = t_acc[...] - t_lse
    s_logp = s_acc[...] - s_lse
    a, b = math.log(MIX_WEIGHT) + t_logp, math.log(1.0 - MIX_WEIGHT) + s_logp
    mix_logp = jnp.maximum(a, b) + jnp.log1p(jnp.exp(-jnp.abs(a - b)))
    p_, q = jnp.exp(t_logp), jnp.exp(s_logp)
    gap = s_logp - mix_logp
    q_gap = q * gap
    weights = mask[...].astype(F32)
    rest = 1.0 - MIX_WEIGHT
    loss_part = weights * over_v(
        MIX_WEIGHT * p_ * (t_logp - mix_logp) + rest * q_gap - NLL_WEIGHT * (onehot * s_logp)
    )
    dot_part = over_v((rest * q_gap + NLL_WEIGHT * (q - onehot)) * s_logp)
    second = []
    finish(exchange(2, pack([loss_part, over_v(q_gap), dot_part, over_v(q * s_logp)]), add_all, second))
    second = second[0]
    kl = unpack(second, 1)
    count = jnp.sum(weights, axis=1, keepdims=True)
    row_scale = LOSS_SCALE * weights / count
    logit_grad = row_scale * (q * (rest * gap - rest * kl) + NLL_WEIGHT * (q - onehot))
    lg[...] = logit_grad.T.reshape(16, 2, 8, WIDTH)
    lhs = jnp.concatenate([lg[:, 1 - c].reshape(128, WIDTH), lg[:, c].reshape(128, WIDTH)], axis=0).astype(BF16)

    sibling = to_c(1 - c)

    def sib_copy(v):
        return remote(sib_out.at[v], sib_in.at[v], sib_send_sem.at[v], sib_recv_sem.at[v], sibling)

    def place(i):
        return lax.rem(y + 2 + 3 * i, Y), lax.div(i, 4)

    def grad_step(i, carry):
        y_, zh_ = place(i)
        v = y_ * 2 + zh_
        halves = []
        for h in range(2):
            w = s_w[pl.ds(pl.multiple_of(v * 1024 + h * 512, 512), 512), :]
            halves.append(
                lax.dot_general(lhs, w, (((1,), (1,)), ((), ())), preferred_element_type=F32).reshape(2, 16, 8, 512)
            )
        chunks = jnp.concatenate(halves, axis=2)
        sib_out[v] = chunks[0].astype(BF16)
        sib_copy(v).start()
        for k in range(16):
            raf[k % 4, zh_, y_, k // 4] = chunks[1, k, :, :256]
            rbf[y_, zh_, k % 4, k // 4] = chunks[1, k, :, 256:]
        return carry

    def sib_step(i, carry):
        y_, zh_ = place(i)
        v = y_ * 2 + zh_
        sib_copy(v).wait()
        for k in range(16):
            got = sib_in[v, k].astype(F32)
            at_a = (k % 4, zh_, y_, k // 4)
            at_b = (y_, zh_, k % 4, k // 4)
            sum_a = raf[at_a] + got[:, :256]
            sum_b = rbf[at_b] + got[:, 256:]
            raf[at_a] = sum_a
            rbf[at_b] = sum_b
            ra_out[at_a] = sum_a.astype(BF16)
            rb_out[at_b] = sum_b.astype(BF16)
        return carry

    class First:
        def __init__(self, part, axis, own, out, via, landing):
            self.part, self.own, self.out, self.via, self.landing = part, own, out, via, landing
            _, self.me, to = axis
            self.to = (to(lax.rem(self.me + 1, 4)), to(lax.rem(self.me + 3, 4)))

        def plane(self, k):
            return lax.rem(self.me + k, 4)

        def send(self, way, item):
            half = way if item != 1 else 1 - way
            k = 2 if item == 0 else (1 if way == 0 else 3)
            src = self.out.at[self.plane(k), half]
            dst = self.via.at[way] if item == 0 else self.landing.at[way, half]
            start(src, dst, first_send.at[self.part, way, item], first_recv.at[self.part, way, item], self.to[way])

        def take(self, way, item):
            half = way if item != 1 else 1 - way
            dst = self.via.at[way] if item == 0 else self.landing.at[way, half]
            arrived(dst, first_send.at[self.part, way, item], first_recv.at[self.part, way, item], self.to[way])

        def middle(self, way):
            self.take(way, 0)
            to = self.plane(1 if way == 0 else 3)

            def step(i, carry):
                row, at = lax.div(i, 4), lax.rem(i, 4)
                total = self.own[to, way, row, at] + self.via[way, row, at].astype(F32)
                self.out[to, way, row, at] = total.astype(BF16)
                return carry

            lax.fori_loop(0, 16, step, 0, unroll=4)
            self.send(way, 2)

        def last(self, half, total, out):
            self.take(1 - half, 1)
            self.take(half, 2)

            def step(row, carry):
                for zl_ in range(4):
                    value = self.own[self.me, half, row, zl_] + (
                        self.landing[0, half, row, zl_].astype(F32) + self.landing[1, half, row, zl_].astype(F32)
                    )
                    total[row, half, zl_] = value
                    out[row, half, zl_] = value.astype(BF16)
                return carry

            lax.fori_loop(0, 4, step, 0)

    first_a = First(0, axis_x, raf, ra_out, ra_via, ra_in)
    first_b = First(1, axis_y, rbf, rb_out, rb_via, rb_in)
    lax.fori_loop(0, 4, grad_step, 0)
    lax.fori_loop(0, 1, sib_step, 0)
    first_b.send(0, 0)
    lax.fori_loop(4, 8, grad_step, 0)
    lax.fori_loop(1, 4, sib_step, 0)
    first_a.send(0, 0)
    first_a.send(1, 1)
    first_b.send(1, 1)
    lax.fori_loop(4, 5, sib_step, 0)
    first_b.send(1, 0)
    lax.fori_loop(5, 6, sib_step, 0)
    first_b.send(0, 1)
    lax.fori_loop(6, 8, sib_step, 0)
    first_a.send(1, 0)
    first_a.send(0, 1)

    def gain_step(v, carry):
        y_, zh_ = lax.div(v, 2), lax.rem(v, 2)
        total = jnp.zeros((16, 512), F32)
        for i in range(16):
            z_ = zh_ * 4 + i // 4
            inv = s_inv[i, c]
            scaled = g2[c, y_, i % 4, z_].astype(F32) * wide(jnp.concatenate([inv, inv], axis=0))
            total += scaled * jnp.concatenate([raf[i % 4, zh_, y_, i // 4], rbf[y_, zh_, i % 4, i // 4]], axis=1)
        pieces = []
        for h in range(2):
            row = jnp.sum(total[8 * h : 8 * h + 8], axis=0, keepdims=True)
            pieces += [row[:, k * 128 : (k + 1) * 128] for k in range(4)]
        gp_c[c, y_, zh_] = jnp.concatenate(pieces, axis=0)
        return carry

    def scatter(axis, src, landing, part, half):
        return all_partners(
            axis,
            lambda j: src.at[j, half],
            lambda j: landing.at[j, half],
            lambda k: rs_send.at[part, half, k],
            lambda j: rs_recv.at[part, half, j],
        )

    def second_sum(axis, half, own, landing, total, out):
        n, me, _ = axis
        for at in range(4):
            value = own[me, half, at]
            for k in range(1, n):
                value = value + landing[lax.rem(me + k, n), half, at].astype(F32)
            total[half * 4 + at] = value
            out[half * 4 + at] = value.astype(BF16)

    own_sends = []

    def send_z(half, src, landing, part):
        for k in range(4):
            j = half * 4 + lax.rem(zl + k, 4)
            copy = remote(
                src.at[j], landing.at[z], z_send.at[part, half, k], z_recv.at[part, z], to_z(j)
            )
            if k:
                copy.start()
                late.append(copy)
            else:
                pl.when(zh != half)(copy.start)
                own_sends.append((half, copy))

    def third_sum(own, landing, part):
        for k in range(1, Z):
            j = lax.rem(z + k, Z)
            arrived(landing.at[j], z_send.at[part, 0, 1], z_recv.at[part, j], to_z(j))
        value = own[z]
        for k in range(1, Z):
            value = value + landing[lax.rem(z + k, Z)].astype(F32)
        return value

    lax.fori_loop(0, 4, gain_step, 0)
    first_b.middle(0)
    first_a.middle(0)
    lax.fori_loop(4, 8, gain_step, 0)
    gain_wait = all_partners(
        axis_c, lambda j: gp_c.at[c], lambda j: gp_c.at[j], lambda k: gp_send.at[0, k], lambda j: gp_recv.at[0, j]
    )
    first_b.middle(1)
    first_a.middle(1)
    first_b.last(0, rbf2, rb2)
    wait_b0 = scatter(axis_x, rb2, rb_in2, 1, 0)
    first_a.last(0, raf2, ra2)
    wait_a0 = scatter(axis_y, ra2, ra_in2, 0, 0)
    gain_wait()
    gp1[...] = gp_c[0] + gp_c[1]
    gp_y[y] = gp1[y]
    gain_wait = all_partners(
        axis_y, lambda j: gp1.at[j], lambda j: gp_y.at[j], lambda k: gp_send.at[1, k], lambda j: gp_recv.at[1, j]
    )
    first_b.last(1, rbf2, rb2)
    wait_b1 = scatter(axis_x, rb2, rb_in2, 1, 1)
    first_a.last(1, raf2, ra2)
    wait_a1 = scatter(axis_y, ra2, ra_in2, 0, 1)
    wait_b0()
    second_sum(axis_x, 0, rbf2, rb_in2, rbf3, rb3)
    send_z(0, rb3, rb_in3, 1)
    wait_a0()
    second_sum(axis_y, 0, raf2, ra_in2, raf3, ra3)
    send_z(0, ra3, ra_in3, 0)
    gain_wait()
    gp_x[x] = add_all([gp_y[j] for j in range(Y)])
    gain_wait = all_partners(
        axis_x, lambda j: gp_x.at[x], lambda j: gp_x.at[j], lambda k: gp_send.at[2, k], lambda j: gp_recv.at[2, j]
    )

    row_dot = row_scale * (unpack(second, 2) - rest * kl * unpack(second, 3)) / DS
    dot_col[...] = column(row_dot).reshape(dot_col.shape)
    loss = jnp.sum(unpack(second, 0), axis=1, keepdims=True) / count
    loss_out[...] = jnp.broadcast_to(loss, loss_out.shape)

    wait_b1()
    second_sum(axis_x, 1, rbf2, rb_in2, rbf3, rb3)
    send_z(1, rb3, rb_in3, 1)
    wait_a1()
    second_sum(axis_y, 1, raf2, ra_in2, raf3, ra3)
    send_z(1, ra3, ra_in3, 0)
    gain_wait()
    gp3[...] = add_all([gp_x[j] for j in range(X)])
    gp_z[z] = gp3[zh]
    gain_wait = all_partners(
        axis_z,
        lambda j: gp3.at[lax.div(j, 4)],
        lambda j: gp_z.at[j],
        lambda k: gp_send.at[3, k],
        lambda j: gp_recv.at[3, j],
    )
    normed_grad = jnp.concatenate([third_sum(raf3, ra_in3, 0), third_sum(rbf3, rb_in3, 1)], axis=1)
    inv = wide(s_inv[lax.div(dp, 2), c])
    dots = wide(dot_col[lax.div(dp, 2), c])
    for h in range(2):
        grad = normed_grad[h * 8 : h * 8 + 8]
        scaled = own_rows[:, h * 512 : (h + 1) * 512] * inv
        gain = s_gain[pl.ds(vo * 2 + h, 1), :]
        grad_out[:, h * 512 : (h + 1) * 512] = inv * (grad * gain - scaled * dots)
    gain_wait()
    gain_out[...] = add_all([gp_z[j] for j in range(Z)])
    for copy in late:
        copy.wait_send()
    for half, copy in own_sends:
        pl.when(zh != half)(copy.wait_send)


def results(loss, grad, gain, loss_out, grad_out, gain_out):
    loss_out[0, 0] = loss[0, 0]
    grad_out[...] = grad[...].astype(BF16)
    gain_out[...] = gain[...]


def shards(t_rows, t_gain, t_head, s_rows, s_gain, s_head, ids, mask):
    vmem = pl.BlockSpec(memory_space=pltpu.VMEM)
    hbm = pl.BlockSpec(memory_space=pl.ANY)
    dma = pltpu.SemaphoreType.DMA
    scratch = [
        pltpu.VMEM((2, Z, X * Y, 16, 512), BF16),
        pltpu.VMEM((2, X, Y, Z, 16, 512), BF16),
        pltpu.VMEM((2, Y, X, Z, 16, 512), BF16),
        pltpu.VMEM((DT, WIDTH), BF16),
        pltpu.VMEM((DS, WIDTH), BF16),
        pltpu.VMEM((DT // 512, 512), F32),
        pltpu.VMEM((DS // 512, 512), F32),
        pltpu.VMEM((TOKENS, 128), F32),
        pltpu.VMEM((16, 2, 8, 128), F32),
        pltpu.VMEM((TOKENS // 2, WIDTH), F32),
        pltpu.VMEM((TOKENS // 2, WIDTH), F32),
        pltpu.VMEM((TOKENS, WIDTH), F32),
        pltpu.VMEM((TOKENS, WIDTH), F32),
        pltpu.VMEM((16, 2, 8, 128), F32),
        pltpu.VMEM((16, 2, 8, WIDTH), F32),
        pltpu.VMEM((8, 16, 16, 512), BF16),
        pltpu.VMEM((8, 16, 16, 512), BF16),
        pltpu.VMEM((X, 2, Y, 4, 16, 256), F32),
        pltpu.VMEM((Y, 2, X, 4, 16, 256), F32),
        pltpu.VMEM((X, 2, Y, 4, 16, 256), BF16),
        pltpu.VMEM((Y, 2, X, 4, 16, 256), BF16),
        pltpu.VMEM((2, 4, 4, 16, 256), BF16),
        pltpu.VMEM((2, 4, 4, 16, 256), BF16),
        pltpu.VMEM((2, 2, Y, 4, 16, 256), BF16),
        pltpu.VMEM((2, 2, X, 4, 16, 256), BF16),
        pltpu.VMEM((Y, 2, 4, 16, 256), F32),
        pltpu.VMEM((X, 2, 4, 16, 256), F32),
        pltpu.VMEM((Y, 2, 4, 16, 256), BF16),
        pltpu.VMEM((X, 2, 4, 16, 256), BF16),
        pltpu.VMEM((Y, 2, 4, 16, 256), BF16),
        pltpu.VMEM((X, 2, 4, 16, 256), BF16),
        pltpu.VMEM((Z, 16, 256), F32),
        pltpu.VMEM((Z, 16, 256), F32),
        pltpu.VMEM((Z, 16, 256), BF16),
        pltpu.VMEM((Z, 16, 256), BF16),
        pltpu.VMEM((Z, 16, 256), BF16),
        pltpu.VMEM((Z, 16, 256), BF16),
        pltpu.VMEM((3, 2, 8, 128), F32),
        pltpu.VMEM((3, X * Y, 8, 128), F32),
        pltpu.VMEM((3, Z, 8, 128), F32),
        pltpu.VMEM((2, Y, 2, 8, 128), F32),
        pltpu.VMEM((Y, 2, 8, 128), F32),
        pltpu.VMEM((Y, 2, 8, 128), F32),
        pltpu.VMEM((X, 2, 8, 128), F32),
        pltpu.VMEM((2, 8, 128), F32),
        pltpu.VMEM((Z, 8, 128), F32),
        pltpu.VMEM(t_rows.shape, BF16),
        pltpu.VMEM(t_gain.shape, BF16),
        pltpu.VMEM(s_rows.shape, BF16),
        pltpu.VMEM(s_gain.shape, BF16),
        pltpu.VMEM((1, TOKENS), jnp.int32),
        pltpu.VMEM((1, TOKENS), jnp.int32),
        dma((2,)),
        dma((6,)),
        dma((3, 16)),
        dma((3, 16)),
        dma((3, 2, 2)),
        dma((3, 2, 2)),
        dma((3, 2, 8)),
        dma((3, 2, 8)),
        dma((3, 16)),
        dma((3, 16)),
        dma((3, 26)),
        dma((3, 26)),
        dma((8,)),
        dma((8,)),
        dma((2, 2, 3)),
        dma((2, 2, 3)),
        dma((2, 2, 4)),
        dma((2, 2, 4)),
        dma((2, 2, 4)),
        dma((2, 8)),
        dma((4, 8)),
        dma((4, 8)),
    ]
    flops = 2 * TOKENS * WIDTH * (DT + 2 * DS)
    shapes = (
        jax.ShapeDtypeStruct((8, 128), F32),
        jax.ShapeDtypeStruct(s_rows.shape, F32),
        jax.ShapeDtypeStruct((8, 128), F32),
    )
    values = pl.pallas_call(
        kernel,
        out_shape=shapes,
        in_specs=[hbm] * 8,
        out_specs=(vmem, vmem, vmem),
        scratch_shapes=scratch,
        compiler_params=pltpu.CompilerParams(
            collective_id=0, has_side_effects=True, vmem_limit_bytes=60 * 1024 * 1024
        ),
        cost_estimate=pl.CostEstimate(flops=flops, bytes_accessed=2 * WIDTH * (DT + DS), transcendentals=0),
    )(t_rows, t_gain, t_head, s_rows, s_gain, s_head, ids.reshape(1, TOKENS), mask.reshape(1, TOKENS))
    loss, grad, gain = pl.pallas_call(
        results,
        out_shape=(jax.ShapeDtypeStruct((1, 1), F32), jax.ShapeDtypeStruct(s_rows.shape, BF16), shapes[2]),
        in_specs=[vmem] * 3,
        out_specs=(pl.BlockSpec(memory_space=pltpu.SMEM), vmem, vmem),
    )(*values)
    return loss.reshape(()), grad, gain.reshape(1024)


def solution(mesh):
    return jax.shard_map(
        shards,
        mesh=mesh,
        in_specs=(
            P("vocab", "dp"),
            P(),
            P(None, ("dp", "vocab")),
            P("dp", "vocab"),
            P(),
            P(None, ("dp", "vocab")),
            P(),
            P(),
        ),
        out_specs=(P(), P("dp", "vocab"), P("vocab")),
        check_vma=False,
    )
```

```python
import functools
import math

import jax
import jax.numpy as jnp
from jax import lax
from jax.experimental import pallas as pl
from jax.experimental.pallas import tpu as pltpu
from jax.sharding import PartitionSpec as P

EPSILON = 1e-05
MIX_WEIGHT = 0.3
NLL_WEIGHT = 0.03
LOSS_SCALE = 8192.0
MESH = pl.DeviceIdType.MESH
F32 = jnp.float32
BF16 = jnp.bfloat16
X, Y, Z = 4, 4, 8
TOKENS, DT, DS, WIDTH = 256, 16384, 8192, 256


def kernel(
    t_rows_in, t_gain_in, t_head, s_rows_in, s_gain_in, s_head, ids_in, mask_in,
    loss_out, grad_out, gain_out,
    g0, g1, g2, t_w, s_w, t_gain, s_gain, t_inv, s_inv, t_acc0, t_acc1, t_acc, s_acc, dot_col, lg,
    sib_out, sib_in, raf, rbf, ra_out, rb_out, ra_via, rb_via, ra_in, rb_in,
    raf2, rbf2, ra2, rb2, ra_in2, rb_in2, raf3, rbf3, ra3, rb3, ra_in3, rb_in3,
    st_c, st_p, st_z, gp_c, gp1, gp_y, gp_x, gp3, gp_z,
    t_rows, t_gain_raw, s_rows, s_gain_raw, ids, mask,
    head_sem, input_sem, a_send, a_recv, b_send, b_recv, ring_send, ring_recv, core_send, core_recv,
    st_send, st_recv, sib_send_sem, sib_recv_sem, first_send, first_recv, rs_send, rs_recv, z_send, z_recv, gp_send, gp_recv,
):
    dp = lax.axis_index("dp")
    vo = lax.axis_index("vocab")
    c = lax.rem(dp, 2)
    x = lax.rem(lax.div(dp, 2), X)
    zl = lax.div(dp, 2 * X)
    y = lax.div(vo, 2)
    zh = lax.rem(vo, 2)
    z = zh * 4 + zl

    def device(x_, y_, z_, c_):
        return ((lax.rem(z_, 4) * X + x_) * 2 + c_, y_ * 2 + lax.div(z_, 4))

    to_c = lambda j: (dp - c + j, vo)
    to_x = lambda j: (dp + (j - x) * 2, vo)
    to_y = lambda j: (dp, vo + (j - y) * 2)
    to_z = lambda j: device(x, y, j, c)
    to_p = lambda j: device(lax.div(j, Y), lax.rem(j, Y), z, c)
    axis_c, axis_x, axis_y, axis_z = (2, c, to_c), (X, x, to_x), (Y, y, to_y), (Z, z, to_z)
    axis_p = (X * Y, x * Y + y, to_p)

    barrier = pltpu.get_barrier_semaphore()
    partners = 0
    for n, me, to in (axis_z, axis_p, axis_c):
        for k in range(1, n):
            pl.semaphore_signal(barrier, inc=1, device_id=to(lax.rem(me + k, n)), device_id_type=MESH)
            partners += 1

    t_load = pltpu.make_async_copy(t_head, t_w, head_sem.at[0])
    s_load = pltpu.make_async_copy(s_head, s_w, head_sem.at[1])
    loads = [
        pltpu.make_async_copy(src, dst, input_sem.at[k])
        for k, (src, dst) in enumerate(
            (
                (t_rows_in, t_rows), (s_rows_in, s_rows), (t_gain_in, t_gain_raw),
                (s_gain_in, s_gain_raw), (ids_in, ids), (mask_in, mask),
            )
        )
    ]
    for load in loads:
        load.start()
    t_load.start()
    s_load.start()
    for load in loads:
        load.wait()

    def remote(src, dst, send, recv, to):
        return pltpu.make_async_remote_copy(
            src_ref=src, dst_ref=dst, send_sem=send, recv_sem=recv, device_id=to, device_id_type=MESH
        )

    late = []

    def start(src, dst, send, recv, to):
        copy = remote(src, dst, send, recv, to)
        copy.start()
        late.append(copy)

    def arrived(dst, send, recv, to):
        remote(dst, dst, send, recv, to).wait_recv()

    p0 = x * Y + y
    g0[c, z, p0] = t_rows[0:16, :]
    g1[c, x, y, z] = t_rows[16:32, :]
    own_rows = s_rows[...].astype(F32)
    g2[c, y, x, z] = jnp.concatenate([own_rows[:, :512], own_rows[:, 512:]], axis=0).astype(BF16)

    def lane_sums(block):
        total = block[:, 0:128]
        for k in range(1, block.shape[1] // 128):
            total = total + block[:, k * 128 : (k + 1) * 128]
        total = jnp.concatenate([total] * (TOKENS // total.shape[0]), axis=0)
        return jnp.sum(total.T, axis=0, keepdims=True)

    lanes = lax.broadcasted_iota(jnp.int32, (1, TOKENS), 1)
    t_own = t_rows[...].astype(F32)
    t_squares = jnp.where(lax.div(lanes, 32) == vo, lane_sums(t_own * t_own), 0.0)
    s_squares = jnp.where(lax.div(lanes, 8) == dp, lane_sums(own_rows * own_rows), 0.0)

    def pack(rows):
        halves = [row[:, 128 * h : 128 * h + 128] for row in rows for h in range(2)]
        return jnp.concatenate(halves + [jnp.zeros((1, 128), F32)] * (8 - len(halves)), axis=0)

    def unpack(block, k):
        return jnp.concatenate([block[2 * k : 2 * k + 1], block[2 * k + 1 : 2 * k + 2]], axis=1)

    squares_value = pack([t_squares, s_squares])

    t_gain[...] = t_gain_raw[...].astype(F32).reshape(t_gain.shape)
    s_gain[...] = s_gain_raw[...].astype(F32).reshape(s_gain.shape)
    for acc in (t_acc0, t_acc1, s_acc):
        acc[...] = jnp.zeros_like(acc)

    pl.semaphore_wait(barrier, partners)

    def all_partners(axis, src, dst, send, recv):
        n, me, to = axis
        arrivals = []
        for k in range(1, n):
            j = lax.rem(me + k, n)
            start(src(j), dst(me), send(k), recv(me), to(j))
            arrivals.append(remote(dst(j), dst(j), send(k), recv(j), to(j)))

        def wait():
            for arrival in arrivals:
                arrival.wait_recv()

        return wait

    over_c, over_p, over_z = (axis_c, st_c, 0), (axis_p, st_p, 2), (axis_z, st_z, 18)

    def exchange(r, value, combine, result, steps=(over_c, over_p, over_z)):
        for axis, buf, base in steps:
            n, me, _ = axis
            buf[r, me] = value
            wait = all_partners(
                axis,
                lambda j: buf.at[r, me],
                lambda j: buf.at[r, j],
                lambda k: st_send.at[r, base + k],
                lambda j: st_recv.at[r, base + j],
            )
            yield
            wait()
            value = combine([buf[r, j] for j in range(n)])
        result.append(value)

    def finish(steps):
        for _ in steps:
            pass

    def add_all(values):
        return functools.reduce(lambda a, b: a + b, values)

    class Rows:
        def __init__(self, p, g, a, b, cc):
            self.p, self.g, self.a, self.b, self.c = p, g, a, b, cc
            step = lambda axis: tuple(axis[2](lax.rem(axis[1] + k, 4)) for k in (1, 3))
            self.to_b, self.to_c = step(b), step(cc)
            self.ready = set()

        def begin(self):
            mine, theirs = self.c[1], self.b[1]
            n, me, to = self.a
            slot = self.g.at[c, mine, theirs, me]
            for k in self.ORDER[1:]:
                j = lax.rem(me + k, n)
                start(slot, slot, a_send.at[self.p, k], a_recv.at[self.p, me], to(j))

        def row(self, core, plane, r):
            return self.g.at[core, lax.rem(self.c[1] + plane, 4), lax.rem(self.b[1] + r, 4)]

        def cross(self, plane, r):
            k = plane * 4 + r
            ref = self.row(c, plane, r)
            start(ref, ref, core_send.at[self.p, k], core_recv.at[self.p, k], to_c(1 - c))

        def crossed(self, plane):
            for r in range(4):
                k = plane * 4 + r
                arrived(self.row(1 - c, plane, r), core_send.at[self.p, k], core_recv.at[self.p, k], to_c(1 - c))

        def half(self, r, way):
            return self.row(c, 0, r).at[4 * way : 4 * way + 4]

        def send_b(self, way, item):
            ref = self.row(c, 0, 0) if item == 0 else self.half(3 if way == 0 else 1, way)
            start(ref, ref, b_send.at[self.p, way, item], b_recv.at[self.p, way, item], self.to_b[way])

        def take_b(self, item):
            for way in range(2):
                ref = self.row(c, 0, 3 if way == 0 else 1) if item == 0 else self.half(2, way)
                arrived(ref, b_send.at[self.p, way, item], b_recv.at[self.p, way, item], self.to_b[way])
                if item == 0:
                    self.send_b(way, 1)
            if item == 0:
                self.send_c(0, 1)
                self.send_c(1, 3)
                self.cross(0, 1)
                self.cross(0, 3)
            else:
                self.send_c(0, 2)
                self.send_c(1, 2)
                self.cross(0, 2)

        def send_c(self, way, r, hop=0):
            ref = self.row(c, 0 if hop == 0 else (3 if way == 0 else 1), r)
            k = r + 4 * hop
            start(ref, ref, ring_send.at[self.p, way, k], ring_recv.at[self.p, way, k], self.to_c[way])

        def take_c(self, way, r, hop=0):
            plane = 2 if hop else (3 if way == 0 else 1)
            k = r + 4 * hop
            arrived(self.row(c, plane, r), ring_send.at[self.p, way, k], ring_recv.at[self.p, way, k], self.to_c[way])
            if hop == 0 and r in ((0, 1), (3, 2))[way]:
                self.send_c(way, r, 1)
            self.cross(plane, r)

        ORDER = (0, 1, 7, 2, 6, 3, 5, 4)

        def after_a(self, steps):
            n, me, to = self.a
            for k in steps:
                j = lax.rem(me + k, n)
                slot = self.g.at[c, self.c[1], self.b[1], j]
                if k:
                    arrived(slot, a_send.at[self.p, k], a_recv.at[self.p, j], to(j))
                for way in range(2):
                    for send, recv, target in (
                        (b_send, b_recv, self.to_b[way]),
                        (ring_send, ring_recv, self.to_c[way]),
                    ):
                        remote(slot, slot, send.at[self.p, way, 0], recv.at[self.p, way, 0], target).start()

        def row_sent(self):
            row = self.row(c, 0, 0)
            for way in range(2):
                for send, recv, target in (
                    (b_send, b_recv, self.to_b[way]),
                    (ring_send, ring_recv, self.to_c[way]),
                ):
                    late.append(remote(row, row, send.at[self.p, way, 0], recv.at[self.p, way, 0], target))
            self.cross(0, 0)

    class Ring:
        def __init__(self, g, n, me, to):
            self.g, self.n, self.me = g, n, me
            self.to = (to(lax.rem(me + 1, n)), to(lax.rem(me + n - 1, n)))

        def piece(self, way, i, distance, core):
            half = i % 2 if way == 0 else 1 - i % 2
            plane = lax.rem(self.me + (self.n - distance if way == 0 else distance), self.n)
            return self.g.at[core, plane, 8 * half : 8 * half + 8]

        def send(self, way, i):
            ref = self.piece(way, i, i // 2, c)
            start(ref, ref, ring_send.at[0, way, i], ring_recv.at[0, way, i], self.to[way])

        def begin(self):
            for i in range(2):
                for way in range(2):
                    self.send(way, i)
            ref = self.g.at[c, self.me]
            start(ref, ref, core_send.at[0, 0], core_recv.at[0, 0], to_c(1 - c))

        def event(self, i):
            for way in range(2):
                ref = self.piece(way, i, i // 2 + 1, c)
                arrived(ref, ring_send.at[0, way, i], ring_recv.at[0, way, i], self.to[way])
                if i + 2 <= self.n - 2:
                    self.send(way, i + 2)
                k = 1 + 2 * i + way
                start(ref, ref, core_send.at[0, k], core_recv.at[0, k], to_c(1 - c))

        def crossed(self, i):
            for way in range(2):
                k = 1 + 2 * i + way
                arrived(self.piece(way, i, i // 2 + 1, 1 - c), core_send.at[0, k], core_recv.at[0, k], to_c(1 - c))

        def crossed_own(self):
            arrived(self.g.at[1 - c, self.me], core_send.at[0, 0], core_recv.at[0, 0], to_c(1 - c))

    part1 = Rows(1, g1, axis_z, axis_y, axis_x)
    part2 = Rows(2, g2, axis_z, axis_x, axis_y)
    part0 = Ring(g0, Z, z, to_z)
    both = (part1, part2)

    wide = lambda block: jnp.concatenate([block] * 4, axis=1)

    def student_planes(count, plane_of):
        def step(i, carry):
            y_, zh_ = plane_of(lax.div(i, 2)), lax.rem(i, 2)
            v = y_ * 2 + zh_
            gains = [s_gain[pl.ds(v * 2 + h, 1), :] for h in range(2)]
            blocks = ([], [])
            for pair in range(16):
                scaled = []
                for core in range(2):
                    raw = g2[core, y_, pair % 4, zh_ * 4 + pair // 4].astype(F32)
                    inv = wide(s_inv[pair, core])
                    scaled.append((raw[0:8] * inv, raw[8:16] * inv))
                for h in range(2):
                    rows = jnp.concatenate([scaled[0][h], scaled[1][h]], axis=0) * gains[h]
                    blocks[h].append(rows.astype(BF16))
            total = s_acc[...]
            for h in range(2):
                w = s_w[pl.ds(pl.multiple_of(v * 1024 + h * 512, 512), 512), :]
                total += jnp.dot(jnp.concatenate(blocks[h], axis=0), w, preferred_element_type=F32)
            s_acc[...] = total
            return carry

        lax.fori_loop(0, 2 * count, step, 0)

    def teacher_step(acc, p, load, first, count):
        lhs = []
        for v in range(8):
            inv = wide(t_inv[v * 32 + p * 16 : v * 32 + p * 16 + 16, :])
            blocks = []
            for k in range(count):
                gain = t_gain[pl.ds(first + k, 1), :]
                blocks.append((load(v, k).astype(F32) * inv * gain).astype(BF16))
            lhs.append(jnp.concatenate(blocks, axis=1))
        w = t_w[pl.ds(pl.multiple_of(first * 512, 512), count * 512), :]
        acc[...] += jnp.dot(jnp.concatenate(lhs, axis=0), w, preferred_element_type=F32)

    def teacher_x(count, plane_of):
        def step(i, carry):
            x_, zl_ = plane_of(lax.div(i, 4)), lax.rem(i, 4)
            load = lambda v, k: g1[k, x_, v // 2, (v % 2) * 4 + zl_]
            teacher_step(t_acc1, 1, load, (zl_ * X + x_) * 2, 2)
            return carry

        lax.fori_loop(0, 4 * count, step, 0, unroll=2)

    def teacher_z(count, plane_of):
        def step(i, carry):
            zl_, x_ = plane_of(lax.div(i, 2)), 2 * lax.rem(i, 2)
            load = lambda v, k: g0[k % 2, (v % 2) * 4 + zl_, (x_ + k // 2) * Y + v // 2]
            teacher_step(t_acc0, 0, load, (zl_ * X + x_) * 2, 4)
            return carry

        lax.fori_loop(0, 2 * count, step, 0)

    squares = []
    round0 = exchange(0, squares_value, add_all, squares, (over_z, over_c, over_p))
    next(round0)
    for part in both:
        part.begin()
    wait_plane = all_partners(
        axis_p,
        lambda j: g0.at[c, z, p0],
        lambda j: g0.at[c, z, j],
        lambda k: a_send.at[0, k],
        lambda j: a_recv.at[0, j],
    )
    for part in both:
        part.after_a(Rows.ORDER[:1])
    part1.after_a(Rows.ORDER[1:])
    wait_plane()
    part0.begin()
    next(round0)
    part2.after_a(Rows.ORDER[1:])
    next(round0)
    for part in both:
        part.row_sent()
    part0.event(0)
    for part in both:
        part.take_b(0)
    for part in both:
        part.take_c(0, 0)
        part.take_c(1, 0)
        part.send_c(0, 3)
        part.send_c(1, 1)
    part0.event(1)
    finish(round0)
    squares = squares[0]
    t_inv_row = lax.rsqrt(unpack(squares, 0) / DT + EPSILON)
    s_inv_row = lax.rsqrt(unpack(squares, 1) / DS + EPSILON)
    column = lambda row: jnp.broadcast_to(row, (128, TOKENS)).T
    t_inv[...] = column(t_inv_row)
    s_inv[...] = column(s_inv_row).reshape(s_inv.shape)
    t_load.wait()
    s_load.wait()
    for part in both:
        part.take_b(1)
    part0.event(2)
    for part in both:
        part.take_c(0, 1)
        part.take_c(1, 3)
    part0.event(3)
    part2.crossed(0)
    student_planes(1, lambda i: y)
    for part in both:
        part.take_c(0, 3)
        part.take_c(1, 1)
    part0.event(4)
    part1.crossed(0)
    teacher_x(1, lambda i: x)
    for part in both:
        part.take_c(0, 2)
        part.take_c(1, 2)
    for i in range(4):
        part0.crossed(i)
    teacher_z(1, lambda i: lax.rem(zl + 2, 4))
    part0.event(5)
    for part in both:
        for way, r in ((0, 0), (1, 3)):
            part.take_c(way, r, 1)
    part2.crossed(1)
    part2.crossed(3)
    student_planes(2, lambda i: lax.rem(y + 1 + 2 * i, Y))
    for part in both:
        part.take_c(0, 1, 1)
    part0.crossed(4)
    part0.crossed(5)
    teacher_z(2, lambda i: lax.rem(zl + 1 + 2 * i, 4))
    part0.event(6)
    part1.crossed(1)
    part1.crossed(3)
    teacher_x(2, lambda i: lax.rem(x + 1 + 2 * i, X))
    for part in both:
        part.take_c(1, 2, 1)
    part0.crossed(6)
    part0.crossed_own()
    teacher_z(1, lambda i: zl)
    part2.crossed(2)
    student_planes(1, lambda i: lax.rem(y + 2, Y))
    part1.crossed(2)
    teacher_x(1, lambda i: lax.rem(x + 2, X))

    order = []
    for v in range(8):
        order += [t_acc0[v * 16 : v * 16 + 16, :], t_acc1[v * 16 : v * 16 + 16, :]]
    tl = jnp.concatenate(order, axis=0).T
    sl = s_acc[...].T
    t_acc[...] = tl
    s_acc[...] = sl
    column_start = (dp * 8 + vo) * WIDTH
    onehot = (column_start + lax.broadcasted_iota(jnp.int32, (WIDTH, TOKENS), 0) == ids[...]).astype(F32)
    t_top = jnp.max(tl, axis=0, keepdims=True)
    s_top = jnp.max(sl, axis=0, keepdims=True)
    over_v = lambda a: jnp.sum(a, axis=0, keepdims=True)

    def merge(values):
        top = functools.reduce(jnp.maximum, [v[0:4] for v in values])
        return jnp.concatenate([top, add_all([v[4:8] * jnp.exp(v[0:4] - top) for v in values])], axis=0)

    first = []
    value = pack([t_top, s_top, over_v(jnp.exp(tl - t_top)), over_v(jnp.exp(sl - s_top))])
    finish(exchange(1, value, merge, first))
    first = first[0]
    t_lse = unpack(first, 0) + jnp.log(unpack(first, 2))
    s_lse = unpack(first, 1) + jnp.log(unpack(first, 3))
    t_logp = t_acc[...] - t_lse
    s_logp = s_acc[...] - s_lse
    a, b = math.log(MIX_WEIGHT) + t_logp, math.log(1.0 - MIX_WEIGHT) + s_logp
    mix_logp = jnp.maximum(a, b) + jnp.log1p(jnp.exp(-jnp.abs(a - b)))
    p_, q = jnp.exp(t_logp), jnp.exp(s_logp)
    gap = s_logp - mix_logp
    q_gap = q * gap
    weights = mask[...].astype(F32)
    rest = 1.0 - MIX_WEIGHT
    loss_part = weights * over_v(
        MIX_WEIGHT * p_ * (t_logp - mix_logp) + rest * q_gap - NLL_WEIGHT * (onehot * s_logp)
    )
    dot_part = over_v((rest * q_gap + NLL_WEIGHT * (q - onehot)) * s_logp)
    second = []
    finish(exchange(2, pack([loss_part, over_v(q_gap), dot_part, over_v(q * s_logp)]), add_all, second))
    second = second[0]
    kl = unpack(second, 1)
    count = jnp.sum(weights, axis=1, keepdims=True)
    row_scale = LOSS_SCALE * weights / count
    logit_grad = row_scale * (q * (rest * gap - rest * kl) + NLL_WEIGHT * (q - onehot))
    lg[...] = logit_grad.T.reshape(16, 2, 8, WIDTH)
    lhs = jnp.concatenate([lg[:, 1 - c].reshape(128, WIDTH), lg[:, c].reshape(128, WIDTH)], axis=0).astype(BF16)

    sibling = to_c(1 - c)

    def sib_copy(v):
        return remote(sib_out.at[v], sib_in.at[v], sib_send_sem.at[v], sib_recv_sem.at[v], sibling)

    def place(i):
        return lax.rem(y + 2 + 3 * i, Y), lax.div(i, 4)

    def grad_step(i, carry):
        y_, zh_ = place(i)
        v = y_ * 2 + zh_
        halves = []
        for h in range(2):
            w = s_w[pl.ds(pl.multiple_of(v * 1024 + h * 512, 512), 512), :]
            halves.append(
                lax.dot_general(lhs, w, (((1,), (1,)), ((), ())), preferred_element_type=F32).reshape(2, 16, 8, 512)
            )
        chunks = jnp.concatenate(halves, axis=2)
        sib_out[v] = chunks[0].astype(BF16)
        sib_copy(v).start()
        for k in range(16):
            raf[k % 4, zh_, y_, k // 4] = chunks[1, k, :, :256]
            rbf[y_, zh_, k % 4, k // 4] = chunks[1, k, :, 256:]
        return carry

    def sib_step(i, carry):
        y_, zh_ = place(i)
        v = y_ * 2 + zh_
        sib_copy(v).wait()
        for k in range(16):
            got = sib_in[v, k].astype(F32)
            at_a = (k % 4, zh_, y_, k // 4)
            at_b = (y_, zh_, k % 4, k // 4)
            sum_a = raf[at_a] + got[:, :256]
            sum_b = rbf[at_b] + got[:, 256:]
            raf[at_a] = sum_a
            rbf[at_b] = sum_b
            ra_out[at_a] = sum_a.astype(BF16)
            rb_out[at_b] = sum_b.astype(BF16)
        return carry

    class First:
        def __init__(self, part, axis, own, out, via, landing):
            self.part, self.own, self.out, self.via, self.landing = part, own, out, via, landing
            _, self.me, to = axis
            self.to = (to(lax.rem(self.me + 1, 4)), to(lax.rem(self.me + 3, 4)))

        def plane(self, k):
            return lax.rem(self.me + k, 4)

        def send(self, way, item):
            half = way if item != 1 else 1 - way
            k = 2 if item == 0 else (1 if way == 0 else 3)
            src = self.out.at[self.plane(k), half]
            dst = self.via.at[way] if item == 0 else self.landing.at[way, half]
            start(src, dst, first_send.at[self.part, way, item], first_recv.at[self.part, way, item], self.to[way])

        def take(self, way, item):
            half = way if item != 1 else 1 - way
            dst = self.via.at[way] if item == 0 else self.landing.at[way, half]
            arrived(dst, first_send.at[self.part, way, item], first_recv.at[self.part, way, item], self.to[way])

        def middle(self, way):
            self.take(way, 0)
            to = self.plane(1 if way == 0 else 3)

            def step(i, carry):
                row, at = lax.div(i, 4), lax.rem(i, 4)
                total = self.own[to, way, row, at] + self.via[way, row, at].astype(F32)
                self.out[to, way, row, at] = total.astype(BF16)
                return carry

            lax.fori_loop(0, 16, step, 0, unroll=4)
            self.send(way, 2)

        def last(self, half, total, out):
            self.take(1 - half, 1)
            self.take(half, 2)

            def step(row, carry):
                for zl_ in range(4):
                    value = self.own[self.me, half, row, zl_] + (
                        self.landing[0, half, row, zl_].astype(F32) + self.landing[1, half, row, zl_].astype(F32)
                    )
                    total[row, half, zl_] = value
                    out[row, half, zl_] = value.astype(BF16)
                return carry

            lax.fori_loop(0, 4, step, 0)

    first_a = First(0, axis_x, raf, ra_out, ra_via, ra_in)
    first_b = First(1, axis_y, rbf, rb_out, rb_via, rb_in)
    lax.fori_loop(0, 4, grad_step, 0)
    lax.fori_loop(0, 1, sib_step, 0)
    first_b.send(0, 0)
    lax.fori_loop(4, 8, grad_step, 0)
    lax.fori_loop(1, 4, sib_step, 0)
    first_a.send(0, 0)
    first_a.send(1, 1)
    first_b.send(1, 1)
    lax.fori_loop(4, 5, sib_step, 0)
    first_b.send(1, 0)
    lax.fori_loop(5, 6, sib_step, 0)
    first_b.send(0, 1)
    lax.fori_loop(6, 8, sib_step, 0)
    first_a.send(1, 0)
    first_a.send(0, 1)

    def gain_step(v, carry):
        y_, zh_ = lax.div(v, 2), lax.rem(v, 2)
        total = jnp.zeros((16, 512), F32)
        for i in range(16):
            z_ = zh_ * 4 + i // 4
            inv = s_inv[i, c]
            scaled = g2[c, y_, i % 4, z_].astype(F32) * wide(jnp.concatenate([inv, inv], axis=0))
            total += scaled * jnp.concatenate([raf[i % 4, zh_, y_, i // 4], rbf[y_, zh_, i % 4, i // 4]], axis=1)
        pieces = []
        for h in range(2):
            row = jnp.sum(total[8 * h : 8 * h + 8], axis=0, keepdims=True)
            pieces += [row[:, k * 128 : (k + 1) * 128] for k in range(4)]
        gp_c[c, y_, zh_] = jnp.concatenate(pieces, axis=0)
        return carry

    def scatter(axis, src, landing, part, half):
        return all_partners(
            axis,
            lambda j: src.at[j, half],
            lambda j: landing.at[j, half],
            lambda k: rs_send.at[part, half, k],
            lambda j: rs_recv.at[part, half, j],
        )

    def second_sum(axis, half, own, landing, total, out):
        n, me, _ = axis
        for at in range(4):
            value = own[me, half, at]
            for k in range(1, n):
                value = value + landing[lax.rem(me + k, n), half, at].astype(F32)
            total[half * 4 + at] = value
            out[half * 4 + at] = value.astype(BF16)

    own_sends = []

    def send_z(half, src, landing, part):
        for k in range(4):
            j = half * 4 + lax.rem(zl + k, 4)
            copy = remote(
                src.at[j], landing.at[z], z_send.at[part, half, k], z_recv.at[part, z], to_z(j)
            )
            if k:
                copy.start()
                late.append(copy)
            else:
                pl.when(zh != half)(copy.start)
                own_sends.append((half, copy))

    def third_sum(own, landing, part):
        for k in range(1, Z):
            j = lax.rem(z + k, Z)
            arrived(landing.at[j], z_send.at[part, 0, 1], z_recv.at[part, j], to_z(j))
        value = own[z]
        for k in range(1, Z):
            value = value + landing[lax.rem(z + k, Z)].astype(F32)
        return value

    lax.fori_loop(0, 8, gain_step, 0)
    gain_wait = all_partners(
        axis_c, lambda j: gp_c.at[c], lambda j: gp_c.at[j], lambda k: gp_send.at[0, k], lambda j: gp_recv.at[0, j]
    )
    first_b.middle(0)
    first_a.middle(0)
    gain_wait()
    gp1[...] = gp_c[0] + gp_c[1]
    gp_y[y] = gp1[y]
    gain_wait = all_partners(
        axis_y, lambda j: gp1.at[j], lambda j: gp_y.at[j], lambda k: gp_send.at[1, k], lambda j: gp_recv.at[1, j]
    )
    first_b.middle(1)
    first_a.middle(1)
    first_b.last(0, rbf2, rb2)
    wait_b0 = scatter(axis_x, rb2, rb_in2, 1, 0)
    first_a.last(0, raf2, ra2)
    wait_a0 = scatter(axis_y, ra2, ra_in2, 0, 0)
    gain_wait()
    gp_x[x] = add_all([gp_y[j] for j in range(Y)])
    gain_wait = all_partners(
        axis_x, lambda j: gp_x.at[x], lambda j: gp_x.at[j], lambda k: gp_send.at[2, k], lambda j: gp_recv.at[2, j]
    )
    first_b.last(1, rbf2, rb2)
    wait_b1 = scatter(axis_x, rb2, rb_in2, 1, 1)
    first_a.last(1, raf2, ra2)
    wait_a1 = scatter(axis_y, ra2, ra_in2, 0, 1)
    wait_b0()
    second_sum(axis_x, 0, rbf2, rb_in2, rbf3, rb3)
    send_z(0, rb3, rb_in3, 1)
    wait_a0()
    second_sum(axis_y, 0, raf2, ra_in2, raf3, ra3)
    send_z(0, ra3, ra_in3, 0)

    gain_wait()
    gp3[...] = add_all([gp_x[j] for j in range(X)])
    gp_z[z] = gp3[zh]
    gain_wait = all_partners(
        axis_z,
        lambda j: gp3.at[lax.div(j, 4)],
        lambda j: gp_z.at[j],
        lambda k: gp_send.at[3, k],
        lambda j: gp_recv.at[3, j],
    )
    row_dot = row_scale * (unpack(second, 2) - rest * kl * unpack(second, 3)) / DS
    dot_col[...] = column(row_dot).reshape(dot_col.shape)
    loss = jnp.sum(unpack(second, 0), axis=1, keepdims=True) / count
    loss_out[...] = jnp.broadcast_to(loss, loss_out.shape)

    wait_b1()
    second_sum(axis_x, 1, rbf2, rb_in2, rbf3, rb3)
    send_z(1, rb3, rb_in3, 1)
    wait_a1()
    second_sum(axis_y, 1, raf2, ra_in2, raf3, ra3)
    send_z(1, ra3, ra_in3, 0)
    normed_grad = jnp.concatenate([third_sum(raf3, ra_in3, 0), third_sum(rbf3, rb_in3, 1)], axis=1)
    inv = wide(s_inv[lax.div(dp, 2), c])
    dots = wide(dot_col[lax.div(dp, 2), c])
    for h in range(2):
        grad = normed_grad[h * 8 : h * 8 + 8]
        scaled = own_rows[:, h * 512 : (h + 1) * 512] * inv
        gain = s_gain[pl.ds(vo * 2 + h, 1), :]
        grad_out[:, h * 512 : (h + 1) * 512] = inv * (grad * gain - scaled * dots)
    gain_wait()
    gain_out[...] = add_all([gp_z[j] for j in range(Z)])
    for copy in late:
        copy.wait_send()
    for half, copy in own_sends:
        pl.when(zh != half)(copy.wait_send)


def results(loss, grad, gain, loss_out, grad_out, gain_out):
    loss_out[0, 0] = loss[0, 0]
    grad_out[...] = grad[...].astype(BF16)
    gain_out[...] = gain[...]


def shards(t_rows, t_gain, t_head, s_rows, s_gain, s_head, ids, mask):
    vmem = pl.BlockSpec(memory_space=pltpu.VMEM)
    hbm = pl.BlockSpec(memory_space=pl.ANY)
    dma = pltpu.SemaphoreType.DMA
    scratch = [
        pltpu.VMEM((2, Z, X * Y, 16, 512), BF16),
        pltpu.VMEM((2, X, Y, Z, 16, 512), BF16),
        pltpu.VMEM((2, Y, X, Z, 16, 512), BF16),
        pltpu.VMEM((DT, WIDTH), BF16),
        pltpu.VMEM((DS, WIDTH), BF16),
        pltpu.VMEM((DT // 512, 512), F32),
        pltpu.VMEM((DS // 512, 512), F32),
        pltpu.VMEM((TOKENS, 128), F32),
        pltpu.VMEM((16, 2, 8, 128), F32),
        pltpu.VMEM((TOKENS // 2, WIDTH), F32),
        pltpu.VMEM((TOKENS // 2, WIDTH), F32),
        pltpu.VMEM((TOKENS, WIDTH), F32),
        pltpu.VMEM((TOKENS, WIDTH), F32),
        pltpu.VMEM((16, 2, 8, 128), F32),
        pltpu.VMEM((16, 2, 8, WIDTH), F32),
        pltpu.VMEM((8, 16, 16, 512), BF16),
        pltpu.VMEM((8, 16, 16, 512), BF16),
        pltpu.VMEM((X, 2, Y, 4, 16, 256), F32),
        pltpu.VMEM((Y, 2, X, 4, 16, 256), F32),
        pltpu.VMEM((X, 2, Y, 4, 16, 256), BF16),
        pltpu.VMEM((Y, 2, X, 4, 16, 256), BF16),
        pltpu.VMEM((2, 4, 4, 16, 256), BF16),
        pltpu.VMEM((2, 4, 4, 16, 256), BF16),
        pltpu.VMEM((2, 2, Y, 4, 16, 256), BF16),
        pltpu.VMEM((2, 2, X, 4, 16, 256), BF16),
        pltpu.VMEM((Y, 2, 4, 16, 256), F32),
        pltpu.VMEM((X, 2, 4, 16, 256), F32),
        pltpu.VMEM((Y, 2, 4, 16, 256), BF16),
        pltpu.VMEM((X, 2, 4, 16, 256), BF16),
        pltpu.VMEM((Y, 2, 4, 16, 256), BF16),
        pltpu.VMEM((X, 2, 4, 16, 256), BF16),
        pltpu.VMEM((Z, 16, 256), F32),
        pltpu.VMEM((Z, 16, 256), F32),
        pltpu.VMEM((Z, 16, 256), BF16),
        pltpu.VMEM((Z, 16, 256), BF16),
        pltpu.VMEM((Z, 16, 256), BF16),
        pltpu.VMEM((Z, 16, 256), BF16),
        pltpu.VMEM((3, 2, 8, 128), F32),
        pltpu.VMEM((3, X * Y, 8, 128), F32),
        pltpu.VMEM((3, Z, 8, 128), F32),
        pltpu.VMEM((2, Y, 2, 8, 128), F32),
        pltpu.VMEM((Y, 2, 8, 128), F32),
        pltpu.VMEM((Y, 2, 8, 128), F32),
        pltpu.VMEM((X, 2, 8, 128), F32),
        pltpu.VMEM((2, 8, 128), F32),
        pltpu.VMEM((Z, 8, 128), F32),
        pltpu.VMEM(t_rows.shape, BF16),
        pltpu.VMEM(t_gain.shape, BF16),
        pltpu.VMEM(s_rows.shape, BF16),
        pltpu.VMEM(s_gain.shape, BF16),
        pltpu.VMEM((1, TOKENS), jnp.int32),
        pltpu.VMEM((1, TOKENS), jnp.int32),
        dma((2,)),
        dma((6,)),
        dma((3, 16)),
        dma((3, 16)),
        dma((3, 2, 2)),
        dma((3, 2, 2)),
        dma((3, 2, 8)),
        dma((3, 2, 8)),
        dma((3, 16)),
        dma((3, 16)),
        dma((3, 26)),
        dma((3, 26)),
        dma((8,)),
        dma((8,)),
        dma((2, 2, 3)),
        dma((2, 2, 3)),
        dma((2, 2, 4)),
        dma((2, 2, 4)),
        dma((2, 2, 4)),
        dma((2, 8)),
        dma((4, 8)),
        dma((4, 8)),
    ]
    flops = 2 * TOKENS * WIDTH * (DT + 2 * DS)
    shapes = (
        jax.ShapeDtypeStruct((8, 128), F32),
        jax.ShapeDtypeStruct(s_rows.shape, F32),
        jax.ShapeDtypeStruct((8, 128), F32),
    )
    values = pl.pallas_call(
        kernel,
        out_shape=shapes,
        in_specs=[hbm] * 8,
        out_specs=(vmem, vmem, vmem),
        scratch_shapes=scratch,
        compiler_params=pltpu.CompilerParams(
            collective_id=0, has_side_effects=True, vmem_limit_bytes=60 * 1024 * 1024
        ),
        cost_estimate=pl.CostEstimate(flops=flops, bytes_accessed=2 * WIDTH * (DT + DS), transcendentals=0),
    )(t_rows, t_gain, t_head, s_rows, s_gain, s_head, ids.reshape(1, TOKENS), mask.reshape(1, TOKENS))
    loss, grad, gain = pl.pallas_call(
        results,
        out_shape=(jax.ShapeDtypeStruct((1, 1), F32), jax.ShapeDtypeStruct(s_rows.shape, BF16), shapes[2]),
        in_specs=[vmem] * 3,
        out_specs=(pl.BlockSpec(memory_space=pltpu.SMEM), vmem, vmem),
    )(*values)
    return loss.reshape(()), grad, gain.reshape(1024)


def solution(mesh):
    return jax.shard_map(
        shards,
        mesh=mesh,
        in_specs=(
            P("vocab", "dp"),
            P(),
            P(None, ("dp", "vocab")),
            P("dp", "vocab"),
            P(),
            P(None, ("dp", "vocab")),
            P(),
            P(),
        ),
        out_specs=(P(), P("dp", "vocab"), P("vocab")),
        check_vma=False,
    )
```

```python
import functools
import math

import jax
import jax.numpy as jnp
from jax import lax
from jax.experimental import pallas as pl
from jax.experimental.pallas import tpu as pltpu
from jax.sharding import PartitionSpec as P

EPSILON = 1e-05
MIX_WEIGHT = 0.3
NLL_WEIGHT = 0.03
LOSS_SCALE = 8192.0
MESH = pl.DeviceIdType.MESH
F32 = jnp.float32
BF16 = jnp.bfloat16
X, Y, Z = 4, 4, 8
TOKENS, DT, DS, WIDTH = 256, 16384, 8192, 256


def kernel(
    t_rows_in, t_gain_in, t_head, s_rows_in, s_gain_in, s_head, ids_in, mask_in,
    loss_out, grad_out, gain_out,
    g0, g1, g2, t_w, s_w, t_gain, s_gain, t_inv, s_inv, t_acc0, t_acc1, t_acc, s_acc, dot_col, lg,
    sib_out, sib_in, raf, rbf, ra_out, rb_out, ra_via, rb_via, ra_in, rb_in,
    raf2, rbf2, ra2, rb2, ra_in2, rb_in2, raf3, rbf3, ra3, rb3, ra_in3, rb_in3,
    st_c, st_p, st_z, gp_c, gp1, gp_y, gp_x, gp3, gp_z,
    t_rows, t_gain_raw, s_rows, s_gain_raw, ids, mask,
    head_sem, input_sem, a_send, a_recv, b_send, b_recv, ring_send, ring_recv, core_send, core_recv,
    st_send, st_recv, sib_send_sem, sib_recv_sem, first_send, first_recv, rs_send, rs_recv, z_send, z_recv, gp_send, gp_recv,
):
    dp = lax.axis_index("dp")
    vo = lax.axis_index("vocab")
    c = lax.rem(dp, 2)
    x = lax.rem(lax.div(dp, 2), X)
    zl = lax.div(dp, 2 * X)
    y = lax.div(vo, 2)
    zh = lax.rem(vo, 2)
    z = zh * 4 + zl

    def device(x_, y_, z_, c_):
        return ((lax.rem(z_, 4) * X + x_) * 2 + c_, y_ * 2 + lax.div(z_, 4))

    to_c = lambda j: (dp - c + j, vo)
    to_x = lambda j: (dp + (j - x) * 2, vo)
    to_y = lambda j: (dp, vo + (j - y) * 2)
    to_z = lambda j: device(x, y, j, c)
    to_p = lambda j: device(lax.div(j, Y), lax.rem(j, Y), z, c)
    axis_c, axis_x, axis_y, axis_z = (2, c, to_c), (X, x, to_x), (Y, y, to_y), (Z, z, to_z)
    axis_p = (X * Y, x * Y + y, to_p)

    barrier = pltpu.get_barrier_semaphore()
    partners = 0
    for n, me, to in (axis_z, axis_p, axis_c):
        for k in range(1, n):
            pl.semaphore_signal(barrier, inc=1, device_id=to(lax.rem(me + k, n)), device_id_type=MESH)
            partners += 1

    t_load = pltpu.make_async_copy(t_head, t_w, head_sem.at[0])
    s_load = pltpu.make_async_copy(s_head, s_w, head_sem.at[1])
    loads = [
        pltpu.make_async_copy(src, dst, input_sem.at[k])
        for k, (src, dst) in enumerate(
            (
                (t_rows_in, t_rows), (s_rows_in, s_rows), (t_gain_in, t_gain_raw),
                (s_gain_in, s_gain_raw), (ids_in, ids), (mask_in, mask),
            )
        )
    ]
    for load in loads:
        load.start()
    t_load.start()
    s_load.start()
    for load in loads:
        load.wait()

    def remote(src, dst, send, recv, to):
        return pltpu.make_async_remote_copy(
            src_ref=src, dst_ref=dst, send_sem=send, recv_sem=recv, device_id=to, device_id_type=MESH
        )

    late = []

    def start(src, dst, send, recv, to):
        copy = remote(src, dst, send, recv, to)
        copy.start()
        late.append(copy)

    def arrived(dst, send, recv, to):
        remote(dst, dst, send, recv, to).wait_recv()

    p0 = x * Y + y
    g0[c, z, p0] = t_rows[0:16, :]
    g1[c, x, y, z] = t_rows[16:32, :]
    own_rows = s_rows[...].astype(F32)
    g2[c, y, x, z] = jnp.concatenate([own_rows[:, :512], own_rows[:, 512:]], axis=0).astype(BF16)

    def lane_sums(block):
        total = block[:, 0:128]
        for k in range(1, block.shape[1] // 128):
            total = total + block[:, k * 128 : (k + 1) * 128]
        total = jnp.concatenate([total] * (TOKENS // total.shape[0]), axis=0)
        return jnp.sum(total.T, axis=0, keepdims=True)

    lanes = lax.broadcasted_iota(jnp.int32, (1, TOKENS), 1)
    t_own = t_rows[...].astype(F32)
    t_squares = jnp.where(lax.div(lanes, 32) == vo, lane_sums(t_own * t_own), 0.0)
    s_squares = jnp.where(lax.div(lanes, 8) == dp, lane_sums(own_rows * own_rows), 0.0)

    def pack(rows):
        halves = [row[:, 128 * h : 128 * h + 128] for row in rows for h in range(2)]
        return jnp.concatenate(halves + [jnp.zeros((1, 128), F32)] * (8 - len(halves)), axis=0)

    def unpack(block, k):
        return jnp.concatenate([block[2 * k : 2 * k + 1], block[2 * k + 1 : 2 * k + 2]], axis=1)

    squares_value = pack([t_squares, s_squares])

    t_gain[...] = t_gain_raw[...].astype(F32).reshape(t_gain.shape)
    s_gain[...] = s_gain_raw[...].astype(F32).reshape(s_gain.shape)
    for acc in (t_acc0, t_acc1, s_acc):
        acc[...] = jnp.zeros_like(acc)

    pl.semaphore_wait(barrier, partners)

    def all_partners(axis, src, dst, send, recv):
        n, me, to = axis
        arrivals = []
        for k in range(1, n):
            j = lax.rem(me + k, n)
            start(src(j), dst(me), send(k), recv(me), to(j))
            arrivals.append(remote(dst(j), dst(j), send(k), recv(j), to(j)))

        def wait():
            for arrival in arrivals:
                arrival.wait_recv()

        return wait

    over_c, over_p, over_z = (axis_c, st_c, 0), (axis_p, st_p, 2), (axis_z, st_z, 18)

    def exchange(r, value, combine, result, steps=(over_c, over_p, over_z)):
        for axis, buf, base in steps:
            n, me, _ = axis
            buf[r, me] = value
            wait = all_partners(
                axis,
                lambda j: buf.at[r, me],
                lambda j: buf.at[r, j],
                lambda k: st_send.at[r, base + k],
                lambda j: st_recv.at[r, base + j],
            )
            yield
            wait()
            value = combine([buf[r, j] for j in range(n)])
        result.append(value)

    def finish(steps):
        for _ in steps:
            pass

    def add_all(values):
        return functools.reduce(lambda a, b: a + b, values)

    class Rows:
        def __init__(self, p, g, a, b, cc):
            self.p, self.g, self.a, self.b, self.c = p, g, a, b, cc
            step = lambda axis: tuple(axis[2](lax.rem(axis[1] + k, 4)) for k in (1, 3))
            self.to_b, self.to_c = step(b), step(cc)
            self.ready = set()

        def begin(self):
            mine, theirs = self.c[1], self.b[1]
            n, me, to = self.a
            slot = self.g.at[c, mine, theirs, me]
            for k in self.ORDER[1:]:
                j = lax.rem(me + k, n)
                start(slot, slot, a_send.at[self.p, k], a_recv.at[self.p, me], to(j))

        def row(self, core, plane, r):
            return self.g.at[core, lax.rem(self.c[1] + plane, 4), lax.rem(self.b[1] + r, 4)]

        def cross(self, plane, r):
            k = plane * 4 + r
            ref = self.row(c, plane, r)
            start(ref, ref, core_send.at[self.p, k], core_recv.at[self.p, k], to_c(1 - c))

        def crossed(self, plane):
            for r in range(4):
                k = plane * 4 + r
                arrived(self.row(1 - c, plane, r), core_send.at[self.p, k], core_recv.at[self.p, k], to_c(1 - c))

        def half(self, r, way):
            return self.row(c, 0, r).at[4 * way : 4 * way + 4]

        def send_b(self, way, item):
            ref = self.row(c, 0, 0) if item == 0 else self.half(3 if way == 0 else 1, way)
            start(ref, ref, b_send.at[self.p, way, item], b_recv.at[self.p, way, item], self.to_b[way])

        def take_b(self, item):
            for way in range(2):
                ref = self.row(c, 0, 3 if way == 0 else 1) if item == 0 else self.half(2, way)
                arrived(ref, b_send.at[self.p, way, item], b_recv.at[self.p, way, item], self.to_b[way])
                if item == 0:
                    self.send_b(way, 1)
            if item == 0:
                self.send_c(0, 1)
                self.send_c(1, 3)
                self.cross(0, 1)
                self.cross(0, 3)
            else:
                self.send_c(0, 2)
                self.send_c(1, 2)
                self.cross(0, 2)

        def send_c(self, way, r, hop=0):
            ref = self.row(c, 0 if hop == 0 else (3 if way == 0 else 1), r)
            k = r + 4 * hop
            start(ref, ref, ring_send.at[self.p, way, k], ring_recv.at[self.p, way, k], self.to_c[way])

        def take_c(self, way, r, hop=0):
            plane = 2 if hop else (3 if way == 0 else 1)
            k = r + 4 * hop
            arrived(self.row(c, plane, r), ring_send.at[self.p, way, k], ring_recv.at[self.p, way, k], self.to_c[way])
            if hop == 0 and r in ((0, 1), (3, 2))[way]:
                self.send_c(way, r, 1)
            self.cross(plane, r)

        ORDER = (0, 1, 7, 2, 6, 3, 5, 4)

        def after_a(self, steps):
            n, me, to = self.a
            for k in steps:
                j = lax.rem(me + k, n)
                slot = self.g.at[c, self.c[1], self.b[1], j]
                if k:
                    arrived(slot, a_send.at[self.p, k], a_recv.at[self.p, j], to(j))
                for way in range(2):
                    for send, recv, target in (
                        (b_send, b_recv, self.to_b[way]),
                        (ring_send, ring_recv, self.to_c[way]),
                    ):
                        remote(slot, slot, send.at[self.p, way, 0], recv.at[self.p, way, 0], target).start()

        def row_sent(self):
            row = self.row(c, 0, 0)
            for way in range(2):
                for send, recv, target in (
                    (b_send, b_recv, self.to_b[way]),
                    (ring_send, ring_recv, self.to_c[way]),
                ):
                    late.append(remote(row, row, send.at[self.p, way, 0], recv.at[self.p, way, 0], target))
            self.cross(0, 0)

    class Ring:
        def __init__(self, g, n, me, to):
            self.g, self.n, self.me = g, n, me
            self.to = (to(lax.rem(me + 1, n)), to(lax.rem(me + n - 1, n)))

        def piece(self, way, i, distance, core):
            half = i % 2 if way == 0 else 1 - i % 2
            plane = lax.rem(self.me + (self.n - distance if way == 0 else distance), self.n)
            return self.g.at[core, plane, 8 * half : 8 * half + 8]

        def send(self, way, i):
            ref = self.piece(way, i, i // 2, c)
            start(ref, ref, ring_send.at[0, way, i], ring_recv.at[0, way, i], self.to[way])

        def begin(self):
            for i in range(2):
                for way in range(2):
                    self.send(way, i)
            ref = self.g.at[c, self.me]
            start(ref, ref, core_send.at[0, 0], core_recv.at[0, 0], to_c(1 - c))

        def event(self, i):
            for way in range(2):
                ref = self.piece(way, i, i // 2 + 1, c)
                arrived(ref, ring_send.at[0, way, i], ring_recv.at[0, way, i], self.to[way])
                if i + 2 <= self.n - 2:
                    self.send(way, i + 2)
                k = 1 + 2 * i + way
                start(ref, ref, core_send.at[0, k], core_recv.at[0, k], to_c(1 - c))

        def crossed(self, i):
            for way in range(2):
                k = 1 + 2 * i + way
                arrived(self.piece(way, i, i // 2 + 1, 1 - c), core_send.at[0, k], core_recv.at[0, k], to_c(1 - c))

        def crossed_own(self):
            arrived(self.g.at[1 - c, self.me], core_send.at[0, 0], core_recv.at[0, 0], to_c(1 - c))

    part1 = Rows(1, g1, axis_z, axis_y, axis_x)
    part2 = Rows(2, g2, axis_z, axis_x, axis_y)
    part0 = Ring(g0, Z, z, to_z)
    both = (part1, part2)

    wide = lambda block: jnp.concatenate([block] * 4, axis=1)

    def student_planes(count, plane_of):
        def step(i, carry):
            y_, zh_ = plane_of(lax.div(i, 2)), lax.rem(i, 2)
            v = y_ * 2 + zh_
            gains = [s_gain[pl.ds(v * 2 + h, 1), :] for h in range(2)]
            blocks = ([], [])
            for pair in range(16):
                scaled = []
                for core in range(2):
                    raw = g2[core, y_, pair % 4, zh_ * 4 + pair // 4].astype(F32)
                    inv = wide(s_inv[pair, core])
                    scaled.append((raw[0:8] * inv, raw[8:16] * inv))
                for h in range(2):
                    rows = jnp.concatenate([scaled[0][h], scaled[1][h]], axis=0) * gains[h]
                    blocks[h].append(rows.astype(BF16))
            total = s_acc[...]
            for h in range(2):
                w = s_w[pl.ds(pl.multiple_of(v * 1024 + h * 512, 512), 512), :]
                total += jnp.dot(jnp.concatenate(blocks[h], axis=0), w, preferred_element_type=F32)
            s_acc[...] = total
            return carry

        lax.fori_loop(0, 2 * count, step, 0, unroll=2)

    def teacher_step(acc, p, load, first, count):
        lhs = []
        for v in range(8):
            inv = wide(t_inv[v * 32 + p * 16 : v * 32 + p * 16 + 16, :])
            blocks = []
            for k in range(count):
                gain = t_gain[pl.ds(first + k, 1), :]
                blocks.append((load(v, k).astype(F32) * inv * gain).astype(BF16))
            lhs.append(jnp.concatenate(blocks, axis=1))
        w = t_w[pl.ds(pl.multiple_of(first * 512, 512), count * 512), :]
        acc[...] += jnp.dot(jnp.concatenate(lhs, axis=0), w, preferred_element_type=F32)

    def teacher_x(count, plane_of):
        def step(i, carry):
            x_, zl_ = plane_of(lax.div(i, 4)), lax.rem(i, 4)
            load = lambda v, k: g1[k, x_, v // 2, (v % 2) * 4 + zl_]
            teacher_step(t_acc1, 1, load, (zl_ * X + x_) * 2, 2)
            return carry

        lax.fori_loop(0, 4 * count, step, 0, unroll=4)

    def teacher_z(count, plane_of):
        def step(i, carry):
            zl_, x_ = plane_of(lax.div(i, 2)), 2 * lax.rem(i, 2)
            load = lambda v, k: g0[k % 2, (v % 2) * 4 + zl_, (x_ + k // 2) * Y + v // 2]
            teacher_step(t_acc0, 0, load, (zl_ * X + x_) * 2, 4)
            return carry

        lax.fori_loop(0, 2 * count, step, 0, unroll=2)

    squares = []
    round0 = exchange(0, squares_value, add_all, squares, (over_z, over_c, over_p))
    next(round0)
    for part in both:
        part.begin()
    wait_plane = all_partners(
        axis_p,
        lambda j: g0.at[c, z, p0],
        lambda j: g0.at[c, z, j],
        lambda k: a_send.at[0, k],
        lambda j: a_recv.at[0, j],
    )
    for part in both:
        part.after_a(Rows.ORDER[:1])
    part1.after_a(Rows.ORDER[1:])
    wait_plane()
    part0.begin()
    next(round0)
    part2.after_a(Rows.ORDER[1:])
    next(round0)
    for part in both:
        part.row_sent()
    part0.event(0)
    for part in both:
        part.take_b(0)
    for part in both:
        part.take_c(0, 0)
        part.take_c(1, 0)
        part.send_c(0, 3)
        part.send_c(1, 1)
    part0.event(1)
    finish(round0)
    squares = squares[0]
    t_inv_row = lax.rsqrt(unpack(squares, 0) / DT + EPSILON)
    s_inv_row = lax.rsqrt(unpack(squares, 1) / DS + EPSILON)
    column = lambda row: jnp.broadcast_to(row, (128, TOKENS)).T
    t_inv[...] = column(t_inv_row)
    s_inv[...] = column(s_inv_row).reshape(s_inv.shape)
    t_load.wait()
    s_load.wait()
    for part in both:
        part.take_b(1)
    part0.event(2)
    for part in both:
        part.take_c(0, 1)
        part.take_c(1, 3)
    part0.event(3)
    part2.crossed(0)
    student_planes(1, lambda i: y)
    for part in both:
        part.take_c(0, 3)
        part.take_c(1, 1)
    part0.event(4)
    part1.crossed(0)
    teacher_x(1, lambda i: x)
    for part in both:
        part.take_c(0, 2)
        part.take_c(1, 2)
    for i in range(4):
        part0.crossed(i)
    teacher_z(1, lambda i: lax.rem(zl + 2, 4))
    part0.event(5)
    for part in both:
        for way, r in ((0, 0), (1, 3)):
            part.take_c(way, r, 1)
    part2.crossed(1)
    part2.crossed(3)
    student_planes(2, lambda i: lax.rem(y + 1 + 2 * i, Y))
    for part in both:
        part.take_c(0, 1, 1)
    part0.crossed(4)
    part0.crossed(5)
    teacher_z(2, lambda i: lax.rem(zl + 1 + 2 * i, 4))
    part0.event(6)
    part1.crossed(1)
    part1.crossed(3)
    teacher_x(2, lambda i: lax.rem(x + 1 + 2 * i, X))
    for part in both:
        part.take_c(1, 2, 1)
    part0.crossed(6)
    part0.crossed_own()
    teacher_z(1, lambda i: zl)
    part2.crossed(2)
    student_planes(1, lambda i: lax.rem(y + 2, Y))
    part1.crossed(2)
    teacher_x(1, lambda i: lax.rem(x + 2, X))

    order = []
    for v in range(8):
        order += [t_acc0[v * 16 : v * 16 + 16, :], t_acc1[v * 16 : v * 16 + 16, :]]
    tl = jnp.concatenate(order, axis=0).T
    sl = s_acc[...].T
    t_acc[...] = tl
    s_acc[...] = sl
    column_start = (dp * 8 + vo) * WIDTH
    onehot = (column_start + lax.broadcasted_iota(jnp.int32, (WIDTH, TOKENS), 0) == ids[...]).astype(F32)
    t_top = jnp.max(tl, axis=0, keepdims=True)
    s_top = jnp.max(sl, axis=0, keepdims=True)
    over_v = lambda a: jnp.sum(a, axis=0, keepdims=True)

    def merge(values):
        top = functools.reduce(jnp.maximum, [v[0:4] for v in values])
        return jnp.concatenate([top, add_all([v[4:8] * jnp.exp(v[0:4] - top) for v in values])], axis=0)

    first = []
    value = pack([t_top, s_top, over_v(jnp.exp(tl - t_top)), over_v(jnp.exp(sl - s_top))])
    finish(exchange(1, value, merge, first))
    first = first[0]
    t_lse = unpack(first, 0) + jnp.log(unpack(first, 2))
    s_lse = unpack(first, 1) + jnp.log(unpack(first, 3))
    t_logp = t_acc[...] - t_lse
    s_logp = s_acc[...] - s_lse
    a, b = math.log(MIX_WEIGHT) + t_logp, math.log(1.0 - MIX_WEIGHT) + s_logp
    mix_logp = jnp.maximum(a, b) + jnp.log1p(jnp.exp(-jnp.abs(a - b)))
    p_, q = jnp.exp(t_logp), jnp.exp(s_logp)
    gap = s_logp - mix_logp
    q_gap = q * gap
    weights = mask[...].astype(F32)
    rest = 1.0 - MIX_WEIGHT
    loss_part = weights * over_v(
        MIX_WEIGHT * p_ * (t_logp - mix_logp) + rest * q_gap - NLL_WEIGHT * (onehot * s_logp)
    )
    dot_part = over_v((rest * q_gap + NLL_WEIGHT * (q - onehot)) * s_logp)
    second = []
    finish(exchange(2, pack([loss_part, over_v(q_gap), dot_part, over_v(q * s_logp)]), add_all, second))
    second = second[0]
    kl = unpack(second, 1)
    count = jnp.sum(weights, axis=1, keepdims=True)
    row_scale = LOSS_SCALE * weights / count
    logit_grad = row_scale * (q * (rest * gap - rest * kl) + NLL_WEIGHT * (q - onehot))
    lg[...] = logit_grad.T.reshape(16, 2, 8, WIDTH)
    lhs = jnp.concatenate([lg[:, 1 - c].reshape(128, WIDTH), lg[:, c].reshape(128, WIDTH)], axis=0).astype(BF16)

    sibling = to_c(1 - c)

    def sib_copy(v):
        return remote(sib_out.at[v], sib_in.at[v], sib_send_sem.at[v], sib_recv_sem.at[v], sibling)

    def place(i):
        return lax.rem(y + 2 + 3 * i, Y), lax.div(i, 4)

    def grad_step(i, carry):
        y_, zh_ = place(i)
        v = y_ * 2 + zh_
        halves = []
        for h in range(2):
            w = s_w[pl.ds(pl.multiple_of(v * 1024 + h * 512, 512), 512), :]
            halves.append(
                lax.dot_general(lhs, w, (((1,), (1,)), ((), ())), preferred_element_type=F32).reshape(2, 16, 8, 512)
            )
        chunks = jnp.concatenate(halves, axis=2)
        sib_out[v] = chunks[0].astype(BF16)
        sib_copy(v).start()
        for k in range(16):
            raf[k % 4, zh_, y_, k // 4] = chunks[1, k, :, :256]
            rbf[y_, zh_, k % 4, k // 4] = chunks[1, k, :, 256:]
        return carry

    def sib_step(i, carry):
        y_, zh_ = place(i)
        v = y_ * 2 + zh_
        sib_copy(v).wait()
        for k in range(16):
            got = sib_in[v, k].astype(F32)
            at_a = (k % 4, zh_, y_, k // 4)
            at_b = (y_, zh_, k % 4, k // 4)
            sum_a = raf[at_a] + got[:, :256]
            sum_b = rbf[at_b] + got[:, 256:]
            raf[at_a] = sum_a
            rbf[at_b] = sum_b
            ra_out[at_a] = sum_a.astype(BF16)
            rb_out[at_b] = sum_b.astype(BF16)
        return carry

    class First:
        def __init__(self, part, axis, own, out, via, landing):
            self.part, self.own, self.out, self.via, self.landing = part, own, out, via, landing
            _, self.me, to = axis
            self.to = (to(lax.rem(self.me + 1, 4)), to(lax.rem(self.me + 3, 4)))

        def plane(self, k):
            return lax.rem(self.me + k, 4)

        def send(self, way, item):
            half = way if item != 1 else 1 - way
            k = 2 if item == 0 else (1 if way == 0 else 3)
            src = self.out.at[self.plane(k), half]
            dst = self.via.at[way] if item == 0 else self.landing.at[way, half]
            start(src, dst, first_send.at[self.part, way, item], first_recv.at[self.part, way, item], self.to[way])

        def take(self, way, item):
            half = way if item != 1 else 1 - way
            dst = self.via.at[way] if item == 0 else self.landing.at[way, half]
            arrived(dst, first_send.at[self.part, way, item], first_recv.at[self.part, way, item], self.to[way])

        def middle(self, way):
            self.take(way, 0)
            to = self.plane(1 if way == 0 else 3)

            def step(i, carry):
                row, at = lax.div(i, 4), lax.rem(i, 4)
                total = self.own[to, way, row, at] + self.via[way, row, at].astype(F32)
                self.out[to, way, row, at] = total.astype(BF16)
                return carry

            lax.fori_loop(0, 16, step, 0, unroll=4)
            self.send(way, 2)

        def last(self, half, total, out):
            self.take(1 - half, 1)
            self.take(half, 2)

            def step(row, carry):
                for zl_ in range(4):
                    value = self.own[self.me, half, row, zl_] + (
                        self.landing[0, half, row, zl_].astype(F32) + self.landing[1, half, row, zl_].astype(F32)
                    )
                    total[row, half, zl_] = value
                    out[row, half, zl_] = value.astype(BF16)
                return carry

            lax.fori_loop(0, 4, step, 0)

    first_a = First(0, axis_x, raf, ra_out, ra_via, ra_in)
    first_b = First(1, axis_y, rbf, rb_out, rb_via, rb_in)
    lax.fori_loop(0, 4, grad_step, 0)
    lax.fori_loop(0, 1, sib_step, 0)
    first_b.send(0, 0)
    lax.fori_loop(4, 8, grad_step, 0)
    lax.fori_loop(1, 4, sib_step, 0)
    first_a.send(0, 0)
    first_a.send(1, 1)
    first_b.send(1, 1)
    lax.fori_loop(4, 5, sib_step, 0)
    first_b.send(1, 0)
    lax.fori_loop(5, 6, sib_step, 0)
    first_b.send(0, 1)
    lax.fori_loop(6, 8, sib_step, 0)
    first_a.send(1, 0)
    first_a.send(0, 1)

    def gain_step(v, carry):
        y_, zh_ = lax.div(v, 2), lax.rem(v, 2)
        total = jnp.zeros((16, 512), F32)
        for i in range(16):
            z_ = zh_ * 4 + i // 4
            inv = s_inv[i, c]
            scaled = g2[c, y_, i % 4, z_].astype(F32) * wide(jnp.concatenate([inv, inv], axis=0))
            total += scaled * jnp.concatenate([raf[i % 4, zh_, y_, i // 4], rbf[y_, zh_, i % 4, i // 4]], axis=1)
        pieces = []
        for h in range(2):
            row = jnp.sum(total[8 * h : 8 * h + 8], axis=0, keepdims=True)
            pieces += [row[:, k * 128 : (k + 1) * 128] for k in range(4)]
        gp_c[c, y_, zh_] = jnp.concatenate(pieces, axis=0)
        return carry

    def scatter(axis, src, landing, part, half):
        return all_partners(
            axis,
            lambda j: src.at[j, half],
            lambda j: landing.at[j, half],
            lambda k: rs_send.at[part, half, k],
            lambda j: rs_recv.at[part, half, j],
        )

    def second_sum(axis, half, own, landing, total, out):
        n, me, _ = axis
        for at in range(4):
            value = own[me, half, at]
            for k in range(1, n):
                value = value + landing[lax.rem(me + k, n), half, at].astype(F32)
            total[half * 4 + at] = value
            out[half * 4 + at] = value.astype(BF16)

    own_sends = []

    def send_z(half, src, landing, part):
        for k in range(4):
            j = half * 4 + lax.rem(zl + k, 4)
            copy = remote(
                src.at[j], landing.at[z], z_send.at[part, half, k], z_recv.at[part, z], to_z(j)
            )
            if k:
                copy.start()
                late.append(copy)
            else:
                pl.when(zh != half)(copy.start)
                own_sends.append((half, copy))

    def third_sum(own, landing, part):
        for k in range(1, Z):
            j = lax.rem(z + k, Z)
            arrived(landing.at[j], z_send.at[part, 0, 1], z_recv.at[part, j], to_z(j))
        value = own[z]
        for k in range(1, Z):
            value = value + landing[lax.rem(z + k, Z)].astype(F32)
        return value

    lax.fori_loop(0, 8, gain_step, 0)
    gain_wait = all_partners(
        axis_c, lambda j: gp_c.at[c], lambda j: gp_c.at[j], lambda k: gp_send.at[0, k], lambda j: gp_recv.at[0, j]
    )
    first_b.middle(0)
    first_a.middle(0)
    gain_wait()
    gp1[...] = gp_c[0] + gp_c[1]
    gp_y[y] = gp1[y]
    gain_wait = all_partners(
        axis_y, lambda j: gp1.at[j], lambda j: gp_y.at[j], lambda k: gp_send.at[1, k], lambda j: gp_recv.at[1, j]
    )
    first_b.middle(1)
    first_a.middle(1)
    first_b.last(0, rbf2, rb2)
    wait_b0 = scatter(axis_x, rb2, rb_in2, 1, 0)
    first_a.last(0, raf2, ra2)
    wait_a0 = scatter(axis_y, ra2, ra_in2, 0, 0)
    gain_wait()
    gp_x[x] = add_all([gp_y[j] for j in range(Y)])
    gain_wait = all_partners(
        axis_x, lambda j: gp_x.at[x], lambda j: gp_x.at[j], lambda k: gp_send.at[2, k], lambda j: gp_recv.at[2, j]
    )
    first_b.last(1, rbf2, rb2)
    wait_b1 = scatter(axis_x, rb2, rb_in2, 1, 1)
    first_a.last(1, raf2, ra2)
    wait_a1 = scatter(axis_y, ra2, ra_in2, 0, 1)
    wait_b0()
    second_sum(axis_x, 0, rbf2, rb_in2, rbf3, rb3)
    send_z(0, rb3, rb_in3, 1)
    wait_a0()
    second_sum(axis_y, 0, raf2, ra_in2, raf3, ra3)
    send_z(0, ra3, ra_in3, 0)

    gain_wait()
    gp3[...] = add_all([gp_x[j] for j in range(X)])
    gp_z[z] = gp3[zh]
    gain_wait = all_partners(
        axis_z,
        lambda j: gp3.at[lax.div(j, 4)],
        lambda j: gp_z.at[j],
        lambda k: gp_send.at[3, k],
        lambda j: gp_recv.at[3, j],
    )
    row_dot = row_scale * (unpack(second, 2) - rest * kl * unpack(second, 3)) / DS
    dot_col[...] = column(row_dot).reshape(dot_col.shape)
    loss = jnp.sum(unpack(second, 0), axis=1, keepdims=True) / count
    loss_out[...] = jnp.broadcast_to(loss, loss_out.shape)

    wait_b1()
    second_sum(axis_x, 1, rbf2, rb_in2, rbf3, rb3)
    send_z(1, rb3, rb_in3, 1)
    wait_a1()
    second_sum(axis_y, 1, raf2, ra_in2, raf3, ra3)
    send_z(1, ra3, ra_in3, 0)
    normed_grad = jnp.concatenate([third_sum(raf3, ra_in3, 0), third_sum(rbf3, rb_in3, 1)], axis=1)
    inv = wide(s_inv[lax.div(dp, 2), c])
    dots = wide(dot_col[lax.div(dp, 2), c])
    for h in range(2):
        grad = normed_grad[h * 8 : h * 8 + 8]
        scaled = own_rows[:, h * 512 : (h + 1) * 512] * inv
        gain = s_gain[pl.ds(vo * 2 + h, 1), :]
        grad_out[:, h * 512 : (h + 1) * 512] = inv * (grad * gain - scaled * dots)
    gain_wait()
    gain_out[...] = add_all([gp_z[j] for j in range(Z)])
    for copy in late:
        copy.wait_send()
    for half, copy in own_sends:
        pl.when(zh != half)(copy.wait_send)


def results(loss, grad, gain, loss_out, grad_out, gain_out):
    loss_out[0, 0] = loss[0, 0]
    grad_out[...] = grad[...].astype(BF16)
    gain_out[...] = gain[...]


def shards(t_rows, t_gain, t_head, s_rows, s_gain, s_head, ids, mask):
    vmem = pl.BlockSpec(memory_space=pltpu.VMEM)
    hbm = pl.BlockSpec(memory_space=pl.ANY)
    dma = pltpu.SemaphoreType.DMA
    scratch = [
        pltpu.VMEM((2, Z, X * Y, 16, 512), BF16),
        pltpu.VMEM((2, X, Y, Z, 16, 512), BF16),
        pltpu.VMEM((2, Y, X, Z, 16, 512), BF16),
        pltpu.VMEM((DT, WIDTH), BF16),
        pltpu.VMEM((DS, WIDTH), BF16),
        pltpu.VMEM((DT // 512, 512), F32),
        pltpu.VMEM((DS // 512, 512), F32),
        pltpu.VMEM((TOKENS, 128), F32),
        pltpu.VMEM((16, 2, 8, 128), F32),
        pltpu.VMEM((TOKENS // 2, WIDTH), F32),
        pltpu.VMEM((TOKENS // 2, WIDTH), F32),
        pltpu.VMEM((TOKENS, WIDTH), F32),
        pltpu.VMEM((TOKENS, WIDTH), F32),
        pltpu.VMEM((16, 2, 8, 128), F32),
        pltpu.VMEM((16, 2, 8, WIDTH), F32),
        pltpu.VMEM((8, 16, 16, 512), BF16),
        pltpu.VMEM((8, 16, 16, 512), BF16),
        pltpu.VMEM((X, 2, Y, 4, 16, 256), F32),
        pltpu.VMEM((Y, 2, X, 4, 16, 256), F32),
        pltpu.VMEM((X, 2, Y, 4, 16, 256), BF16),
        pltpu.VMEM((Y, 2, X, 4, 16, 256), BF16),
        pltpu.VMEM((2, 4, 4, 16, 256), BF16),
        pltpu.VMEM((2, 4, 4, 16, 256), BF16),
        pltpu.VMEM((2, 2, Y, 4, 16, 256), BF16),
        pltpu.VMEM((2, 2, X, 4, 16, 256), BF16),
        pltpu.VMEM((Y, 2, 4, 16, 256), F32),
        pltpu.VMEM((X, 2, 4, 16, 256), F32),
        pltpu.VMEM((Y, 2, 4, 16, 256), BF16),
        pltpu.VMEM((X, 2, 4, 16, 256), BF16),
        pltpu.VMEM((Y, 2, 4, 16, 256), BF16),
        pltpu.VMEM((X, 2, 4, 16, 256), BF16),
        pltpu.VMEM((Z, 16, 256), F32),
        pltpu.VMEM((Z, 16, 256), F32),
        pltpu.VMEM((Z, 16, 256), BF16),
        pltpu.VMEM((Z, 16, 256), BF16),
        pltpu.VMEM((Z, 16, 256), BF16),
        pltpu.VMEM((Z, 16, 256), BF16),
        pltpu.VMEM((3, 2, 8, 128), F32),
        pltpu.VMEM((3, X * Y, 8, 128), F32),
        pltpu.VMEM((3, Z, 8, 128), F32),
        pltpu.VMEM((2, Y, 2, 8, 128), F32),
        pltpu.VMEM((Y, 2, 8, 128), F32),
        pltpu.VMEM((Y, 2, 8, 128), F32),
        pltpu.VMEM((X, 2, 8, 128), F32),
        pltpu.VMEM((2, 8, 128), F32),
        pltpu.VMEM((Z, 8, 128), F32),
        pltpu.VMEM(t_rows.shape, BF16),
        pltpu.VMEM(t_gain.shape, BF16),
        pltpu.VMEM(s_rows.shape, BF16),
        pltpu.VMEM(s_gain.shape, BF16),
        pltpu.VMEM((1, TOKENS), jnp.int32),
        pltpu.VMEM((1, TOKENS), jnp.int32),
        dma((2,)),
        dma((6,)),
        dma((3, 16)),
        dma((3, 16)),
        dma((3, 2, 2)),
        dma((3, 2, 2)),
        dma((3, 2, 8)),
        dma((3, 2, 8)),
        dma((3, 16)),
        dma((3, 16)),
        dma((3, 26)),
        dma((3, 26)),
        dma((8,)),
        dma((8,)),
        dma((2, 2, 3)),
        dma((2, 2, 3)),
        dma((2, 2, 4)),
        dma((2, 2, 4)),
        dma((2, 2, 4)),
        dma((2, 8)),
        dma((4, 8)),
        dma((4, 8)),
    ]
    flops = 2 * TOKENS * WIDTH * (DT + 2 * DS)
    shapes = (
        jax.ShapeDtypeStruct((8, 128), F32),
        jax.ShapeDtypeStruct(s_rows.shape, F32),
        jax.ShapeDtypeStruct((8, 128), F32),
    )
    values = pl.pallas_call(
        kernel,
        out_shape=shapes,
        in_specs=[hbm] * 8,
        out_specs=(vmem, vmem, vmem),
        scratch_shapes=scratch,
        compiler_params=pltpu.CompilerParams(
            collective_id=0, has_side_effects=True, vmem_limit_bytes=60 * 1024 * 1024
        ),
        cost_estimate=pl.CostEstimate(flops=flops, bytes_accessed=2 * WIDTH * (DT + DS), transcendentals=0),
    )(t_rows, t_gain, t_head, s_rows, s_gain, s_head, ids.reshape(1, TOKENS), mask.reshape(1, TOKENS))
    loss, grad, gain = pl.pallas_call(
        results,
        out_shape=(jax.ShapeDtypeStruct((1, 1), F32), jax.ShapeDtypeStruct(s_rows.shape, BF16), shapes[2]),
        in_specs=[vmem] * 3,
        out_specs=(pl.BlockSpec(memory_space=pltpu.SMEM), vmem, vmem),
    )(*values)
    return loss.reshape(()), grad, gain.reshape(1024)


def solution(mesh):
    return jax.shard_map(
        shards,
        mesh=mesh,
        in_specs=(
            P("vocab", "dp"),
            P(),
            P(None, ("dp", "vocab")),
            P("dp", "vocab"),
            P(),
            P(None, ("dp", "vocab")),
            P(),
            P(),
        ),
        out_specs=(P(), P("dp", "vocab"), P("vocab")),
        check_vma=False,
    )
```
